32 devices in a mesh: dp: 8 (over z, y), head: 4 (over x, core).
Axes of the slice: x: 2, y: 2, z: 4, core: 2. Of those that a mesh axis runs over, the one named last changes fastest.
Arguments:
- inputs: bfloat16 [128, 256, 384], P(('dp', 'head')), may hold values from -64 to 64
- embedding: bfloat16 [128, 512], P(('dp', 'head')), may hold values from -6 to 6
- region: int32 [128, 256], P('dp'), may hold values from 0 to 4, as said below
- cotangent: bfloat16 [128, 256, 384], P(('dp', 'head')), may hold values from -6 to 6
- conv_one: bfloat16 [3456, 384], P('dp', 'head'), may hold values from -0.109375 to 0.109375
- bias_one: float32 [384], replicated, may hold values from -3 to 3
- conv_two: bfloat16 [3456, 384], P('dp', 'head'), may hold values from -0.109375 to 0.109375
- bias_two: float32 [384], replicated, may hold values from -3 to 3
- emb_weight: bfloat16 [512, 768], P('dp', 'head'), may hold values from -0.25 to 0.25
- emb_bias: float32 [768], replicated, may hold values from -2 to 2
- qkv_weight: bfloat16 [384, 1152], P('dp', 'head'), may hold values from -0.3125 to 0.3125
- q_bias: float32 [384], replicated, may hold values from -2 to 2
- v_bias: float32 [384], replicated, may hold values from -2 to 2
- proj_weight: bfloat16 [384, 384], P('dp', 'head'), may hold values from -1.75 to 1.75
- proj_bias: float32 [384], replicated, may hold values from -3 to 3
- gain_one: float32 [384], replicated, may hold values from 0.1 to 1.9
- shift_one: float32 [384], replicated, may hold values from -3 to 3
- gain_two: float32 [384], replicated, may hold values from 0.1 to 1.9
- shift_two: float32 [384], replicated, may hold values from -3 to 3
- gain_three: float32 [384], replicated, may hold values from 0.1 to 1.9
- shift_three: float32 [384], replicated, may hold values from -3 to 3
Outputs:
- output: bfloat16 [128, 256, 384], P(('dp', 'head'))
- grad_inputs: bfloat16 [128, 256, 384], P(('dp', 'head'))
- grad_embedding: float32 [128, 512], P(('dp', 'head'))
- grad_conv_one: float32 [3456, 384], P('dp', 'head')
- grad_conv_two: float32 [3456, 384], P('dp', 'head')
- grad_emb_weight: float32 [512, 768], P('dp', 'head')
- grad_qkv_weight: float32 [384, 1152], P('dp', 'head')
- grad_proj_weight: float32 [384, 384], P('dp', 'head')
- grad_bias_one: float32 [384], replicated
- grad_bias_two: float32 [384], replicated
- grad_emb_bias: float32 [768], replicated
- grad_q_bias: float32 [384], replicated
- grad_v_bias: float32 [384], replicated
- grad_proj_bias: float32 [384], replicated
- grad_gain_one: float32 [384], replicated
- grad_shift_one: float32 [384], replicated
- grad_gain_two: float32 [384], replicated
- grad_shift_two: float32 [384], replicated
- grad_gain_three: float32 [384], replicated
- grad_shift_three: float32 [384], replicated
The draws below stay inside these ranges and needn't reach their ends.
Inputs may be any that keep to these rules, and one draw needn't show every extreme that they name: Even-numbered maps hold region 1 at every pixel. In an odd-numbered map, quadrant k (k = 2 (i // 8) + j // 8) holds one crop: pixels in a rectangle of 4 to 8 rows and columns starting at the quadrant's first row and column carry k + 1, the rest of the quadrant 0.
All inputs are finite; a program needn't handle non-finite values.
Results may differ from the reference program's by a relative error of at most 0.015.
Values may be sent and summed in bfloat16 or wider, within the bound.
No kernel may reach another device: no remote copies, remote signals or barrier semaphores. Data moves between devices by JAX's collectives and lax.ppermute only.
A program may use at most 128 MiB of HBM per device.

```python
import jax
import jax.numpy as jnp
from jax import lax

WIDTH = 384
EMBED = 512
HEADS = 4
HEAD_DIM = 96
GROUPS = 32
SIDE = 16
PIXELS = 256
MAPS = 128


def draw_inputs(key, part):
    key = jax.random.fold_in(key, 11)
    subkeys = jax.random.split(key, 2)
    row_index = jnp.arange(PIXELS) // SIDE
    row_scale = 3.0 ** (row_index.astype(jnp.float32) / (SIDE - 1))
    channel_scale = jax.random.uniform(subkeys[1], (WIDTH,), jnp.float32, 0.5, 2.0)
    values = jax.random.normal(subkeys[0], (MAPS, PIXELS, WIDTH), jnp.float32)
    return (values * row_scale[None, :, None] * channel_scale).astype(jnp.bfloat16)


def draw_region(key, part):
    key = jax.random.fold_in(key, 23)
    half_side = SIDE // 2
    heights = jax.random.randint(jax.random.fold_in(key, 1), (MAPS, 4), SIDE // 4, half_side + 1)
    widths = jax.random.randint(jax.random.fold_in(key, 2), (MAPS, 4), SIDE // 4, half_side + 1)
    row_index = jnp.arange(PIXELS) // SIDE
    col_index = jnp.arange(PIXELS) % SIDE
    quadrant = row_index // half_side * 2 + col_index // half_side
    inside = ((row_index % half_side)[None, :] < heights[:, quadrant]) & ((col_index % half_side)[None, :] < widths[:, quadrant])
    crops = jnp.where(inside, quadrant[None, :] + 1, 0)
    whole_map = (jnp.arange(MAPS) % 2 == 0)[:, None]
    return jnp.where(whole_map, 1, crops).astype(jnp.int32)


def levels(stream_key, shape, pieces, least, top_value):
    level, own = 1.0, jax.random.fold_in(stream_key, 6)
    for position, blocks in pieces:
        steps = jnp.exp(jax.random.uniform(jax.random.fold_in(own, position), (blocks,), jnp.float32, least / len(pieces), top_value / len(pieces)))
        level = level * jnp.repeat(steps, shape[position] // blocks).reshape([-1 if axis == position else 1 for axis in range(len(shape))])
    return level


def centred(rng, shape, width, most, cuts=(), kind=jnp.bfloat16):
    drawn = width * jax.random.normal(rng, shape, jnp.float32)
    if cuts:
        drawn = drawn * levels(rng, shape, cuts, -0.22, 0.18)
    return jnp.clip(drawn, -most, most).astype(kind)


def setup_inputs(seed: int = 0) -> dict:
    key_of = jax.random.split(jax.random.key(seed), 22)
    return {
        "inputs": draw_inputs(jax.random.fold_in(key_of[21], 71), 0),
        "embedding": centred(key_of[1], (MAPS, EMBED), 1.0, 6.0, ((0, 32),)),
        "region": draw_region(jax.random.fold_in(key_of[21], 71), 0),
        "cotangent": centred(key_of[3], (MAPS, PIXELS, WIDTH), 1.0, 6.0, ((0, 32),)),
        "conv_one": centred(key_of[4], (9 * WIDTH, WIDTH), (9 * WIDTH) ** -0.5, 0.109375, ((0, 8), (1, 4))),
        "bias_one": centred(key_of[5], (WIDTH,), 0.5, 3.0, (), jnp.float32),
        "conv_two": centred(key_of[6], (9 * WIDTH, WIDTH), (9 * WIDTH) ** -0.5, 0.109375, ((0, 8), (1, 4))),
        "bias_two": centred(key_of[7], (WIDTH,), 0.5, 3.0, (), jnp.float32),
        "emb_weight": centred(key_of[8], (EMBED, 2 * WIDTH), EMBED ** -0.5, 0.25, ((0, 8), (1, 4))),
        "emb_bias": centred(key_of[9], (2 * WIDTH,), 0.3, 2.0, (), jnp.float32),
        "qkv_weight": centred(key_of[10], (WIDTH, 3 * WIDTH), WIDTH ** -0.5, 0.3125, ((0, 8), (1, 4))),
        "q_bias": centred(key_of[11], (WIDTH,), 0.3, 2.0, (), jnp.float32),
        "v_bias": centred(key_of[12], (WIDTH,), 0.3, 2.0, (), jnp.float32),
        "proj_weight": centred(key_of[13], (WIDTH, WIDTH), (WIDTH // 32) ** -0.5, 1.75, ((0, 8), (1, 4))),
        "proj_bias": centred(key_of[14], (WIDTH,), 0.5, 3.0, (), jnp.float32),
        "gain_one": jnp.clip(1.0 + 0.18 * jax.random.normal(key_of[15], (WIDTH,), jnp.float32), 0.1, 1.9),
        "shift_one": centred(key_of[16], (WIDTH,), 0.5, 3.0, (), jnp.float32),
        "gain_two": jnp.clip(1.0 + 0.18 * jax.random.normal(key_of[17], (WIDTH,), jnp.float32), 0.1, 1.9),
        "shift_two": centred(key_of[18], (WIDTH,), 0.5, 3.0, (), jnp.float32),
        "gain_three": jnp.clip(1.0 + 0.18 * jax.random.normal(key_of[19], (WIDTH,), jnp.float32), 0.1, 1.9),
        "shift_three": centred(key_of[20], (WIDTH,), 0.5, 3.0, (), jnp.float32),
    }


@jax.custom_vjp
def low(v):
    return lax.optimization_barrier(v.astype(jnp.bfloat16)).astype(jnp.float32)

@jax.custom_vjp
def low_back(v):
    return v

def low_keep(v):
    return (low(v), None)

def low_pass(kept, grad):
    return (grad,)

def back_keep(v):
    return (v, None)

def back_low(kept, grad):
    return (low(grad),)
low.defvjp(low_keep, low_pass)
low_back.defvjp(back_keep, back_low)
EPS = 1e-05

def round_both(values):
    return low_back(low(values))

def group_norm(tensor, validity, gain_vec, bias_vec):
    number = tensor.shape[0]
    cells_total = lax.optimization_barrier(jnp.sum(validity, axis=1)) * (WIDTH // GROUPS)
    shaped = tensor.reshape(number, PIXELS, GROUPS, WIDTH // GROUPS)
    weight_mask = validity[..., None]
    group_sum = lax.optimization_barrier(jnp.sum(shaped * weight_mask, axis=(1, 3)))
    square = lax.optimization_barrier(jnp.sum(shaped * shaped * weight_mask, axis=(1, 3)))
    average = group_sum / cells_total
    spread = square / cells_total - average * average
    inverse = lax.rsqrt(spread + EPS)
    normed = (shaped - average[:, None, :, None]) * inverse[:, None, :, None]
    return normed.reshape(tensor.shape) * gain_vec + bias_vec

def convolve(tensor, kernel):
    number = tensor.shape[0]
    picture = tensor.reshape(number, SIDE, SIDE, WIDTH)
    result = lax.conv_general_dilated(picture, kernel.reshape(3, 3, WIDTH, WIDTH), (1, 1), 'SAME', dimension_numbers=('NHWC', 'HWIO', 'NHWC'), precision=lax.Precision.HIGHEST)
    return result.reshape(number, PIXELS, WIDTH)

def forward(inputs, embedding, validity, allowed, params):
    conv_one, bias_one, conv_two, bias_two, emb_weight, emb_bias, qkv_weight, q_bias, v_bias, proj_weight, proj_bias, gain_one, shift_one, gain_two, shift_two, gain_three, shift_three = params
    number = inputs.shape[0]
    highest = lax.Precision.HIGHEST
    normed_one = group_norm(inputs, validity, gain_one, shift_one)
    hidden_one = low(jax.nn.silu(normed_one) * validity)
    conv_out_one = low_back(convolve(hidden_one, conv_one) + bias_one)
    film_vector = jnp.dot(low(jax.nn.silu(embedding)), emb_weight, precision=highest) + emb_bias
    normed_two = group_norm(conv_out_one, validity, gain_two, shift_two) * (1.0 + film_vector[:, None, :WIDTH]) + film_vector[:, None, WIDTH:]
    hidden_two = low(jax.nn.silu(normed_two) * validity)
    conv_out_two = low_back(convolve(hidden_two, conv_two) + bias_two)
    residual = inputs + conv_out_two
    attend_in = low(group_norm(residual, validity, gain_three, shift_three))
    columns = jnp.einsum('bpc,cf->bpf', attend_in, qkv_weight, precision=highest).reshape(number, PIXELS, HEADS, 3, HEAD_DIM)
    queries = round_both(columns[:, :, :, 0] + q_bias.reshape(HEADS, HEAD_DIM))
    key_rows = round_both(columns[:, :, :, 1])
    value_rows = round_both(columns[:, :, :, 2] + v_bias.reshape(HEADS, HEAD_DIM))
    scores = low_back(jnp.einsum('bqhd,bkhd->bhqk', queries, key_rows, precision=highest) * HEAD_DIM ** (-0.5))
    scores = jnp.where(allowed[:, None], scores, -1e+30)
    weights = low(jax.nn.softmax(scores, axis=-1))
    attended = round_both(jnp.einsum('bhqk,bkhd->bqhd', weights, value_rows, precision=highest)).reshape(number, PIXELS, WIDTH)
    return residual + jnp.einsum('bpi,oi->bpo', attended, proj_weight, precision=highest) + proj_bias

def reference(inputs, embedding, region, cotangent, conv_one, bias_one, conv_two, bias_two, emb_weight, emb_bias, qkv_weight, q_bias, v_bias, proj_weight, proj_bias, gain_one, shift_one, gain_two, shift_two, gain_three, shift_three):
    params = tuple((weight_in.astype(jnp.float32) for weight_in in (conv_one, bias_one, conv_two, bias_two, emb_weight, emb_bias, qkv_weight, q_bias, v_bias, proj_weight, proj_bias, gain_one, shift_one, gain_two, shift_two, gain_three, shift_three)))
    per_step = 4
    num_steps = inputs.shape[0] // per_step

    def by_steps(values):
        return values.reshape((num_steps, per_step) + values.shape[1:])

    def advance(totals, batch_in):
        map_in, embed_in, region_in, grad_in = batch_in
        validity = (region_in > 0).astype(jnp.float32)[..., None]
        allowed = (region_in[:, None, :] > 0) & ((region_in[:, None, :] == region_in[:, :, None]) | (region_in[:, :, None] == 0))

        def apply_block(map_value, embed_value, param_value):
            return forward(map_value, embed_value, validity, allowed, param_value)
        result, pullback = jax.vjp(apply_block, map_in.astype(jnp.float32), embed_in.astype(jnp.float32), params)
        grad_map, grad_embed, grad_params = pullback(grad_in.astype(jnp.float32))
        totals = jax.tree.map(jnp.add, totals, grad_params)
        return (totals, (result.astype(jnp.bfloat16), grad_map.astype(jnp.bfloat16), grad_embed))
    initial = jax.tree.map(jnp.zeros_like, params)
    totals, stacked = lax.scan(advance, initial, (by_steps(inputs), by_steps(embedding), by_steps(region), by_steps(cotangent)))
    results, grad_maps, grad_embeds = stacked
    output = results.reshape(inputs.shape)
    grad_inputs = grad_maps.reshape(inputs.shape)
    grad_embedding = grad_embeds.reshape(embedding.shape)
    return (output, grad_inputs, grad_embedding, totals[0], totals[2], totals[4], totals[6], totals[9], totals[1], totals[3], totals[5], totals[7], totals[8], totals[10], totals[11], totals[12], totals[13], totals[14], totals[15], totals[16])
```

```python
import jax
import jax.numpy as jnp
from jax import lax
from jax.sharding import PartitionSpec as P

WIDTH = 384
HEAD_DIM = 96
GROUPS = 32
SIDE = 16
PIXELS = 256


EPS = 1e-05


def silu_slope(values):
    sigmoid_value = jax.nn.sigmoid(values)
    return sigmoid_value * (1.0 + values * (1.0 - sigmoid_value))


def norm_forward(tensor, validity, count_cells):
    number = tensor.shape[0]
    shaped = tensor.reshape(number, PIXELS, GROUPS, WIDTH // GROUPS)
    masked = shaped * validity[..., None]
    group_sum = jnp.sum(masked, axis=(1, 3))
    square = jnp.sum(masked * shaped, axis=(1, 3))
    average = group_sum / count_cells
    inverse = lax.rsqrt(square / count_cells - average * average + EPS)
    normed = (shaped - average[:, None, :, None]) * inverse[:, None, :, None]
    return (normed.reshape(tensor.shape), inverse)


def norm_backward(grad_hat, normed, inverse, validity, count_cells):
    number = grad_hat.shape[0]
    grad_shaped = grad_hat.reshape(number, PIXELS, GROUPS, WIDTH // GROUPS)
    hat_shaped = normed.reshape(number, PIXELS, GROUPS, WIDTH // GROUPS)
    along = jnp.sum(grad_shaped, axis=(1, 3))[:, None, :, None]
    cross = jnp.sum(grad_shaped * hat_shaped, axis=(1, 3))[:, None, :, None]
    correction = (along + cross * hat_shaped) * validity[..., None] / count_cells[:, None, :, None]
    grad_tensor = inverse[:, None, :, None] * (grad_shaped - correction)
    return grad_tensor.reshape(grad_hat.shape)


def tap_patches(tensor):
    number = tensor.shape[0]
    picture = tensor.reshape(number, SIDE, SIDE, WIDTH)
    padded = jnp.pad(picture, ((0, 0), (1, 1), (1, 1), (0, 0)))
    tap_list = [
        padded[:, row_shift : row_shift + SIDE, col_shift : col_shift + SIDE, :]
        for row_shift in range(3)
        for col_shift in range(3)
    ]
    return jnp.stack(tap_list, axis=3).reshape(number, PIXELS, 9, WIDTH)


def allowed_pairs(map_region):
    query_region = map_region[:, :, None]
    key_region = map_region[:, None, :]
    return (key_region > 0) & ((key_region == query_region) | (query_region == 0))


def score_block(queries, key_rows, allowed):
    logits = jnp.einsum(
        "bqhd,bkhd->bhqk", queries, key_rows, preferred_element_type=jnp.float32
    ) * HEAD_DIM ** (-0.5)
    return jnp.where(allowed[:, None], logits, -1e30)


def attend_forward(queries, key_rows, value_rows, allowed):
    logits = score_block(queries, key_rows, allowed)
    row_peak = jnp.max(logits, axis=-1, keepdims=True)
    raised = jnp.exp(logits - row_peak)
    denominator = jnp.sum(raised, axis=-1, keepdims=True)
    weights = (raised / denominator).astype(jnp.bfloat16)
    attended = jnp.einsum(
        "bhqk,bkhd->bqhd", weights, value_rows, preferred_element_type=jnp.float32
    ).astype(jnp.bfloat16)
    return (attended, row_peak + jnp.log(denominator))


def attend_backward(queries, key_rows, value_rows, allowed, log_total, grad_attended):
    factor = HEAD_DIM ** (-0.5)
    logits = score_block(queries, key_rows, allowed)
    weights_exact = jnp.where(allowed[:, None], jnp.exp(logits - log_total), 0.0)
    grad_weights = jnp.einsum(
        "bqhd,bkhd->bhqk", grad_attended, value_rows, preferred_element_type=jnp.float32
    )
    row_inner = jnp.sum(grad_weights * weights_exact, axis=-1, keepdims=True)
    grad_logits = (weights_exact * (grad_weights - row_inner)).astype(jnp.bfloat16)
    grad_query = (
        jnp.einsum("bhqk,bkhd->bqhd", grad_logits, key_rows, preferred_element_type=jnp.float32)
        * factor
    )
    grad_key = (
        jnp.einsum("bhqk,bqhd->bkhd", grad_logits, queries, preferred_element_type=jnp.float32)
        * factor
    )
    grad_value = jnp.einsum(
        "bhqk,bqhd->bkhd",
        weights_exact.astype(jnp.bfloat16),
        grad_attended,
        preferred_element_type=jnp.float32,
    )
    return jnp.stack([grad_query, grad_key, grad_value], axis=3).astype(jnp.bfloat16)


def swap_pairs(sizes, masks):
    count = sizes[0] * sizes[1]
    return [(own, own ^ masks[own % 2]) for own in range(count)]


def butterfly_masks(sizes):
    head_bits = [1 << k for k in range(1, sizes[1].bit_length() - 1)]
    dp_bits = [sizes[1] << k for k in range(sizes[0].bit_length() - 1)]
    early = dp_bits[:0:-1]
    late = head_bits + dp_bits[:1]
    stages = [(bit, bit) for bit in early]
    stages += list(zip(late, late[::-1]))
    return stages + [(1, 1)]


def block_places(sizes):
    stages = butterfly_masks(sizes)
    own = lax.axis_index(("dp", "head"))
    others = jnp.arange(sizes[0] * sizes[1])
    apart = others ^ own
    place = jnp.zeros_like(others)
    for step, (even, odd) in enumerate(stages):
        mask = jnp.where(others % 2 == 0, even, odd)
        place = place + jnp.where((apart & mask) != 0, 1 << step, 0)
    return place


def gather_weights(shards, sizes):
    flat = jnp.concatenate([shard.reshape(-1) for shard in shards])
    length = flat.shape[0]
    buffer = jnp.pad(flat, (0, -length % 1024)).reshape(1, -1, 128)
    for masks in butterfly_masks(sizes):
        other = lax.ppermute(buffer, ("dp", "head"), swap_pairs(sizes, masks))
        buffer = jnp.concatenate([buffer, other], axis=0)
    blocks = buffer[block_places(sizes)].reshape(sizes[0], sizes[1], -1)
    whole, start = [], 0
    for shard in shards:
        rows, cols = shard.shape
        part = blocks[:, :, start : start + rows * cols].reshape(sizes[0], sizes[1], rows, cols)
        whole.append(part.transpose(0, 2, 1, 3).reshape(sizes[0] * rows, sizes[1] * cols))
        start += rows * cols
    return whole


def scatter_grads(grads, shapes, sizes):
    parts = []
    for grad, (rows, cols) in zip(grads, shapes):
        part = grad.astype(jnp.bfloat16).reshape(sizes[0], rows, sizes[1], cols)
        parts.append(part.transpose(0, 2, 1, 3).reshape(sizes[0] * sizes[1], rows * cols))
    flat = jnp.concatenate(parts, axis=1)
    flat = jnp.pad(flat, ((0, 0), (0, -flat.shape[1] % 1024)))
    places = block_places(sizes)
    order = jnp.argsort(places)
    buffer = flat.reshape(flat.shape[0], -1, 128)[order]
    for masks in butterfly_masks(sizes)[::-1]:
        half = buffer.shape[0] // 2
        other = lax.ppermute(buffer[half:], ("dp", "head"), swap_pairs(sizes, masks))
        buffer = (buffer[:half].astype(jnp.float32) + other.astype(jnp.float32)).astype(
            jnp.bfloat16
        )
    flat = buffer.reshape(-1).astype(jnp.float32)
    result, start = [], 0
    for rows, cols in shapes:
        result.append(flat[start : start + rows * cols].reshape(rows, cols))
        start += rows * cols
    return result


def per_device(
    inputs,
    embedding,
    region,
    cotangent,
    conv_one,
    bias_one,
    conv_two,
    bias_two,
    emb_weight,
    emb_bias,
    qkv_weight,
    q_bias,
    v_bias,
    proj_weight,
    proj_bias,
    gain_one,
    shift_one,
    gain_two,
    shift_two,
    gain_three,
    shift_three,
):
    number = inputs.shape[0]
    head_id = lax.axis_index("head")
    highest = lax.Precision.HIGHEST
    sizes = (lax.axis_size("dp"), lax.axis_size("head"))
    (kernel_one,) = gather_weights((conv_one,), sizes)
    kernel_two, film_weight, attend_qkv, attend_proj = gather_weights(
        (conv_two, emb_weight, qkv_weight, proj_weight), sizes
    )
    head_count = WIDTH // HEAD_DIM
    kernel_one = kernel_one.reshape(9, WIDTH, WIDTH)
    kernel_two = kernel_two.reshape(9, WIDTH, WIDTH)
    region_own = lax.dynamic_slice_in_dim(region, head_id * number, number, 0)
    validity = (region_own > 0).astype(jnp.float32)[..., None]
    count_cells = jnp.sum(validity[..., 0], axis=1, keepdims=True) * (WIDTH // GROUPS)
    start_values = inputs.astype(jnp.float32)
    hat_one, inverse_one = norm_forward(start_values, validity, count_cells)
    normed_one = hat_one * gain_one + shift_one
    hidden_one = (jax.nn.silu(normed_one) * validity).astype(jnp.bfloat16)
    patches_one = tap_patches(hidden_one)
    conv_out_one = (
        jnp.einsum("bptc,tck->bpk", patches_one, kernel_one, preferred_element_type=jnp.float32)
        + bias_one
    )
    embed_low = jax.nn.silu(embedding.astype(jnp.float32)).astype(jnp.bfloat16)
    film_vector = jnp.dot(embed_low, film_weight, preferred_element_type=jnp.float32) + emb_bias
    scale_part = 1.0 + film_vector[:, None, :WIDTH]
    shift_part = film_vector[:, None, WIDTH:]
    hat_two, inverse_two = norm_forward(conv_out_one, validity, count_cells)
    modulated = hat_two * gain_two + shift_two
    normed_two = modulated * scale_part + shift_part
    hidden_two = (jax.nn.silu(normed_two) * validity).astype(jnp.bfloat16)
    patches_two = tap_patches(hidden_two)
    conv_out_two = (
        jnp.einsum("bptc,tck->bpk", patches_two, kernel_two, preferred_element_type=jnp.float32)
        + bias_two
    )
    residual = start_values + conv_out_two
    hat_three, inverse_three = norm_forward(residual, validity, count_cells)
    attend_local = (hat_three * gain_three + shift_three).astype(jnp.bfloat16)
    attend_in = attend_local
    query_add = q_bias.reshape(head_count, HEAD_DIM)
    value_add = v_bias.reshape(head_count, HEAD_DIM)
    group_count = attend_in.shape[0]
    allowed = allowed_pairs(region_own)
    columns = jnp.einsum(
        "bpc,cf->bpf", attend_in, attend_qkv, preferred_element_type=jnp.float32
    ).reshape(group_count, PIXELS, head_count, 3, HEAD_DIM)
    queries = (columns[:, :, :, 0] + query_add).astype(jnp.bfloat16)
    key_rows = columns[:, :, :, 1].astype(jnp.bfloat16)
    value_rows = (columns[:, :, :, 2] + value_add).astype(jnp.bfloat16)
    attended, log_total = attend_forward(queries, key_rows, value_rows, allowed)
    attended_flat = attended.reshape(group_count, PIXELS, head_count * HEAD_DIM)
    partial_out = jnp.einsum(
        "bpd,od->bpo", attended_flat, attend_proj, preferred_element_type=jnp.float32
    )
    projected = partial_out
    output = (residual + projected + proj_bias).astype(jnp.bfloat16)
    grad_top = cotangent.astype(jnp.float32)
    grad_full = cotangent
    grad_proj = jnp.einsum(
        "bpo,bpd->od", grad_full, attended_flat, preferred_element_type=jnp.float32
    )
    grad_attended = (
        jnp.einsum("bpo,od->bpd", grad_full, attend_proj, preferred_element_type=jnp.float32)
        .astype(jnp.bfloat16)
        .reshape(group_count, PIXELS, head_count, HEAD_DIM)
    )
    grad_qkv = attend_backward(
        queries, key_rows, value_rows, allowed, log_total, grad_attended
    ).reshape(group_count, PIXELS, head_count * 3 * HEAD_DIM)
    grad_qkv_weight = jnp.einsum(
        "bpc,bpf->cf", attend_in, grad_qkv, preferred_element_type=jnp.float32
    )
    bias_columns = jnp.sum(grad_qkv, axis=(0, 1), dtype=jnp.float32).reshape(
        head_count, 3, HEAD_DIM
    )
    grad_query_part = bias_columns[:, 0].reshape(head_count * HEAD_DIM)
    grad_value_part = bias_columns[:, 2].reshape(head_count * HEAD_DIM)
    grad_attend_full = jnp.einsum(
        "bpf,cf->bpc", grad_qkv, attend_qkv, preferred_element_type=jnp.float32
    )
    grad_q_bias, grad_v_bias = grad_query_part, grad_value_part
    grad_attend = grad_attend_full
    grad_gain_three = jnp.sum(grad_attend * hat_three, axis=(0, 1))
    grad_shift_three = jnp.sum(grad_attend, axis=(0, 1))
    grad_norm_three = norm_backward(
        grad_attend * gain_three, hat_three, inverse_three, validity, count_cells
    )
    grad_residual = grad_top + grad_norm_three
    grad_proj_bias = jnp.sum(grad_top, axis=(0, 1))
    grad_conv_two_out = grad_residual.astype(jnp.bfloat16)
    grad_bias_two = jnp.sum(grad_conv_two_out, axis=(0, 1), dtype=jnp.float32)
    grad_kernel_two = jnp.einsum(
        "bptc,bpk->tck", patches_two, grad_conv_two_out, preferred_element_type=jnp.float32
    ).reshape(9 * WIDTH, WIDTH)
    grad_patches_two = tap_patches(grad_conv_two_out)
    grad_hidden_two = jnp.einsum(
        "bptk,tck->bpc", grad_patches_two, kernel_two[::-1], preferred_element_type=jnp.float32
    )
    grad_normed_two = grad_hidden_two * validity * silu_slope(normed_two)
    grad_shift_film = jnp.sum(grad_normed_two, axis=1)
    grad_scale_film = jnp.sum(grad_normed_two * modulated, axis=1)
    grad_modulated = grad_normed_two * scale_part
    grad_gain_two = jnp.sum(grad_modulated * hat_two, axis=(0, 1))
    grad_shift_two = jnp.sum(grad_modulated, axis=(0, 1))
    grad_conv_one_in = norm_backward(
        grad_modulated * gain_two, hat_two, inverse_two, validity, count_cells
    )
    grad_film = jnp.concatenate([grad_scale_film, grad_shift_film], axis=1)
    grad_emb_weight = jnp.dot(embed_low.astype(jnp.float32).T, grad_film, precision=highest)
    grad_emb_bias = jnp.sum(grad_film, axis=0)
    grad_embedding = jnp.dot(
        grad_film, film_weight.astype(jnp.float32).T, precision=highest
    ) * silu_slope(embedding.astype(jnp.float32))
    grad_conv_one_out = grad_conv_one_in.astype(jnp.bfloat16)
    grad_bias_one = jnp.sum(grad_conv_one_out, axis=(0, 1), dtype=jnp.float32)
    grad_kernel_one = jnp.einsum(
        "bptc,bpk->tck", patches_one, grad_conv_one_out, preferred_element_type=jnp.float32
    ).reshape(9 * WIDTH, WIDTH)
    grad_patches_one = tap_patches(grad_conv_one_out)
    grad_hidden_one = jnp.einsum(
        "bptk,tck->bpc", grad_patches_one, kernel_one[::-1], preferred_element_type=jnp.float32
    )
    grad_normed_one = grad_hidden_one * validity * silu_slope(normed_one)
    grad_gain_one = jnp.sum(grad_normed_one * hat_one, axis=(0, 1))
    grad_shift_one = jnp.sum(grad_normed_one, axis=(0, 1))
    grad_norm_one = norm_backward(
        grad_normed_one * gain_one, hat_one, inverse_one, validity, count_cells
    )
    grad_inputs = (grad_residual + grad_norm_one).astype(jnp.bfloat16)
    finals_two = scatter_grads(
        (grad_kernel_two, grad_qkv_weight, grad_proj),
        (conv_two.shape, qkv_weight.shape, proj_weight.shape),
        sizes,
    )
    finals_one = scatter_grads(
        (grad_kernel_one, grad_emb_weight), (conv_one.shape, emb_weight.shape), sizes
    )
    finals = (finals_one[0], finals_two[0], finals_one[1], finals_two[1], finals_two[2])
    small = lax.psum(
        (
            grad_bias_one,
            grad_bias_two,
            grad_emb_bias,
            grad_q_bias,
            grad_v_bias,
            grad_proj_bias,
            grad_gain_one,
            grad_shift_one,
            grad_gain_two,
            grad_shift_two,
            grad_gain_three,
            grad_shift_three,
        ),
        ("dp", "head"),
    )
    return (
        output,
        grad_inputs,
        grad_embedding,
        finals[0],
        finals[1],
        finals[2],
        finals[3],
        finals[4],
        small[0],
        small[1],
        small[2],
        small[3],
        small[4],
        small[5],
        small[6],
        small[7],
        small[8],
        small[9],
        small[10],
        small[11],
    )


def solution(mesh):
    return jax.shard_map(
        per_device,
        mesh=mesh,
        in_specs=(
            P(("dp", "head"), None, None),
            P(("dp", "head"), None),
            P("dp", None),
            P(("dp", "head"), None, None),
            P("dp", "head"),
            P(),
            P("dp", "head"),
            P(),
            P("dp", "head"),
            P(),
            P("dp", "head"),
            P(),
            P(),
            P("dp", "head"),
            P(),
            P(),
            P(),
            P(),
            P(),
            P(),
            P(),
        ),
        out_specs=(
            P(("dp", "head"), None, None),
            P(("dp", "head"), None, None),
            P(("dp", "head"), None),
            P("dp", "head"),
            P("dp", "head"),
            P("dp", "head"),
            P("dp", "head"),
            P("dp", "head"),
            P(),
            P(),
            P(),
            P(),
            P(),
            P(),
            P(),
            P(),
            P(),
            P(),
            P(),
            P(),
        ),
        check_vma=False,
    )
```

```python
import functools

import jax
import jax.numpy as jnp
from jax import lax
from jax.experimental import pallas as pl
from jax.experimental.pallas import tpu as pltpu
from jax.sharding import PartitionSpec as P

WIDTH = 384
EMBED = 512
HEADS = 4
HEAD_DIM = 96
GROUP_SIZE = 12
SIDE = 16
PIXELS = 256
MAPS = 4
LANES = 128
TAPS = 9 * WIDTH
PADDED = PIXELS + 2 * SIDE
SLOTS = 3 * HEADS * LANES
FACTOR = HEAD_DIM ** (-0.5)
EPS = 1e-05
AXES = ("dp", "head")

BLOCK_GROUPS = 8
CONV_ROWS = TAPS // BLOCK_GROUPS
CONV_PACK = 336
CONV_MAIN = 320
EMB_PACK = 96
PROJ_PACK = 144

F32 = jnp.float32
BF16 = jnp.bfloat16
BIAS_ONE, BIAS_TWO, GAIN_ONE, SHIFT_ONE, GAIN_TWO, SHIFT_TWO, GAIN_THREE, SHIFT_THREE, PROJ_BIAS = (
    range(9)
)

VMEM = pl.BlockSpec(memory_space=pltpu.VMEM)
SMEM = pl.BlockSpec(memory_space=pltpu.SMEM)


def run_kernel(kernel, name, operands, outs, scratch=(), flops=0):
    specs = [SMEM if operand.dtype == jnp.int32 and operand.ndim == 1 else VMEM for operand in operands]
    moved = sum(value.size * value.dtype.itemsize for value in (*operands, *outs))
    return pl.pallas_call(
        kernel,
        out_shape=list(outs),
        in_specs=specs,
        out_specs=[VMEM] * len(outs),
        scratch_shapes=list(scratch),
        compiler_params=pltpu.CompilerParams(vmem_limit_bytes=48 * 2**20),
        cost_estimate=pl.CostEstimate(flops=flops, bytes_accessed=moved, transcendentals=0),
        name=name,
    )(*operands)


def shape_of(shape, dtype):
    return jax.ShapeDtypeStruct(shape, dtype)


def dot(left, right, dims=(1, 0)):
    return lax.dot_general(
        left, right, (((dims[0],), (dims[1],)), ((), ())), preferred_element_type=F32
    )


def group_total(rows, grouping):
    return lax.dot_general(
        rows,
        grouping,
        (((1,), (0,)), ((), ())),
        preferred_element_type=F32,
        precision=lax.Precision.HIGHEST,
    )


def sigmoid(values):
    return 1.0 / (1.0 + jnp.exp(-values))


def valid_of(region_ref, index):
    return (region_ref[index] > 0).astype(F32)


def cells_of(region_ref):
    counts = [jnp.sum(valid_of(region_ref, m), axis=0, keepdims=True) for m in range(MAPS)]
    return jnp.concatenate(counts, axis=0) * float(GROUP_SIZE)


def column_sum(values):
    return jnp.sum(values, axis=0, keepdims=True)


def store_shifted(target_ref, index, values):
    column = lax.broadcasted_iota(jnp.int32, (PIXELS, 1), 0) % SIDE
    left = jnp.where(column == 0, 0.0, pltpu.roll(values, 1, 0))
    right = jnp.where(column == SIDE - 1, 0.0, pltpu.roll(values, PIXELS - 1, 0))
    border = jnp.zeros((SIDE, 3 * WIDTH), BF16)
    target_ref[index, 0:SIDE, :] = border
    target_ref[index, SIDE + PIXELS : PADDED, :] = border
    for position, part in enumerate((left, values, right)):
        target_ref[index, SIDE : SIDE + PIXELS, position * WIDTH : (position + 1) * WIDTH] = (
            part.astype(BF16)
        )


def convolve(shifted_ref, index, weight_ref):
    total = None
    for tap_row in range(3):
        part = dot(
            shifted_ref[index, tap_row * SIDE : tap_row * SIDE + PIXELS, :],
            weight_ref[tap_row * 3 * WIDTH : (tap_row + 1) * 3 * WIDTH, :],
        )
        total = part if total is None else total + part
    return total


def flip_weight(flipped_ref, weight_ref):
    for tap_row in range(3):
        for tap_col in range(3):
            start = (3 * (2 - tap_row) + 2 - tap_col) * WIDTH
            flipped_ref[tap_row, :, tap_col * WIDTH : (tap_col + 1) * WIDTH] = weight_ref[
                start : start + WIDTH, :
            ]


def convolve_back(shifted_ref, index, flipped_ref):
    total = None
    for tap_row in range(3):
        part = dot(
            shifted_ref[index, tap_row * SIDE : tap_row * SIDE + PIXELS, :],
            flipped_ref[tap_row],
            (1, 1),
        )
        total = part if total is None else total + part
    return total


def pack_conv(shard):
    tail = shard[CONV_MAIN:]
    strips = jnp.concatenate([tail[:, 32 * k : 32 * k + 32] for k in range(3)], axis=0)
    main = jnp.concatenate([shard[:CONV_MAIN], jnp.zeros((16, HEAD_DIM), shard.dtype)], axis=0)
    return jnp.concatenate([main, strips], axis=1)


def pack_proj(qkv, proj):
    wide = jnp.concatenate([qkv, proj], axis=1)
    return jnp.concatenate([wide[:, LANES * k : LANES * (k + 1)] for k in range(3)], axis=0)


def pack_emb(shard):
    side = shard[:, LANES:]
    half = side.shape[0] // 2
    return jnp.concatenate(
        [shard[:, :LANES], jnp.concatenate([side[:half], side[half:]], axis=1)], axis=0
    )


def pack_kernel(conv_one, conv_two, emb, qkv, proj, first, second):
    first[0] = pack_conv(conv_one[...].astype(F32)).astype(BF16)
    second[0, 0:CONV_PACK] = pack_conv(conv_two[...].astype(F32)).astype(BF16)
    second[0, CONV_PACK : CONV_PACK + PROJ_PACK] = pack_proj(
        qkv[...].astype(F32), proj[...].astype(F32)
    ).astype(BF16)
    second[0, CONV_PACK + PROJ_PACK :] = pack_emb(emb[...].astype(F32)).astype(BF16)


def place_of(group, head, me_ref):
    far_group = group ^ me_ref[0]
    far_head = head ^ me_ref[1]
    over_y = far_group & 1
    over_x = far_head // 2
    place = (far_group // 4) + 2 * ((far_group // 2) & 1)
    if head % 2 == 0:
        place = place + 4 * over_x + 8 * over_y
    else:
        place = place + 4 * over_y + 8 * over_x
    return place + 16 * (far_head & 1)


def collect_blocks(parts, blocks):
    for index, part in enumerate(parts):
        blocks[8 * index : 8 * index + 8] = part[...]


def unpack_conv(blocks, me_ref, weight_ref):
    for group in range(BLOCK_GROUPS):
        mains, tails = [], []
        for head in range(HEADS):
            block = blocks[place_of(group, head, me_ref), 0:CONV_PACK].astype(F32)
            mains.append(block[:CONV_MAIN, :HEAD_DIM])
            tails += [block[112 * k : 112 * k + 112, HEAD_DIM:] for k in range(3)]
        start = group * CONV_ROWS
        weight_ref[start : start + CONV_MAIN] = jnp.concatenate(mains, axis=1).astype(BF16)
        weight_ref[start + CONV_MAIN : start + CONV_ROWS] = jnp.concatenate(tails, axis=1).astype(
            BF16
        )


def first_weights_kernel(me_ref, near, far, near_core, far_core, weight_ref, blocks):
    collect_blocks((near, far, near_core, far_core), blocks)
    unpack_conv(blocks, me_ref, weight_ref)


def second_weights_kernel(
    me_ref, near, far, near_core, far_core, conv_ref, emb_ref, qkv_ref, proj_ref, blocks
):
    collect_blocks((near, far, near_core, far_core), blocks)
    unpack_conv(blocks, me_ref, conv_ref)
    gap = jnp.zeros((48, LANES - HEAD_DIM), F32)
    for group in range(BLOCK_GROUPS):
        embs = []
        for head in range(HEADS):
            block = blocks[place_of(group, head, me_ref), CONV_PACK:].astype(F32)
            wide = jnp.concatenate([block[48 * k : 48 * k + 48] for k in range(3)], axis=1)
            rows = slice(48 * group, 48 * group + 48)
            for part in range(3):
                piece = wide[:, HEAD_DIM * part : HEAD_DIM * (part + 1)]
                slot = (3 * head + part) * LANES
                qkv_ref[rows, slot : slot + LANES] = jnp.concatenate([piece, gap], axis=1).astype(
                    BF16
                )
            proj_ref[rows, LANES * head : LANES * (head + 1)] = jnp.concatenate(
                [wide[:, 3 * HEAD_DIM :], gap], axis=1
            ).astype(BF16)
            emb = block[PROJ_PACK:]
            side = jnp.concatenate([emb[64:96, :64], emb[64:96, 64:]], axis=0)
            embs.append(jnp.concatenate([emb[:64], side], axis=1))
        emb_ref[64 * group : 64 * group + 64] = jnp.concatenate(embs, axis=1).astype(BF16)


def norm_stats(sums, squares, cells, grouping):
    totals = group_total(jnp.concatenate([sums, squares], axis=0), grouping)
    mean = totals[:MAPS] / cells
    inverse = lax.rsqrt(totals[MAPS:] / cells - mean * mean + EPS)
    return jnp.concatenate([mean, inverse], axis=0)


def norm_one_kernel(inputs, region, params, grouping, shifted, stats):
    sums, squares = [], []
    for m in range(MAPS):
        values = inputs[m].astype(F32)
        masked = values * valid_of(region, m)
        sums.append(column_sum(masked))
        squares.append(column_sum(masked * values))
    stats[...] = norm_stats(
        jnp.concatenate(sums, axis=0),
        jnp.concatenate(squares, axis=0),
        cells_of(region),
        grouping[...],
    )
    for m in range(MAPS):
        hat = (inputs[m].astype(F32) - stats[m : m + 1]) * stats[MAPS + m : MAPS + m + 1]
        normed = hat * params[GAIN_ONE : GAIN_ONE + 1] + params[SHIFT_ONE : SHIFT_ONE + 1]
        store_shifted(shifted, m, normed * sigmoid(normed) * valid_of(region, m))


def conv_one_kernel(shifted, weight, region, params, grouping, result, stats, sums):
    def one_map(m, carry):
        value = convolve(shifted, m, weight) + params[BIAS_ONE : BIAS_ONE + 1]
        result[m] = value
        masked = value * valid_of(region, m)
        sums[pl.ds(m, 1)] = column_sum(masked)
        sums[pl.ds(MAPS + m, 1)] = column_sum(masked * value)
        return carry

    lax.fori_loop(0, MAPS, one_map, 0)
    stats[...] = norm_stats(sums[:MAPS], sums[MAPS:], cells_of(region), grouping[...])


def modulate(value, stats, film, params, m):
    hat = (value - stats[pl.ds(m, 1)]) * stats[pl.ds(MAPS + m, 1)]
    modulated = hat * params[GAIN_TWO : GAIN_TWO + 1] + params[SHIFT_TWO : SHIFT_TWO + 1]
    scale = 1.0 + film[pl.ds(m, 1), :WIDTH]
    return hat, modulated, scale, modulated * scale + film[pl.ds(m, 1), WIDTH:]


def conv_two_kernel(
    conv_out, stats_two, inputs, embedding, emb_weight, emb_bias, weight, region, params, grouping,
    shifted, residual, attend_in, stats, film, sums,
):
    embed = embedding[...].astype(F32)
    film[...] = dot((embed * sigmoid(embed)).astype(BF16), emb_weight[...]) + emb_bias[...]

    def one_map(m, carry):
        _, _, _, normed = modulate(conv_out[m], stats_two, film, params, m)
        valid = valid_of(region, m)
        store_shifted(shifted, m, normed * sigmoid(normed) * valid)
        value = (
            inputs[m].astype(F32)
            + convolve(shifted, m, weight)
            + params[BIAS_TWO : BIAS_TWO + 1]
        )
        residual[m] = value
        sums[pl.ds(m, 1)] = column_sum(value * valid)
        sums[pl.ds(MAPS + m, 1)] = column_sum(value * value * valid)
        return carry

    lax.fori_loop(0, MAPS, one_map, 0)
    stats[...] = norm_stats(sums[:MAPS], sums[MAPS:], cells_of(region), grouping[...])
    for m in range(MAPS):
        hat = (residual[m] - stats[m : m + 1]) * stats[MAPS + m : MAPS + m + 1]
        attend_in[m] = (
            hat * params[GAIN_THREE : GAIN_THREE + 1] + params[SHIFT_THREE : SHIFT_THREE + 1]
        ).astype(BF16)


def norm_back(grad, hat, along, cross, inverse, valid, cells):
    return inverse * (grad - valid * (along + cross * hat) / cells)


def attend_kernel(
    attend_in, qkv_weight, qkv_bias, proj_weight, region, region_row, cotangent, residual, stats,
    params, grouping,
    output, grad_residual, grad_conv, grad_qkv_weight, grad_proj, bias_sums, small_sums,
    columns, grad_columns, attended, grad_attend, sums,
):
    def one_map(m, carry):
        rows = pl.ds(pl.multiple_of(m * PIXELS, PIXELS), PIXELS)
        columns[...] = (dot(attend_in[m], qkv_weight[...]) + qkv_bias[...]).astype(BF16)
        grad_attended = dot(cotangent[m], proj_weight[...]).astype(BF16)
        key_region = region[m]
        query_region = region_row[m]
        allowed = (key_region > 0) & ((key_region == query_region) | (query_region == 0))
        for head in range(HEADS):
            base = 3 * LANES * head
            queries = columns[:, base : base + LANES]
            keys = columns[:, base + LANES : base + 2 * LANES]
            values = columns[:, base + 2 * LANES : base + 3 * LANES]
            grad_out = grad_attended[:, LANES * head : LANES * (head + 1)]
            logits = jnp.where(allowed, dot(keys, queries, (1, 1)) * FACTOR, -1e30)
            raised = jnp.exp(logits - jnp.max(logits, axis=0, keepdims=True))
            weights = raised * (1.0 / jnp.sum(raised, axis=0, keepdims=True))
            weights_low = weights.astype(BF16)
            attended[rows, LANES * head : LANES * (head + 1)] = dot(
                weights_low, values, (0, 0)
            ).astype(BF16)
            grad_weights = dot(values, grad_out, (1, 1))
            inner = jnp.sum(grad_weights * weights, axis=0, keepdims=True)
            grad_logits = (weights * (grad_weights - inner)).astype(BF16)
            grad_columns[rows, base : base + LANES] = (
                dot(grad_logits, keys, (0, 0)) * FACTOR
            ).astype(BF16)
            grad_columns[rows, base + LANES : base + 2 * LANES] = (
                dot(grad_logits, queries) * FACTOR
            ).astype(BF16)
            grad_columns[rows, base + 2 * LANES : base + 3 * LANES] = dot(
                weights_low, grad_out
            ).astype(BF16)
        output[m] = (
            residual[m]
            + dot(attended[rows, :], proj_weight[...], (1, 1))
            + params[PROJ_BIAS : PROJ_BIAS + 1]
        ).astype(BF16)
        grad = dot(grad_columns[rows, :], qkv_weight[...], (1, 1))
        grad_attend[m] = grad
        hat = (residual[m] - stats[pl.ds(m, 1)]) * stats[pl.ds(MAPS + m, 1)]
        sums[pl.ds(m, 1)] = column_sum(grad)
        sums[pl.ds(MAPS + m, 1)] = column_sum(grad * hat)
        return carry

    lax.fori_loop(0, MAPS, one_map, 0)
    gain = params[GAIN_THREE : GAIN_THREE + 1]
    totals = group_total(sums[...] * gain, grouping[...])
    cells = cells_of(region)
    small_sums[...] = jnp.zeros_like(small_sums)
    small_sums[0:1] = column_sum(sums[MAPS:])
    small_sums[1:2] = column_sum(sums[:MAPS])
    top_sum = jnp.zeros((1, WIDTH), F32)
    low_sum = jnp.zeros((1, WIDTH), F32)
    for m in range(MAPS):
        inverse = stats[MAPS + m : MAPS + m + 1]
        hat = (residual[m] - stats[m : m + 1]) * inverse
        top = cotangent[m].astype(F32)
        grad = top + norm_back(
            grad_attend[m] * gain,
            hat,
            totals[m : m + 1],
            totals[MAPS + m : MAPS + m + 1],
            inverse,
            valid_of(region, m),
            cells[m : m + 1],
        )
        grad_residual[m] = grad
        low = grad.astype(BF16)
        grad_conv[m] = low
        top_sum = top_sum + column_sum(top)
        low_sum = low_sum + column_sum(low.astype(F32))
    small_sums[2:3] = top_sum
    small_sums[3:4] = low_sum
    bias_sums[...] = column_sum(grad_columns[...].astype(F32))
    for m in range(MAPS):
        rows = slice(m * PIXELS, (m + 1) * PIXELS)
        qkv_part = dot(attend_in[m], grad_columns[rows, :], (0, 0))
        proj_part = dot(cotangent[m], attended[rows, :], (0, 0))
        if m == 0:
            grad_qkv_weight[...] = qkv_part
            grad_proj[...] = proj_part
        else:
            grad_qkv_weight[...] += qkv_part
            grad_proj[...] += proj_part


def back_two_kernel(
    grad_conv, weight, conv_out, stats, film, embedding, emb_weight, region, params, grouping,
    grad_low, grad_film, grad_embed, small_sums,
    flipped, shifted, grad_normed, sums,
):
    flip_weight(flipped, weight)

    def one_map(m, carry):
        store_shifted(shifted, m, grad_conv[m].astype(F32))
        hat, modulated, scale, normed = modulate(conv_out[m], stats, film, params, m)
        logistic = sigmoid(normed)
        slope = logistic * (1.0 + normed * (1.0 - logistic)) * valid_of(region, m)
        grad = convolve_back(shifted, m, flipped) * slope
        grad_film[pl.ds(m, 1), :WIDTH] = column_sum(grad * modulated)
        grad_film[pl.ds(m, 1), WIDTH:] = column_sum(grad)
        scaled = grad * scale
        grad_normed[m] = scaled
        sums[pl.ds(m, 1)] = column_sum(scaled)
        sums[pl.ds(MAPS + m, 1)] = column_sum(scaled * hat)
        return carry

    lax.fori_loop(0, MAPS, one_map, 0)
    gain = params[GAIN_TWO : GAIN_TWO + 1]
    totals = group_total(sums[...] * gain, grouping[...])
    cells = cells_of(region)
    small_sums[...] = jnp.zeros_like(small_sums)
    small_sums[0:1] = column_sum(sums[MAPS:])
    small_sums[1:2] = column_sum(sums[:MAPS])
    low_sum = jnp.zeros((1, WIDTH), F32)
    for m in range(MAPS):
        inverse = stats[MAPS + m : MAPS + m + 1]
        low = norm_back(
            grad_normed[m] * gain,
            (conv_out[m] - stats[m : m + 1]) * inverse,
            totals[m : m + 1],
            totals[MAPS + m : MAPS + m + 1],
            inverse,
            valid_of(region, m),
            cells[m : m + 1],
        ).astype(BF16)
        grad_low[m] = low
        low_sum = low_sum + column_sum(low.astype(F32))
    small_sums[2:3] = low_sum
    embed = embedding[...].astype(F32)
    logistic = sigmoid(embed)
    film_high = grad_film[...].astype(BF16)
    film_rest = (grad_film[...] - film_high.astype(F32)).astype(BF16)
    grad_embed[...] = (
        dot(film_high, emb_weight[...], (1, 1)) + dot(film_rest, emb_weight[...], (1, 1))
    ) * (logistic * (1.0 + embed * (1.0 - logistic)))


def back_one_kernel(
    grad_conv, weight, inputs, stats, grad_residual, region, params, grouping,
    grad_inputs, small_sums,
    flipped, shifted, grad_normed, sums,
):
    flip_weight(flipped, weight)
    gain = params[GAIN_ONE : GAIN_ONE + 1]

    def one_map(m, carry):
        store_shifted(shifted, m, grad_conv[m].astype(F32))
        hat = (inputs[m].astype(F32) - stats[pl.ds(m, 1)]) * stats[pl.ds(MAPS + m, 1)]
        normed = hat * gain + params[SHIFT_ONE : SHIFT_ONE + 1]
        logistic = sigmoid(normed)
        slope = logistic * (1.0 + normed * (1.0 - logistic)) * valid_of(region, m)
        grad = convolve_back(shifted, m, flipped) * slope
        grad_normed[m] = grad
        sums[pl.ds(m, 1)] = column_sum(grad)
        sums[pl.ds(MAPS + m, 1)] = column_sum(grad * hat)
        return carry

    lax.fori_loop(0, MAPS, one_map, 0)
    totals = group_total(sums[...] * gain, grouping[...])
    cells = cells_of(region)
    small_sums[...] = jnp.zeros_like(small_sums)
    small_sums[0:1] = column_sum(sums[MAPS:])
    small_sums[1:2] = column_sum(sums[:MAPS])
    for m in range(MAPS):
        inverse = stats[MAPS + m : MAPS + m + 1]
        grad_inputs[m] = (
            grad_residual[m]
            + norm_back(
                grad_normed[m] * gain,
                (inputs[m].astype(F32) - stats[m : m + 1]) * inverse,
                totals[m : m + 1],
                totals[MAPS + m : MAPS + m + 1],
                inverse,
                valid_of(region, m),
                cells[m : m + 1],
            )
        ).astype(BF16)


def conv_weight_grads(shifted, grad_conv, turned, total):
    for m in range(MAPS):
        turned[:, m * PIXELS : (m + 1) * PIXELS] = grad_conv[m].astype(F32).T.astype(BF16)

    def one_row(tap_row, carry):
        rows = pl.ds(pl.multiple_of(tap_row * SIDE, SIDE), PIXELS)
        part = dot(turned[:, 0:PIXELS], shifted[0, rows, :])
        for m in range(1, MAPS):
            part += dot(turned[:, m * PIXELS : (m + 1) * PIXELS], shifted[m, rows, :])
        total[tap_row] = part
        return carry

    lax.fori_loop(0, 3, one_row, 0)


def pack_conv_grads(total, me_ref, blocks):
    for group in range(BLOCK_GROUPS):
        start, stop = group * CONV_ROWS, (group + 1) * CONV_ROWS
        pieces = []
        for tap_row in range(3):
            low, high = tap_row * 3 * WIDTH, (tap_row + 1) * 3 * WIDTH
            if max(low, start) < min(high, stop):
                pieces.append((tap_row, max(low, start) - low, min(high, stop) - low))
        for head in range(HEADS):
            rows = slice(HEAD_DIM * head, HEAD_DIM * (head + 1))
            values = [total[tap_row, rows, a:b] for tap_row, a, b in pieces]
            block = values[0] if len(values) == 1 else jnp.concatenate(values, axis=1)
            place = place_of(group, head, me_ref)
            for part in range(3):
                blocks[place, HEAD_DIM * part : HEAD_DIM * (part + 1), :] = block[
                    :, LANES * part : LANES * (part + 1)
                ].astype(BF16)
            tail = block[:, 3 * LANES :]
            blocks[place, 288:CONV_PACK, :] = jnp.concatenate(
                [tail[:48], tail[48:], jnp.zeros((48, 32), F32)], axis=1
            ).astype(BF16)


def split_blocks(blocks, parts):
    for index, part in enumerate(parts):
        part[...] = blocks[8 * index : 8 * index + 8]


def grads_one_kernel(
    me_ref, shifted, grad_conv, near, far, near_core, far_core, turned, total, blocks
):
    conv_weight_grads(shifted, grad_conv, turned, total)
    pack_conv_grads(total, me_ref, blocks)
    split_blocks(blocks, (near, far, near_core, far_core))


def grads_two_kernel(
    me_ref, shifted, grad_conv, grad_qkv, grad_proj, near, far, near_core, far_core, turned, total,
    blocks,
):
    conv_weight_grads(shifted, grad_conv, turned, total)
    pack_conv_grads(total, me_ref, blocks)
    for group in range(BLOCK_GROUPS):
        rows = slice(48 * group, 48 * group + 48)
        for head in range(HEADS):
            pieces = [
                grad_qkv[rows, slot * LANES : slot * LANES + HEAD_DIM]
                for slot in range(3 * head, 3 * head + 3)
            ]
            pieces.append(grad_proj[rows, head * LANES : head * LANES + HEAD_DIM])
            wide = jnp.concatenate(pieces, axis=1)
            place = place_of(group, head, me_ref)
            for part in range(3):
                start = CONV_PACK + 48 * part
                blocks[place, start : start + 48, :] = wide[
                    :, LANES * part : LANES * (part + 1)
                ].astype(BF16)
    split_blocks(blocks, (near, far, near_core, far_core))


def unpack_conv_grad(block):
    wide = jnp.concatenate(
        [block[HEAD_DIM * k : HEAD_DIM * (k + 1)] for k in range(3)]
        + [
            jnp.concatenate(
                [
                    jnp.concatenate([block[288:336, :48], block[288:336, 48:96]], axis=0),
                    jnp.zeros((HEAD_DIM, 80), F32),
                ],
                axis=1,
            )
        ],
        axis=1,
    )
    wide = jnp.concatenate([wide, jnp.zeros((32, 512), F32)], axis=0)
    return wide.T[:CONV_ROWS, :HEAD_DIM]


def finish_one_kernel(mine, other, result):
    result[...] = unpack_conv_grad(mine[0].astype(F32) + other[0].astype(F32))


def finish_two_kernel(mine, other, result, qkv, proj):
    block = mine[0].astype(F32) + other[0].astype(F32)
    result[...] = unpack_conv_grad(block[:CONV_PACK])
    start = CONV_PACK
    wide = jnp.concatenate([block[start + 48 * k : start + 48 * k + 48] for k in range(3)], axis=1)
    qkv[...] = wide[:, : 3 * HEAD_DIM]
    proj[...] = wide[:, 3 * HEAD_DIM :]


def swap(values, masks, sizes):
    pairs = [(own, own ^ masks[own % 2]) for own in range(sizes[0] * sizes[1])]
    return lax.ppermute(values, AXES, pairs)


def stages_of(sizes):
    inner = sizes[0] // BLOCK_GROUPS
    group_bit = sizes[1] * inner
    over_x, over_y = 2, group_bit
    return ((4 * group_bit,) * 2, (2 * group_bit,) * 2, (over_x, over_y), (over_y, over_x))


def gather_blocks(block, sizes):
    first, second, third, fourth = stages_of(sizes)
    held = block
    for masks in (first, second, third):
        held = jnp.concatenate([held, swap(held, masks, sizes)], axis=0)
    far = swap(held, fourth, sizes)
    return held, far, swap(held, (1, 1), sizes), swap(far, (1, 1), sizes)


def add_low(left, right):
    return (left.astype(F32) + right.astype(F32)).astype(BF16)


def reduce_blocks(near, far, near_core, far_core, sizes):
    first, second, third, fourth = stages_of(sizes)
    far = add_low(far, swap(far_core, (1, 1), sizes))
    near = add_low(near, swap(near_core, (1, 1), sizes))
    other = swap(far, fourth, sizes)
    for masks in (third, second, first):
        half = near.shape[0] // 2
        send = add_low(near[half:], other[half:])
        near = add_low(near[:half], other[:half])
        other = swap(send, masks, sizes)
    return near, other


def sum_and_gather(sums, rows, sizes):
    first, second, third, fourth = stages_of(sizes)
    for masks in (first, second, third, fourth, (1, 1)):
        other_sums, other_rows = swap((sums, rows), masks, sizes)
        sums = sums + other_sums
        rows = jnp.concatenate([rows, other_rows], axis=0)
    return sums, rows


def inner_groups(sizes):
    inner = sizes[0] // BLOCK_GROUPS
    return [[group * inner + k for k in range(inner)] for group in range(BLOCK_GROUPS)]


def inner_gather(shard, sizes):
    if sizes[0] == BLOCK_GROUPS:
        return shard
    return lax.all_gather(shard, "dp", axis=0, tiled=True, axis_index_groups=inner_groups(sizes))


def inner_scatter(grad, sizes):
    if sizes[0] == BLOCK_GROUPS:
        return grad
    return lax.psum_scatter(
        grad, "dp", scatter_dimension=0, tiled=True, axis_index_groups=inner_groups(sizes)
    )


def per_device(
    inputs, embedding, region, cotangent, conv_one, bias_one, conv_two, bias_two, emb_weight,
    emb_bias, qkv_weight, q_bias, v_bias, proj_weight, proj_bias, gain_one, shift_one, gain_two,
    shift_two, gain_three, shift_three,
):
    sizes = (lax.axis_size("dp"), lax.axis_size("head"))
    inner = sizes[0] // BLOCK_GROUPS
    dp_id, head_id = lax.axis_index("dp"), lax.axis_index("head")
    me = jnp.stack([dp_id // inner, head_id]).astype(jnp.int32)
    kernel = functools.partial
    map_shape = (MAPS, PIXELS, WIDTH)
    shifted_shape = (MAPS, PADDED, 3 * WIDTH)
    conv_flops = 2 * MAPS * PIXELS * TAPS * WIDTH

    shards = [inner_gather(w, sizes) for w in (conv_one, conv_two, emb_weight, qkv_weight, proj_weight)]
    second_rows = CONV_PACK + PROJ_PACK + EMB_PACK
    pack_one, pack_two = run_kernel(
        pack_kernel,
        "pack_weights",
        shards,
        (shape_of((1, CONV_PACK, LANES), BF16), shape_of((1, second_rows, LANES), BF16)),
    )
    blocks_one = gather_blocks(pack_one, sizes)
    blocks_two = gather_blocks(pack_two, sizes)

    region_own = lax.dynamic_slice_in_dim(region, head_id * MAPS, MAPS, 0)
    region_col = region_own.reshape(MAPS, PIXELS, 1)
    region_row = region_own.reshape(MAPS, 1, PIXELS)
    params = jnp.stack(
        [bias_one, bias_two, gain_one, shift_one, gain_two, shift_two, gain_three, shift_three, proj_bias]
        + [jnp.zeros_like(bias_one)] * 7
    )
    channel = jnp.arange(WIDTH) // GROUP_SIZE
    grouping = (channel[:, None] == channel[None, :]).astype(F32)
    qkv_bias = jnp.zeros((HEADS, 3, LANES), F32)
    qkv_bias = qkv_bias.at[:, 0, :HEAD_DIM].set(q_bias.reshape(HEADS, HEAD_DIM))
    qkv_bias = qkv_bias.at[:, 2, :HEAD_DIM].set(v_bias.reshape(HEADS, HEAD_DIM)).reshape(1, SLOTS)

    stats_shape = shape_of((2 * MAPS, WIDTH), F32)
    small_shape = shape_of((8, WIDTH), F32)
    sums_scratch = pltpu.VMEM((2 * MAPS, WIDTH), F32)
    shifted_one, stats_one = run_kernel(
        norm_one_kernel,
        "norm_one",
        (inputs, region_col, params, grouping),
        (shape_of(shifted_shape, BF16), stats_shape),
    )
    (weight_one,) = run_kernel(
        first_weights_kernel,
        "first_weights",
        (me, *blocks_one),
        (shape_of((TAPS, WIDTH), BF16),),
        (pltpu.VMEM((32, CONV_PACK, LANES), BF16),),
    )
    conv_out, stats_two = run_kernel(
        conv_one_kernel,
        "conv_one",
        (shifted_one, weight_one, region_col, params, grouping),
        (shape_of(map_shape, F32), stats_shape),
        (sums_scratch,),
        conv_flops,
    )
    weight_two, film_weight, attend_weight, attend_proj = run_kernel(
        second_weights_kernel,
        "second_weights",
        (me, *blocks_two),
        (
            shape_of((TAPS, WIDTH), BF16),
            shape_of((EMBED, 2 * WIDTH), BF16),
            shape_of((WIDTH, SLOTS), BF16),
            shape_of((WIDTH, HEADS * LANES), BF16),
        ),
        (pltpu.VMEM((32, second_rows, LANES), BF16),),
    )
    shifted_two, residual, attend_in, stats_three, film = run_kernel(
        conv_two_kernel,
        "conv_two",
        (
            conv_out, stats_two, inputs, embedding, film_weight, emb_bias.reshape(1, 2 * WIDTH),
            weight_two, region_col, params, grouping,
        ),
        (
            shape_of(shifted_shape, BF16),
            shape_of(map_shape, F32),
            shape_of(map_shape, BF16),
            stats_shape,
            shape_of((MAPS, 2 * WIDTH), F32),
        ),
        (sums_scratch,),
        conv_flops,
    )
    output, grad_residual, grad_conv_two, grad_qkv, grad_proj, column_sums, small_three = run_kernel(
        attend_kernel,
        "attend",
        (
            attend_in, attend_weight, qkv_bias, attend_proj, region_col, region_row, cotangent,
            residual, stats_three, params, grouping,
        ),
        (
            shape_of(map_shape, BF16),
            shape_of(map_shape, F32),
            shape_of(map_shape, BF16),
            shape_of((WIDTH, SLOTS), F32),
            shape_of((WIDTH, HEADS * LANES), F32),
            shape_of((1, SLOTS), F32),
            small_shape,
        ),
        (
            pltpu.VMEM((PIXELS, SLOTS), BF16),
            pltpu.VMEM((MAPS * PIXELS, SLOTS), BF16),
            pltpu.VMEM((MAPS * PIXELS, HEADS * LANES), BF16),
            pltpu.VMEM(map_shape, F32),
            sums_scratch,
        ),
        2 * conv_flops,
    )
    grads_scratch = (
        pltpu.VMEM((WIDTH, MAPS * PIXELS), BF16),
        pltpu.VMEM((3, WIDTH, 3 * WIDTH), F32),
    )
    grads_rows = CONV_PACK + PROJ_PACK
    terms_two = run_kernel(
        grads_two_kernel,
        "weight_grads_two",
        (me, shifted_two, grad_conv_two, grad_qkv, grad_proj),
        (shape_of((8, grads_rows, LANES), BF16),) * 4,
        grads_scratch + (pltpu.VMEM((32, grads_rows, LANES), BF16),),
        conv_flops,
    )
    parts_two = reduce_blocks(*terms_two, sizes)
    back_scratch = (
        pltpu.VMEM((3, WIDTH, 3 * WIDTH), BF16),
        pltpu.VMEM(shifted_shape, BF16),
        pltpu.VMEM(map_shape, F32),
        sums_scratch,
    )
    grad_conv_one, grad_film, grad_embedding, small_two = run_kernel(
        back_two_kernel,
        "back_two",
        (
            grad_conv_two, weight_two, conv_out, stats_two, film, embedding, film_weight,
            region_col, params, grouping,
        ),
        (
            shape_of(map_shape, BF16),
            shape_of((MAPS, 2 * WIDTH), F32),
            shape_of((MAPS, EMBED), F32),
            small_shape,
        ),
        back_scratch,
        conv_flops,
    )
    terms_one = run_kernel(
        grads_one_kernel,
        "weight_grads_one",
        (me, shifted_one, grad_conv_one),
        (shape_of((8, CONV_PACK, LANES), BF16),) * 4,
        grads_scratch + (pltpu.VMEM((32, CONV_PACK, LANES), BF16),),
        conv_flops,
    )
    parts_one = reduce_blocks(*terms_one, sizes)
    grad_inputs, small_one = run_kernel(
        back_one_kernel,
        "back_one",
        (grad_conv_one, weight_one, inputs, stats_one, grad_residual, region_col, params, grouping),
        (shape_of(map_shape, BF16), small_shape),
        back_scratch,
        conv_flops,
    )

    embed = embedding.astype(F32)
    embed_low = jax.nn.silu(embed).astype(BF16).astype(F32)
    film_sums = jnp.sum(grad_film, axis=0).reshape(2, WIDTH)
    slots = column_sums.reshape(HEADS, 3, LANES)[:, :, :HEAD_DIM]
    sums = jnp.concatenate(
        [
            small_one[:2],
            small_two[:3],
            small_three[:4],
            film_sums,
            slots[:, 0].reshape(1, WIDTH),
            slots[:, 2].reshape(1, WIDTH),
        ]
    )
    sums, rows = sum_and_gather(sums, jnp.concatenate([embed_low, grad_film], axis=1), sizes)
    own_embed = lax.dynamic_slice_in_dim(rows, dp_id * emb_weight.shape[0], emb_weight.shape[0], 1)
    own_film = lax.dynamic_slice_in_dim(
        rows, EMBED + head_id * emb_weight.shape[1], emb_weight.shape[1], 1
    )
    grad_emb_weight = jnp.dot(own_embed.T, own_film, precision=lax.Precision.HIGHEST)
    conv_grad_shape = shape_of((CONV_ROWS, HEAD_DIM), F32)
    grad_weight_two, grad_qkv_weight, grad_proj_weight = run_kernel(
        finish_two_kernel,
        "finish_two",
        parts_two,
        (conv_grad_shape, shape_of((48, 3 * HEAD_DIM), F32), shape_of((48, HEAD_DIM), F32)),
    )
    (grad_weight_one,) = run_kernel(finish_one_kernel, "finish_one", parts_one, (conv_grad_shape,))
    finals = [
        inner_scatter(grad, sizes)
        for grad in (grad_weight_one, grad_weight_two, grad_qkv_weight, grad_proj_weight)
    ]
    return (
        output,
        grad_inputs,
        grad_embedding,
        finals[0],
        finals[1],
        grad_emb_weight,
        finals[2],
        finals[3],
        sums[4],
        sums[8],
        sums[9:11].reshape(2 * WIDTH),
        sums[11],
        sums[12],
        sums[7],
        sums[0],
        sums[1],
        sums[2],
        sums[3],
        sums[5],
        sums[6],
    )


def solution(mesh):
    own = P(AXES)
    split = P("dp", "head")
    whole = P()
    in_specs = (own, own, P("dp"), own, split, whole, split, whole, split, whole, split) + (
        (whole, whole, split) + (whole,) * 7
    )
    out_specs = (own,) * 3 + (split,) * 5 + (whole,) * 12
    return jax.shard_map(
        per_device, mesh=mesh, in_specs=in_specs, out_specs=out_specs, check_vma=False
    )
```

```python
import functools

import jax
import jax.numpy as jnp
from jax import lax
from jax.experimental import pallas as pl
from jax.experimental.pallas import tpu as pltpu
from jax.sharding import PartitionSpec as P

WIDTH = 384
EMBED = 512
HEADS = 4
HEAD_DIM = 96
GROUP_SIZE = 12
SIDE = 16
PIXELS = 256
MAPS = 4
LANES = 128
TAPS = 9 * WIDTH
PADDED = PIXELS + 2 * SIDE
SLOTS = 3 * HEADS * LANES
FACTOR = HEAD_DIM ** (-0.5)
EPS = 1e-05
AXES = ("dp", "head")

BLOCK_GROUPS = 8
CONV_ROWS = TAPS // BLOCK_GROUPS
CONV_PACK = 336
EMB_PACK = 96
PROJ_PACK = 144
SECOND_ROWS = CONV_PACK + EMB_PACK
ROOM = 28

F32 = jnp.float32
BF16 = jnp.bfloat16
BIAS_ONE, BIAS_TWO, GAIN_ONE, SHIFT_ONE, GAIN_TWO, SHIFT_TWO, GAIN_THREE, SHIFT_THREE, PROJ_BIAS = (
    range(9)
)

VMEM = pl.BlockSpec(memory_space=pltpu.VMEM)
SMEM = pl.BlockSpec(memory_space=pltpu.SMEM)


def after(value, *others):
    return lax.optimization_barrier((value, *others))[0]


class Moved:
    def __init__(self, pairs, semaphores, ref):
        self.pairs, self.semaphores, self.ref = pairs, semaphores, ref

    def copy(self, piece):
        source, target = self.pairs(piece)
        return pltpu.make_async_copy(source, target, self.semaphores.at[piece])

    def start(self, piece=0):
        self.copy(piece).start()

    def wait(self, piece=0):
        self.copy(piece).wait()

    def wait_all(self):
        for piece in range(self.semaphores.shape[0]):
            self.wait(piece)


def count_of(shape):
    return shape[0] if len(shape) == 3 else 1


def piece_of(ref, piece):
    return ref.at[piece] if len(ref.shape) == 3 else ref


class Parts:
    def __init__(self, parts, ref):
        self.parts, self.ref = parts, ref

    def wait_all(self):
        first = self.ref.shape[1] - self.parts[0].shape[1]
        for index, part in enumerate(self.parts):
            self.ref[8 * index : 8 * index + 8, first:] = part[...]


def run_kernel(
    kernel, name, operands, outs, scratch=(), room=ROOM, fetch=(), flush=(), double=(), blocks=None,
    terms=False,
):
    operands = tuple(operands)
    plain = len(operands) - (4 if blocks else 0)
    direct = len(outs) - (4 if terms else 0)
    outs = tuple(outs) + tuple(outs[k] for k in double)
    any_space = pl.BlockSpec(memory_space=pltpu.HBM)
    in_specs = []
    for position, operand in enumerate(operands):
        if position in fetch:
            in_specs.append(any_space)
        else:
            in_specs.append(SMEM if operand.dtype == jnp.int32 and operand.ndim == 1 else VMEM)
    plain_outs = len(outs) - len(double)
    out_specs = [any_space if k in flush or k >= plain_outs else VMEM for k in range(len(outs))]
    scratch = list(scratch)
    own = len(scratch)
    for position in fetch:
        scratch.append(pltpu.VMEM(operands[position].shape, operands[position].dtype))
        scratch.append(pltpu.SemaphoreType.DMA((count_of(operands[position].shape),)))
    for position in flush:
        scratch.append(pltpu.VMEM(outs[position].shape, outs[position].dtype))
        scratch.append(pltpu.SemaphoreType.DMA((count_of(outs[position].shape),)))
    for position in double:
        scratch.append(pltpu.SemaphoreType.DMA((count_of(outs[position].shape),)))
    if blocks:
        scratch.append(pltpu.VMEM(blocks, BF16))

    def body(*refs):
        ins = list(refs[: len(operands)])
        results = list(refs[len(operands) : len(operands) + len(outs)])
        spare = list(refs[len(operands) + len(outs) :])
        given, extra = spare[:own], spare[own:]
        for position in fetch:
            target, semaphores = extra.pop(0), extra.pop(0)
            source = ins[position]
            ins[position] = Moved(
                lambda k, s=source, t=target: (piece_of(s, k), piece_of(t, k)), semaphores, target
            )
            for k in range(semaphores.shape[0]):
                ins[position].start(k)
        sent = []
        for position in flush:
            source, semaphores = extra.pop(0), extra.pop(0)
            target = results[position]
            results[position] = Moved(
                lambda k, s=source, t=target: (piece_of(s, k), piece_of(t, k)), semaphores, source
            )
            sent.append(results[position])
        for order, position in enumerate(double):
            source, semaphores = results[position], extra.pop(0)
            target = results[plain_outs + order]
            results[position] = Moved(
                lambda k, s=source, t=target: (piece_of(s, k), piece_of(t, k)), semaphores, source
            )
            sent.append(results[position])
        held = [Parts(ins[plain:], extra.pop(0))] if blocks else []
        kernel(*ins[:plain], *held, *results[:direct], *given)
        if terms:
            for k in range(4):
                results[direct + k][...] = given[-1][8 * k : 8 * k + 8]
        for moved in sent:
            moved.wait_all()

    return pl.pallas_call(
        body,
        out_shape=list(outs),
        in_specs=in_specs,
        out_specs=out_specs,
        scratch_shapes=scratch,
        compiler_params=pltpu.CompilerParams(vmem_limit_bytes=room * 2**20),
        cost_estimate=pl.CostEstimate(flops=0, bytes_accessed=0, transcendentals=0),
        name=name,
    )(*operands)


def shape_of(shape, dtype):
    return jax.ShapeDtypeStruct(shape, dtype)


def dot(left, right, dims=(1, 0)):
    return lax.dot_general(
        left, right, (((dims[0],), (dims[1],)), ((), ())), preferred_element_type=F32
    )


def group_total(rows, grouping):
    return lax.dot_general(
        rows,
        grouping,
        (((1,), (0,)), ((), ())),
        preferred_element_type=F32,
        precision=lax.Precision.HIGHEST,
    )


def sigmoid(values):
    return 1.0 / (1.0 + jnp.exp(-values))


def valid_of(region_ref, index):
    return (region_ref[index] > 0).astype(F32)


def cells_of(region_ref):
    counts = [jnp.sum(valid_of(region_ref, m), axis=0, keepdims=True) for m in range(MAPS)]
    return jnp.concatenate(counts, axis=0) * float(GROUP_SIZE)


def column_sum(values):
    return jnp.sum(values, axis=0, keepdims=True)


def store_shifted(target_ref, index, values):
    column = lax.broadcasted_iota(jnp.int32, (PIXELS, 1), 0) % SIDE
    left = jnp.where(column == 0, 0.0, pltpu.roll(values, 1, 0))
    right = jnp.where(column == SIDE - 1, 0.0, pltpu.roll(values, PIXELS - 1, 0))
    border = jnp.zeros((SIDE, 3 * WIDTH), BF16)
    target_ref[index, 0:SIDE, :] = border
    target_ref[index, SIDE + PIXELS : PADDED, :] = border
    for position, part in enumerate((left, values, right)):
        target_ref[index, SIDE : SIDE + PIXELS, position * WIDTH : (position + 1) * WIDTH] = (
            part.astype(BF16)
        )


def convolve(shifted_ref, index, weight_ref):
    total = None
    for tap_row in range(3):
        part = dot(
            shifted_ref[index, tap_row * SIDE : tap_row * SIDE + PIXELS, :],
            weight_ref[:, tap_row * 3 * WIDTH : (tap_row + 1) * 3 * WIDTH],
            (1, 1),
        )
        total = part if total is None else total + part
    return total


def flip_weight(flipped_ref, weight_ref):
    for tap_row in range(3):
        for tap_col in range(3):
            start = (3 * (2 - tap_row) + 2 - tap_col) * WIDTH
            flipped_ref[tap_row, tap_col * WIDTH : (tap_col + 1) * WIDTH, :] = weight_ref[
                :, start : start + WIDTH
            ]


def convolve_back(shifted_ref, index, flipped_ref):
    total = None
    for tap_row in range(3):
        part = dot(
            shifted_ref[index, tap_row * SIDE : tap_row * SIDE + PIXELS, :],
            flipped_ref[tap_row],
        )
        total = part if total is None else total + part
    return total


def pack_conv(shard):
    tail = shard[:, 3 * LANES :]
    parts = [shard[:, LANES * k : LANES * (k + 1)] for k in range(3)]
    parts.append(jnp.concatenate([tail[:48], tail[48:], jnp.zeros((48, 32), shard.dtype)], axis=1))
    return jnp.concatenate(parts, axis=0)


def pack_proj(qkv, proj):
    wide = jnp.concatenate([qkv, proj], axis=1)
    return jnp.concatenate([wide[:, LANES * k : LANES * (k + 1)] for k in range(3)], axis=0)


def pack_emb(shard):
    side = shard[:, LANES:]
    half = side.shape[0] // 2
    return jnp.concatenate(
        [shard[:, :LANES], jnp.concatenate([side[:half], side[half:]], axis=1)], axis=0
    )


def prepare_kernel(
    me_ref, region, bias_one, bias_two, gain_one, shift_one, gain_two, shift_two, gain_three,
    shift_three, proj_bias, q_bias, v_bias, emb_bias,
    params, qkv_bias, film_bias, region_col, region_row, grouping,
):
    vectors = (
        bias_one, bias_two, gain_one, shift_one, gain_two, shift_two, gain_three, shift_three,
        proj_bias,
    )
    for row, vector in enumerate(vectors):
        params[row : row + 1, :] = vector[...].reshape(1, WIDTH)
    queries, values = q_bias[...].reshape(1, WIDTH), v_bias[...].reshape(1, WIDTH)
    gap = jnp.zeros((1, LANES - HEAD_DIM), F32)
    for head in range(HEADS):
        part = slice(HEAD_DIM * head, HEAD_DIM * (head + 1))
        base = 3 * LANES * head
        qkv_bias[:, base : base + LANES] = jnp.concatenate([queries[:, part], gap], axis=1)
        qkv_bias[:, base + LANES : base + 2 * LANES] = jnp.zeros((1, LANES), F32)
        qkv_bias[:, base + 2 * LANES : base + 3 * LANES] = jnp.concatenate(
            [values[:, part], gap], axis=1
        )
    film_bias[...] = emb_bias[...].reshape(1, 2 * WIDTH)
    rows = region[...].astype(F32)
    home = me_ref[1] * MAPS
    turned = jnp.concatenate([rows, jnp.zeros((LANES - rows.shape[0], PIXELS), F32)], axis=0).T
    lane = lax.broadcasted_iota(jnp.int32, (PIXELS, LANES), 1)
    for m in range(MAPS):
        region_row[m] = region[pl.ds(home + m, 1)]
        region_col[m] = jnp.sum(
            jnp.where(lane == home + m, turned, 0.0), axis=1, keepdims=True
        ).astype(jnp.int32)
    down = lax.broadcasted_iota(jnp.int32, (WIDTH, WIDTH), 0)
    along = lax.broadcasted_iota(jnp.int32, (WIDTH, WIDTH), 1)
    grouping[...] = (down // GROUP_SIZE == along // GROUP_SIZE).astype(F32)


def pack_kernel(conv_one, conv_two, emb, qkv, proj, first, second, third):
    first[0] = pack_conv(conv_one[...].astype(F32)).astype(BF16)
    second[0, 0:CONV_PACK] = pack_conv(conv_two[...].astype(F32)).astype(BF16)
    second[0, CONV_PACK:] = pack_emb(emb[...].astype(F32)).astype(BF16)
    third[0] = pack_proj(qkv[...].astype(F32), proj[...].astype(F32)).astype(BF16)


def place_of(group, head, me_ref):
    far_group = group ^ me_ref[0]
    far_head = head ^ me_ref[1]
    bits = [far_group // 4, (far_group // 2) & 1, far_head // 2, far_group & 1]
    if head % 2 == 1:
        bits[2:] = bits[:1:-1]
    place = 16 * (far_head & 1)
    for position, bit in enumerate(bits):
        place = place + (1 << position) * bit
    return place


def unpack_conv(blocks, me_ref, weight_ref):
    for head in range(HEADS):
        pieces = []
        for group in range(BLOCK_GROUPS):
            block = blocks[place_of(group, head, me_ref), 0:CONV_PACK].astype(F32)
            pieces += [block[HEAD_DIM * k : HEAD_DIM * (k + 1)] for k in range(3)]
            pieces.append(jnp.concatenate([block[288:, :48], block[288:, 48:96]], axis=0))
        weight_ref[HEAD_DIM * head : HEAD_DIM * (head + 1), :] = jnp.concatenate(
            pieces, axis=1
        ).astype(BF16)


def unpack_emb(blocks, me_ref, emb_ref):
    for group in range(BLOCK_GROUPS):
        embs = []
        for head in range(HEADS):
            emb = blocks[place_of(group, head, me_ref), CONV_PACK:].astype(F32)
            side = jnp.concatenate([emb[64:96, :64], emb[64:96, 64:]], axis=0)
            embs.append(jnp.concatenate([emb[:64], side], axis=1))
        emb_ref[64 * group : 64 * group + 64] = jnp.concatenate(embs, axis=1).astype(BF16)


def unpack_proj(blocks, me_ref, qkv_ref, proj_ref):
    gap = jnp.zeros((48, LANES - HEAD_DIM), F32)
    for group in range(BLOCK_GROUPS):
        rows = slice(48 * group, 48 * group + 48)
        for head in range(HEADS):
            block = blocks[place_of(group, head, me_ref)].astype(F32)
            wide = jnp.concatenate([block[48 * k : 48 * k + 48] for k in range(3)], axis=1)
            for part in range(3):
                piece = wide[:, HEAD_DIM * part : HEAD_DIM * (part + 1)]
                slot = (3 * head + part) * LANES
                qkv_ref[rows, slot : slot + LANES] = jnp.concatenate([piece, gap], axis=1).astype(
                    BF16
                )
            proj_ref[rows, LANES * head : LANES * (head + 1)] = jnp.concatenate(
                [wide[:, 3 * HEAD_DIM :], gap], axis=1
            ).astype(BF16)


def norm_stats(sums, squares, cells, grouping):
    totals = group_total(jnp.concatenate([sums, squares], axis=0), grouping)
    mean = totals[:MAPS] / cells
    inverse = lax.rsqrt(totals[MAPS:] / cells - mean * mean + EPS)
    return jnp.concatenate([mean, inverse], axis=0)


def norm_one_kernel(inputs, region, params, grouping, shifted, stats):
    sums, squares = [], []
    for m in range(MAPS):
        inputs.wait(m)
        values = inputs.ref[m].astype(F32)
        masked = values * valid_of(region, m)
        sums.append(column_sum(masked))
        squares.append(column_sum(masked * values))
    stats[...] = norm_stats(
        jnp.concatenate(sums, axis=0),
        jnp.concatenate(squares, axis=0),
        cells_of(region),
        grouping[...],
    )
    for m in range(MAPS):
        hat = (inputs.ref[m].astype(F32) - stats[m : m + 1]) * stats[MAPS + m : MAPS + m + 1]
        normed = hat * params[GAIN_ONE : GAIN_ONE + 1] + params[SHIFT_ONE : SHIFT_ONE + 1]
        store_shifted(shifted.ref, m, normed * sigmoid(normed) * valid_of(region, m))
        shifted.start(m)


def conv_one_kernel(
    me_ref, shifted, region, params, grouping, blocks, weight, result, stats, sums
):
    blocks.wait_all()
    unpack_conv(blocks.ref, me_ref, weight.ref)
    weight.start()

    def one_map(m, carry):
        shifted.wait(m)
        value = convolve(shifted.ref, m, weight.ref) + params[BIAS_ONE : BIAS_ONE + 1]
        result.ref[m] = value
        result.start(m)
        masked = value * valid_of(region, m)
        sums[pl.ds(m, 1)] = column_sum(masked)
        sums[pl.ds(MAPS + m, 1)] = column_sum(masked * value)
        return carry

    lax.fori_loop(0, MAPS, one_map, 0)
    stats[...] = norm_stats(sums[:MAPS], sums[MAPS:], cells_of(region), grouping[...])


def modulate(value, stats, film, params, m):
    hat = (value - stats[pl.ds(m, 1)]) * stats[pl.ds(MAPS + m, 1)]
    modulated = hat * params[GAIN_TWO : GAIN_TWO + 1] + params[SHIFT_TWO : SHIFT_TWO + 1]
    scale = 1.0 + film[pl.ds(m, 1), :WIDTH]
    return hat, modulated, scale, modulated * scale + film[pl.ds(m, 1), WIDTH:]


def conv_two_kernel(
    me_ref, conv_out, stats_two, inputs, embedding, emb_bias, region, params, grouping, blocks,
    weight, emb_weight, shifted, residual, attend_in, stats, film,
    sums,
):
    blocks.wait_all()
    unpack_conv(blocks.ref, me_ref, weight.ref)
    weight.start()
    unpack_emb(blocks.ref, me_ref, emb_weight.ref)
    emb_weight.start()
    embed = embedding[...].astype(F32)
    film[...] = dot((embed * sigmoid(embed)).astype(BF16), emb_weight.ref[...]) + emb_bias[...]

    def one_map(m, carry):
        _, _, _, normed = modulate(conv_out[m], stats_two, film, params, m)
        valid = valid_of(region, m)
        store_shifted(shifted, m, normed * sigmoid(normed) * valid)
        inputs.wait(m)
        value = (
            inputs.ref[m].astype(F32)
            + convolve(shifted, m, weight.ref)
            + params[BIAS_TWO : BIAS_TWO + 1]
        )
        residual[m] = value
        sums[pl.ds(m, 1)] = column_sum(value * valid)
        sums[pl.ds(MAPS + m, 1)] = column_sum(value * value * valid)
        return carry

    lax.fori_loop(0, MAPS, one_map, 0)
    stats[...] = norm_stats(sums[:MAPS], sums[MAPS:], cells_of(region), grouping[...])
    for m in range(MAPS):
        hat = (residual[m] - stats[m : m + 1]) * stats[MAPS + m : MAPS + m + 1]
        attend_in[m] = (
            hat * params[GAIN_THREE : GAIN_THREE + 1] + params[SHIFT_THREE : SHIFT_THREE + 1]
        ).astype(BF16)


def norm_back(grad, hat, along, cross, inverse, valid, cells):
    return inverse * (grad - valid * (along + cross * hat) / cells)


def attend_kernel(
    me_ref, attend_in, qkv_bias, region, region_row, cotangent, residual, stats, params, grouping,
    blocks,
    output, grad_residual, grad_conv, bias_sums, small_sums,
    qkv_weight, proj_weight, columns, grad_columns, attended, grad_attend, sums, terms,
):
    blocks.wait_all()
    unpack_proj(blocks.ref, me_ref, qkv_weight, proj_weight)

    def one_map(m, carry):
        rows = pl.ds(pl.multiple_of(m * PIXELS, PIXELS), PIXELS)
        cotangent.wait(m)
        columns[...] = (dot(attend_in[m], qkv_weight[...]) + qkv_bias[...]).astype(BF16)
        grad_attended = dot(cotangent.ref[m], proj_weight[...]).astype(BF16)
        key_region = region[m]
        query_region = region_row[m]
        allowed = (key_region > 0) & ((key_region == query_region) | (query_region == 0))
        for head in range(HEADS):
            base = 3 * LANES * head
            queries = columns[:, base : base + LANES]
            keys = columns[:, base + LANES : base + 2 * LANES]
            values = columns[:, base + 2 * LANES : base + 3 * LANES]
            grad_out = grad_attended[:, LANES * head : LANES * (head + 1)]
            logits = jnp.where(allowed, dot(keys, queries, (1, 1)) * FACTOR, -1e30)
            raised = jnp.exp(logits - jnp.max(logits, axis=0, keepdims=True))
            weights = raised * (1.0 / jnp.sum(raised, axis=0, keepdims=True))
            weights_low = weights.astype(BF16)
            attended[rows, LANES * head : LANES * (head + 1)] = dot(
                weights_low, values, (0, 0)
            ).astype(BF16)
            grad_weights = dot(values, grad_out, (1, 1))
            inner = jnp.sum(grad_weights * weights, axis=0, keepdims=True)
            grad_logits = (weights * (grad_weights - inner)).astype(BF16)
            grad_columns[rows, base : base + LANES] = (
                dot(grad_logits, keys, (0, 0)) * FACTOR
            ).astype(BF16)
            grad_columns[rows, base + LANES : base + 2 * LANES] = (
                dot(grad_logits, queries) * FACTOR
            ).astype(BF16)
            grad_columns[rows, base + 2 * LANES : base + 3 * LANES] = dot(
                weights_low, grad_out
            ).astype(BF16)
        output.ref[m] = (
            residual[m]
            + dot(attended[rows, :], proj_weight[...], (1, 1))
            + params[PROJ_BIAS : PROJ_BIAS + 1]
        ).astype(BF16)
        output.start(m)
        grad = dot(grad_columns[rows, :], qkv_weight[...], (1, 1))
        grad_attend[m] = grad
        hat = (residual[m] - stats[pl.ds(m, 1)]) * stats[pl.ds(MAPS + m, 1)]
        sums[pl.ds(m, 1)] = column_sum(grad)
        sums[pl.ds(MAPS + m, 1)] = column_sum(grad * hat)
        return carry

    lax.fori_loop(0, MAPS, one_map, 0)
    gain = params[GAIN_THREE : GAIN_THREE + 1]
    totals = group_total(sums[...] * gain, grouping[...])
    cells = cells_of(region)
    small_sums[...] = jnp.zeros_like(small_sums)
    small_sums[0:1] = column_sum(sums[MAPS:])
    small_sums[1:2] = column_sum(sums[:MAPS])
    top_sum = jnp.zeros((1, WIDTH), F32)
    low_sum = jnp.zeros((1, WIDTH), F32)
    for m in range(MAPS):
        inverse = stats[MAPS + m : MAPS + m + 1]
        hat = (residual[m] - stats[m : m + 1]) * inverse
        top = cotangent.ref[m].astype(F32)
        grad = top + norm_back(
            grad_attend[m] * gain,
            hat,
            totals[m : m + 1],
            totals[MAPS + m : MAPS + m + 1],
            inverse,
            valid_of(region, m),
            cells[m : m + 1],
        )
        grad_residual.ref[m] = grad
        grad_residual.start(m)
        low = grad.astype(BF16)
        grad_conv[m] = low
        top_sum = top_sum + column_sum(top)
        low_sum = low_sum + column_sum(low.astype(F32))
    small_sums[2:3] = top_sum
    small_sums[3:4] = low_sum
    bias_sums[...] = column_sum(grad_columns[...].astype(F32))
    grad_qkv, grad_proj = None, None
    for m in range(MAPS):
        rows = slice(m * PIXELS, (m + 1) * PIXELS)
        qkv_part = dot(attend_in[m], grad_columns[rows, :], (0, 0))
        proj_part = dot(cotangent.ref[m], attended[rows, :], (0, 0))
        grad_qkv = qkv_part if m == 0 else grad_qkv + qkv_part
        grad_proj = proj_part if m == 0 else grad_proj + proj_part
    for group in range(BLOCK_GROUPS):
        rows = slice(48 * group, 48 * group + 48)
        for head in range(HEADS):
            pieces = [
                grad_qkv[rows, slot * LANES : slot * LANES + HEAD_DIM]
                for slot in range(3 * head, 3 * head + 3)
            ]
            pieces.append(grad_proj[rows, head * LANES : head * LANES + HEAD_DIM])
            wide = jnp.concatenate(pieces, axis=1)
            terms[place_of(group, head, me_ref)] = jnp.concatenate(
                [wide[:, LANES * part : LANES * (part + 1)] for part in range(3)], axis=0
            ).astype(BF16)


def back_two_kernel(
    grad_conv, weight, conv_out, stats, film, embedding, emb_weight, region, params, grouping,
    grad_low, grad_film, grad_embed, small_sums,
    flipped, shifted, grad_normed, sums,
):
    weight.wait()
    flip_weight(flipped, weight.ref)

    def one_map(m, carry):
        conv_out.wait(m)
        store_shifted(shifted, m, grad_conv[m].astype(F32))
        hat, modulated, scale, normed = modulate(conv_out.ref[m], stats, film, params, m)
        logistic = sigmoid(normed)
        slope = logistic * (1.0 + normed * (1.0 - logistic)) * valid_of(region, m)
        grad = convolve_back(shifted, m, flipped) * slope
        grad_film[pl.ds(m, 1), :WIDTH] = column_sum(grad * modulated)
        grad_film[pl.ds(m, 1), WIDTH:] = column_sum(grad)
        scaled = grad * scale
        grad_normed[m] = scaled
        sums[pl.ds(m, 1)] = column_sum(scaled)
        sums[pl.ds(MAPS + m, 1)] = column_sum(scaled * hat)
        return carry

    lax.fori_loop(0, MAPS, one_map, 0)
    gain = params[GAIN_TWO : GAIN_TWO + 1]
    totals = group_total(sums[...] * gain, grouping[...])
    cells = cells_of(region)
    small_sums[...] = jnp.zeros_like(small_sums)
    small_sums[0:1] = column_sum(sums[MAPS:])
    small_sums[1:2] = column_sum(sums[:MAPS])
    low_sum = jnp.zeros((1, WIDTH), F32)
    for m in range(MAPS):
        inverse = stats[MAPS + m : MAPS + m + 1]
        low = norm_back(
            grad_normed[m] * gain,
            (conv_out.ref[m] - stats[m : m + 1]) * inverse,
            totals[m : m + 1],
            totals[MAPS + m : MAPS + m + 1],
            inverse,
            valid_of(region, m),
            cells[m : m + 1],
        ).astype(BF16)
        grad_low[m] = low
        low_sum = low_sum + column_sum(low.astype(F32))
    small_sums[2:3] = low_sum
    embed = embedding[...].astype(F32)
    logistic = sigmoid(embed)
    film_high = grad_film[...].astype(BF16)
    film_rest = (grad_film[...] - film_high.astype(F32)).astype(BF16)
    emb_weight.wait()
    grad_embed[...] = (
        dot(film_high, emb_weight.ref[...], (1, 1)) + dot(film_rest, emb_weight.ref[...], (1, 1))
    ) * (logistic * (1.0 + embed * (1.0 - logistic)))


def back_one_kernel(
    grad_conv, weight, inputs, stats, grad_residual, region, params, grouping,
    grad_inputs, small_sums,
    flipped, shifted, grad_normed, sums,
):
    weight.wait()
    flip_weight(flipped, weight.ref)
    gain = params[GAIN_ONE : GAIN_ONE + 1]

    def one_map(m, carry):
        inputs.wait(m)
        store_shifted(shifted, m, grad_conv[m].astype(F32))
        hat = (inputs.ref[m].astype(F32) - stats[pl.ds(m, 1)]) * stats[pl.ds(MAPS + m, 1)]
        normed = hat * gain + params[SHIFT_ONE : SHIFT_ONE + 1]
        logistic = sigmoid(normed)
        slope = logistic * (1.0 + normed * (1.0 - logistic)) * valid_of(region, m)
        grad = convolve_back(shifted, m, flipped) * slope
        grad_normed[m] = grad
        sums[pl.ds(m, 1)] = column_sum(grad)
        sums[pl.ds(MAPS + m, 1)] = column_sum(grad * hat)
        return carry

    lax.fori_loop(0, MAPS, one_map, 0)
    totals = group_total(sums[...] * gain, grouping[...])
    cells = cells_of(region)
    small_sums[...] = jnp.zeros_like(small_sums)
    small_sums[0:1] = column_sum(sums[MAPS:])
    small_sums[1:2] = column_sum(sums[:MAPS])
    for m in range(MAPS):
        inverse = stats[MAPS + m : MAPS + m + 1]
        grad_residual.wait(m)
        grad_inputs.ref[m] = (
            grad_residual.ref[m]
            + norm_back(
                grad_normed[m] * gain,
                (inputs.ref[m].astype(F32) - stats[m : m + 1]) * inverse,
                totals[m : m + 1],
                totals[MAPS + m : MAPS + m + 1],
                inverse,
                valid_of(region, m),
                cells[m : m + 1],
            )
        ).astype(BF16)
        grad_inputs.start(m)


def conv_weight_grads(shifted, grad_conv, turned, total):
    for m in range(MAPS):
        turned[:, m * PIXELS : (m + 1) * PIXELS] = grad_conv[m].astype(F32).T.astype(BF16)

    def one_row(tap_row, carry):
        rows = pl.ds(pl.multiple_of(tap_row * SIDE, SIDE), PIXELS)
        part = dot(turned[:, 0:PIXELS], shifted[0, rows, :])
        for m in range(1, MAPS):
            part += dot(turned[:, m * PIXELS : (m + 1) * PIXELS], shifted[m, rows, :])
        total[tap_row] = part
        return carry

    lax.fori_loop(0, 3, one_row, 0)


def pack_conv_grads(total, me_ref, blocks):
    for group in range(BLOCK_GROUPS):
        start, stop = group * CONV_ROWS, (group + 1) * CONV_ROWS
        pieces = []
        for tap_row in range(3):
            low, high = tap_row * 3 * WIDTH, (tap_row + 1) * 3 * WIDTH
            if max(low, start) < min(high, stop):
                pieces.append((tap_row, max(low, start) - low, min(high, stop) - low))
        for head in range(HEADS):
            rows = slice(HEAD_DIM * head, HEAD_DIM * (head + 1))
            values = [total[tap_row, rows, a:b] for tap_row, a, b in pieces]
            block = values[0] if len(values) == 1 else jnp.concatenate(values, axis=1)
            place = place_of(group, head, me_ref)
            blocks[place, 0:CONV_PACK, :] = pack_conv(block).astype(BF16)


def grads_one_kernel(me_ref, grad_conv, shifted, turned, total, blocks):
    shifted.wait_all()
    conv_weight_grads(shifted.ref, grad_conv, turned, total)
    pack_conv_grads(total, me_ref, blocks)


def grads_two_kernel(me_ref, grad_conv, shifted, proj_terms, turned, total, blocks):
    conv_weight_grads(shifted, grad_conv, turned, total)
    pack_conv_grads(total, me_ref, blocks)
    proj_terms.wait_all()
    blocks[:, CONV_PACK:, :] = proj_terms.ref[...]


def unpack_conv_grad(block, result):
    for part in range(3):
        result[:, LANES * part : LANES * (part + 1)] = block[HEAD_DIM * part : HEAD_DIM * (part + 1)]
    result[:, 3 * LANES :] = jnp.concatenate([block[288:336, :48], block[288:336, 48:96]], axis=0)


def split_sums(part):
    return part[:MAPS].astype(F32) + part[MAPS : 2 * MAPS].astype(F32)


def finish_one_kernel(me_ref, mine, other, first, second, third, fourth, result, sums, emb):
    unpack_conv_grad(mine[0].astype(F32) + other[0].astype(F32), result)
    parts = [part[...] for part in (first, second, third, fourth)]
    sums[...] = sum(split_sums(part) for part in parts)
    total = None
    for part in parts:
        rows = part[2 * MAPS :]
        term = dot(rows[:, :EMBED], rows[:, EMBED:], (0, 0))
        total = term if total is None else total + term
    emb[...] = total


def finish_two_kernel(mine, other, result, qkv, proj):
    block = mine[0].astype(F32) + other[0].astype(F32)
    unpack_conv_grad(block, result)
    tiles = [block[CONV_PACK + 48 * k : CONV_PACK + 48 * k + 48] for k in range(3)]
    wide = jnp.concatenate(tiles, axis=1)
    qkv[...] = wide[:, : 3 * HEAD_DIM]
    proj[...] = wide[:, 3 * HEAD_DIM :]


def join_kernel(left, right, joined):
    count = left.shape[0]
    joined[:count] = left[...]
    joined[count:] = right[...]


def add_kernel(left, right, total):
    total[...] = (left[...].astype(F32) + right[...].astype(F32)).astype(BF16)


def add_split_kernel(left, right, send, keep):
    half = keep.shape[0]
    send[...] = (left[half:].astype(F32) + right[half:].astype(F32)).astype(BF16)
    keep[...] = (left[:half].astype(F32) + right[:half].astype(F32)).astype(BF16)


def swap(values, masks, sizes):
    pairs = [(own, own ^ masks[own % 2]) for own in range(sizes[0] * sizes[1])]
    return lax.ppermute(values, AXES, pairs)


def stages_of(sizes):
    inner = sizes[0] // BLOCK_GROUPS
    group_bit = sizes[1] * inner
    over_x, over_y = 2, group_bit
    return ((4 * group_bit,) * 2, (2 * group_bit,) * 2, (over_x, over_y), (over_y, over_x))


def join(left, right):
    joined = shape_of((left.shape[0] + right.shape[0],) + left.shape[1:], left.dtype)
    return run_kernel(join_kernel, "join", (left, right), (joined,), room=8)[0]


def add_parts(left, right):
    total = shape_of(left.shape, BF16)
    return run_kernel(add_kernel, "add", (left, right), (total,), room=8)[0]


def add_split(left, right):
    half = shape_of((left.shape[0] // 2,) + left.shape[1:], BF16)
    return run_kernel(add_split_kernel, "add_split", (left, right), (half, half), room=8)


def inner_groups(sizes):
    inner = sizes[0] // BLOCK_GROUPS
    return [[group * inner + k for k in range(inner)] for group in range(BLOCK_GROUPS)]


def inner_gather(shard, sizes):
    if sizes[0] == BLOCK_GROUPS:
        return shard
    return lax.all_gather(shard, "dp", axis=0, tiled=True, axis_index_groups=inner_groups(sizes))


def inner_scatter(grad, sizes):
    if sizes[0] == BLOCK_GROUPS:
        return grad
    return lax.psum_scatter(
        grad, "dp", scatter_dimension=0, tiled=True, axis_index_groups=inner_groups(sizes)
    )


def per_device(
    inputs, embedding, region, cotangent, conv_one, bias_one, conv_two, bias_two, emb_weight,
    emb_bias, qkv_weight, q_bias, v_bias, proj_weight, proj_bias, gain_one, shift_one, gain_two,
    shift_two, gain_three, shift_three,
):
    sizes = (lax.axis_size("dp"), lax.axis_size("head"))
    inner = sizes[0] // BLOCK_GROUPS
    dp_id, head_id = lax.axis_index("dp"), lax.axis_index("head")
    me = jnp.stack([dp_id // inner, head_id]).astype(jnp.int32)
    kernel = functools.partial
    map_shape = (MAPS, PIXELS, WIDTH)
    shifted_shape = (MAPS, PADDED, 3 * WIDTH)

    shards = [inner_gather(w, sizes) for w in (conv_one, conv_two, emb_weight, qkv_weight, proj_weight)]

    first, second, third, fourth = stages_of(sizes)
    core = (1, 1)

    def send(values, masks):
        return swap(values, masks, sizes)

    stats_shape = shape_of((2 * MAPS, WIDTH), F32)
    small_shape = shape_of((8, WIDTH), F32)
    sums_scratch = pltpu.VMEM((2 * MAPS, WIDTH), F32)
    pack_one, pack_two, pack_three = run_kernel(
        pack_kernel,
        "pack",
        (shards[0].T, shards[1].T, *shards[2:]),
        (
            shape_of((1, CONV_PACK, LANES), BF16),
            shape_of((1, SECOND_ROWS, LANES), BF16),
            shape_of((1, PROJ_PACK, LANES), BF16),
        ),
        room=62,
    )
    one = send(pack_one, first)
    two = send(pack_two, first)
    three = send(pack_three, first)
    params, qkv_bias, film_bias, region_col, region_row, grouping = run_kernel(
        prepare_kernel,
        "prepare",
        (
            me, after(region, pack_one), bias_one, bias_two, gain_one, shift_one, gain_two, shift_two,
            gain_three, shift_three, proj_bias, q_bias, v_bias, emb_bias,
        ),
        (
            shape_of((16, WIDTH), F32),
            shape_of((1, SLOTS), F32),
            shape_of((1, 2 * WIDTH), F32),
            shape_of((MAPS, PIXELS, 1), jnp.int32),
            shape_of((MAPS, 1, PIXELS), jnp.int32),
            shape_of((WIDTH, WIDTH), F32),
        ),
        room=62,
    )
    held_one = join(pack_one, one)
    one = send(held_one, second)
    held_two = join(pack_two, after(two, held_one))
    two = send(held_two, second)
    held_one = join(held_one, after(one, held_two, params))
    one = send(held_one, third)
    held_three = join(pack_three, after(three, held_one))
    three = send(held_three, second)
    held_one = join(held_one, after(one, held_three))
    far_one = send(held_one, fourth)
    near_core_one = send(held_one, core)
    held_two = join(held_two, after(two, held_one))
    two = send(held_two, third)
    shifted_one, stats_one = run_kernel(
        norm_one_kernel,
        "norm_one",
        (after(inputs, held_two), region_col, params, grouping),
        (shape_of(shifted_shape, BF16), stats_shape),
        fetch=(0,),
        flush=(0,),
    )
    held_two = join(held_two, after(two, stats_one))
    far_two = send(held_two, fourth)
    near_core_two = send(held_two, core)
    far_one = after(far_one, held_two)
    far_core_one = send(far_one, core)
    held_three = join(held_three, after(three, held_two))
    three = send(held_three, third)
    weight_shape = shape_of((WIDTH, TAPS), BF16)
    weight_one, conv_out, stats_two, conv_kept = run_kernel(
        conv_one_kernel,
        "conv_one",
        (
            me, after(shifted_one, held_three), region_col, params, grouping,
            held_one, far_one, near_core_one, far_core_one,
        ),
        (weight_shape, shape_of(map_shape, F32), stats_shape),
        (sums_scratch,),
        fetch=(1,),
        flush=(0,),
        double=(1,),
        blocks=(32, CONV_PACK, LANES),
    )
    held_three = join(held_three, after(three, conv_out))
    far_three = send(held_three, fourth)
    near_core_three = send(held_three, core)
    far_two = after(far_two, conv_out)
    far_core_two = send(far_two, core)
    weight_two, film_weight, shifted_two, residual, attend_in, stats_three, film = run_kernel(
        conv_two_kernel,
        "conv_two",
        (
            me, conv_out, stats_two, inputs, embedding, film_bias, region_col, params, grouping,
            held_two, far_two, near_core_two, far_core_two,
        ),
        (
            weight_shape,
            shape_of((EMBED, 2 * WIDTH), BF16),
            shape_of(shifted_shape, BF16),
            shape_of(map_shape, F32),
            shape_of(map_shape, BF16),
            stats_shape,
            shape_of((MAPS, 2 * WIDTH), F32),
        ),
        (sums_scratch,),
        fetch=(3,),
        flush=(0, 1),
        blocks=(32, SECOND_ROWS, LANES),
    )
    far_three = after(far_three, attend_in)
    far_core_three = send(far_three, core)
    proj_shape = shape_of((8, PROJ_PACK, LANES), BF16)
    output, grad_residual, grad_conv_two, column_sums, small_three, *proj_terms = run_kernel(
        attend_kernel,
        "attend",
        (
            me, attend_in, qkv_bias, region_col, region_row, cotangent, residual, stats_three, params,
            grouping, held_three, far_three, near_core_three, far_core_three,
        ),
        (
            shape_of(map_shape, BF16),
            shape_of(map_shape, F32),
            shape_of(map_shape, BF16),
            shape_of((1, SLOTS), F32),
            small_shape,
        )
        + (proj_shape,) * 4,
        (
            pltpu.VMEM((WIDTH, SLOTS), BF16),
            pltpu.VMEM((WIDTH, HEADS * LANES), BF16),
            pltpu.VMEM((PIXELS, SLOTS), BF16),
            pltpu.VMEM((MAPS * PIXELS, SLOTS), BF16),
            pltpu.VMEM((MAPS * PIXELS, HEADS * LANES), BF16),
            pltpu.VMEM(map_shape, F32),
            sums_scratch,
            pltpu.VMEM((32, PROJ_PACK, LANES), BF16),
        ),
        fetch=(5,),
        flush=(0, 1),
        blocks=(32, PROJ_PACK, LANES),
        terms=True,
    )
    grads_scratch = (
        pltpu.VMEM((WIDTH, MAPS * PIXELS), BF16),
        pltpu.VMEM((3, WIDTH, 3 * WIDTH), F32),
    )
    grads_rows = CONV_PACK + PROJ_PACK
    terms_two = run_kernel(
        grads_two_kernel,
        "weight_grads_two",
        (me, grad_conv_two, shifted_two, *proj_terms),
        (shape_of((8, grads_rows, LANES), BF16),) * 4,
        grads_scratch + (pltpu.VMEM((32, grads_rows, LANES), BF16),),
        blocks=(32, PROJ_PACK, LANES),
        terms=True,
    )
    back_scratch = (
        pltpu.VMEM((3, 3 * WIDTH, WIDTH), BF16),
        pltpu.VMEM(shifted_shape, BF16),
        pltpu.VMEM(map_shape, F32),
        sums_scratch,
    )
    near_two, far_two, near_core_two, far_core_two = terms_two
    far_came, near_came = send(far_core_two, core), send(near_core_two, core)
    grad_conv_one, grad_film, grad_embedding, small_two = run_kernel(
        back_two_kernel,
        "back_two",
        (
            after(grad_conv_two, near_two), weight_two, conv_kept, stats_two, film, embedding,
            film_weight, region_col, params, grouping,
        ),
        (
            shape_of(map_shape, BF16),
            shape_of((MAPS, 2 * WIDTH), F32),
            shape_of((MAPS, EMBED), F32),
            small_shape,
        ),
        back_scratch,
        fetch=(1, 2, 6),
    )
    far_two = add_parts(far_two, after(far_came, grad_film))
    two = send(far_two, fourth)
    near_two = add_parts(near_two, after(near_came, far_two))
    terms_one = run_kernel(
        grads_one_kernel,
        "weight_grads_one",
        (me, after(grad_conv_one, near_two), shifted_one),
        (shape_of((8, CONV_PACK, LANES), BF16),) * 4,
        grads_scratch + (pltpu.VMEM((32, CONV_PACK, LANES), BF16),),
        fetch=(2,),
        terms=True,
    )
    near_one, far_one, near_core_one, far_core_one = terms_one
    far_came, near_came = send(far_core_one, core), send(near_core_one, core)
    far_two, near_two = add_split(near_two, after(two, near_one))
    two = send(far_two, third)
    far_one = add_parts(far_one, after(far_came, far_two))
    one = send(far_one, fourth)
    near_one = add_parts(near_one, after(near_came, far_one))
    grad_inputs, small_one = run_kernel(
        back_one_kernel,
        "back_one",
        (
            after(grad_conv_one, near_one), weight_one, inputs, stats_one, grad_residual, region_col,
            params, grouping,
        ),
        (shape_of(map_shape, BF16), small_shape),
        back_scratch,
        fetch=(1, 2, 4),
        flush=(0,),
    )
    far_one, near_one = add_split(near_one, after(one, small_one))
    one = send(far_one, third)
    far_two, near_two = add_split(near_two, after(two, far_one))
    two = send(far_two, second)
    embed = embedding.astype(F32)
    embed_low = jax.nn.silu(embed).astype(BF16)
    film_sums = jnp.sum(grad_film, axis=0).reshape(2, WIDTH)
    slots = column_sums.reshape(HEADS, 3, LANES)[:, :, :HEAD_DIM]
    sums = jnp.concatenate(
        [
            small_one[:2],
            small_two[:3],
            small_three[:4],
            film_sums,
            slots[:, 0].reshape(1, WIDTH),
            slots[:, 2].reshape(1, WIDTH),
        ]
    )
    sums = jnp.pad(sums.reshape(-1), (0, 128)).reshape(MAPS, 1280)
    rows = jnp.concatenate([embed_low, grad_film.astype(BF16)], axis=1)

    def message(sums, rows):
        high = sums.astype(BF16)
        return jnp.concatenate([high, (sums - high.astype(F32)).astype(BF16), rows], axis=0)

    def mix(parts):
        sums = sum(part[:4].astype(F32) + part[4:8].astype(F32) for part in parts)
        return sums, jnp.concatenate([part[8:] for part in parts], axis=0)

    def both(left, right):
        return tuple(a ^ b for a, b in zip(left, right))

    rows = message(sums, after(rows, far_two))
    came = [rows, send(rows, core)]
    far_two, near_two = add_split(near_two, after(two, rows))
    two = send(far_two, first)
    rows = message(*mix([after(part, far_two) for part in came]))
    came = [rows] + [send(rows, masks) for masks in (first, second, both(first, second))]
    far_one, near_one = add_split(near_one, after(one, rows))
    one = send(far_one, second)
    rows = message(*mix([after(part, far_one) for part in came]))
    came = [rows] + [send(rows, masks) for masks in (third, fourth, both(third, fourth))]
    conv_grad_shape = shape_of((HEAD_DIM, CONV_ROWS), F32)
    grad_weight_two, grad_qkv_weight, grad_proj_weight = run_kernel(
        finish_two_kernel,
        "finish_two",
        (near_two, after(two, rows)),
        (conv_grad_shape, shape_of((48, 3 * HEAD_DIM), F32), shape_of((48, HEAD_DIM), F32)),
        room=8,
    )
    far_one, near_one = add_split(near_one, after(one, grad_weight_two))
    one = send(far_one, first)
    grad_weight_one, sums, emb_products = run_kernel(
        finish_one_kernel,
        "finish_one",
        (me, near_one, one, *came),
        (conv_grad_shape, shape_of((MAPS, 1280), F32), shape_of((EMBED, 2 * WIDTH), F32)),
        room=8,
    )
    sums = sums.reshape(-1)[: 13 * WIDTH].reshape(13, WIDTH)
    rows, cols = emb_weight.shape
    grad_emb_weight = lax.dynamic_slice(emb_products, (dp_id * rows, head_id * cols), (rows, cols))
    finals = [
        inner_scatter(grad, sizes)
        for grad in (grad_weight_one.T, grad_weight_two.T, grad_qkv_weight, grad_proj_weight)
    ]
    return (
        output,
        grad_inputs,
        grad_embedding,
        finals[0],
        finals[1],
        grad_emb_weight,
        finals[2],
        finals[3],
        sums[4],
        sums[8],
        sums[9:11].reshape(2 * WIDTH),
        sums[11],
        sums[12],
        sums[7],
        sums[0],
        sums[1],
        sums[2],
        sums[3],
        sums[5],
        sums[6],
    )


def solution(mesh):
    own = P(AXES)
    split = P("dp", "head")
    whole = P()
    in_specs = (own, own, P("dp"), own, split, whole, split, whole, split, whole, split) + (
        (whole, whole, split) + (whole,) * 7
    )
    out_specs = (own,) * 3 + (split,) * 5 + (whole,) * 12
    return jax.shard_map(
        per_device, mesh=mesh, in_specs=in_specs, out_specs=out_specs, check_vma=False
    )
```

```python
import functools

import jax
import jax.numpy as jnp
from jax import lax
from jax.experimental import pallas as pl
from jax.experimental.pallas import tpu as pltpu
from jax.sharding import PartitionSpec as P

WIDTH = 384
EMBED = 512
HEADS = 4
HEAD_DIM = 96
GROUP_SIZE = 12
SIDE = 16
PIXELS = 256
MAPS = 4
LANES = 128
TAPS = 9 * WIDTH
PADDED = PIXELS + 2 * SIDE
SLOTS = 3 * HEADS * LANES
FACTOR = HEAD_DIM ** (-0.5)
EPS = 1e-05
AXES = ("dp", "head")

BLOCK_GROUPS = 8
CONV_ROWS = TAPS // BLOCK_GROUPS
CONV_PACK = 336
EMB_PACK = 96
SUM_ROWS = 16
PROJ_PACK = 144
SECOND_ROWS = CONV_PACK + EMB_PACK
ROOM = 28
FLOPS_PER_US = 1.15e9
DURATIONS = {
    "norm_one": 2.4,
    "conv_one": 7,
    "conv_two": 9,
    "attend": 16,
    "back_three": 2.5,
    "weight_grads_two": 7,
    "back_two": 8,
    "weight_grads_one": 7,
    "back_one": 8,
    "back_film": 1.1,
}

F32 = jnp.float32
BF16 = jnp.bfloat16
BIAS_ONE, BIAS_TWO, GAIN_ONE, SHIFT_ONE, GAIN_TWO, SHIFT_TWO, GAIN_THREE, SHIFT_THREE, PROJ_BIAS = (
    range(9)
)

VMEM = pl.BlockSpec(memory_space=pltpu.VMEM)
SMEM = pl.BlockSpec(memory_space=pltpu.SMEM)


def after(value, *others):
    return lax.optimization_barrier((value, *others))[0]


class Parts:
    def __init__(self, parts, ref):
        self.parts, self.ref = parts, ref

    def collect(self):
        first = self.ref.shape[1] - self.parts[0].shape[1]
        for index, part in enumerate(self.parts):
            self.ref[8 * index : 8 * index + 8, first:] = part[...]


def run_kernel(kernel, name, operands, outs, scratch=(), room=ROOM, blocks=None, terms=0):
    operands = tuple(operands)
    plain = len(operands) - (blocks[0] // 8 if blocks else 0)
    direct = len(outs) - terms
    in_specs = [SMEM if value.dtype == jnp.int32 and value.ndim == 1 else VMEM for value in operands]
    scratch = list(scratch)
    own = len(scratch)
    if blocks:
        scratch.append(pltpu.VMEM(blocks, BF16))

    def body(*refs):
        ins = refs[: len(operands)]
        results = refs[len(operands) : len(operands) + len(outs)]
        given = refs[len(operands) + len(outs) :]
        held = [Parts(ins[plain:], given[own])] if blocks else []
        kernel(*ins[:plain], *held, *results[:direct], *given[:own])
        for k in range(terms):
            results[direct + k][...] = given[own - 1][8 * k : 8 * k + 8]

    return pl.pallas_call(
        body,
        out_shape=list(outs),
        in_specs=in_specs,
        out_specs=[VMEM] * len(outs),
        scratch_shapes=scratch,
        compiler_params=pltpu.CompilerParams(vmem_limit_bytes=room * 2**20),
        cost_estimate=pl.CostEstimate(
            flops=int(FLOPS_PER_US * DURATIONS.get(name, 0.5)), bytes_accessed=0, transcendentals=0
        ),
        name=name,
    )(*operands)


def shape_of(shape, dtype):
    return jax.ShapeDtypeStruct(shape, dtype)


def dot(left, right, dims=(1, 0)):
    return lax.dot_general(
        left, right, (((dims[0],), (dims[1],)), ((), ())), preferred_element_type=F32
    )


def group_total(rows, grouping):
    return lax.dot_general(
        rows,
        grouping,
        (((1,), (0,)), ((), ())),
        preferred_element_type=F32,
        precision=lax.Precision.HIGHEST,
    )


def sigmoid(values):
    return 1.0 / (1.0 + jnp.exp(-values))


def valid_of(region_ref, index):
    return (region_ref[index] > 0).astype(F32)


def cells_of(region_ref):
    counts = [jnp.sum(valid_of(region_ref, m), axis=0, keepdims=True) for m in range(MAPS)]
    return jnp.concatenate(counts, axis=0) * float(GROUP_SIZE)


def column_sum(values):
    return jnp.sum(values, axis=0, keepdims=True)


def store_shifted(target_ref, index, values):
    column = lax.broadcasted_iota(jnp.int32, (PIXELS, 1), 0) % SIDE
    left = jnp.where(column == 0, 0.0, pltpu.roll(values, 1, 0))
    right = jnp.where(column == SIDE - 1, 0.0, pltpu.roll(values, PIXELS - 1, 0))
    border = jnp.zeros((SIDE, 3 * WIDTH), BF16)
    target_ref[index, 0:SIDE, :] = border
    target_ref[index, SIDE + PIXELS : PADDED, :] = border
    for position, part in enumerate((left, values, right)):
        target_ref[index, SIDE : SIDE + PIXELS, position * WIDTH : (position + 1) * WIDTH] = (
            part.astype(BF16)
        )


def convolve(shifted_ref, index, weight_ref):
    total = None
    for tap_row in range(3):
        part = dot(
            shifted_ref[index, tap_row * SIDE : tap_row * SIDE + PIXELS, :],
            weight_ref[:, tap_row * 3 * WIDTH : (tap_row + 1) * 3 * WIDTH],
            (1, 1),
        )
        total = part if total is None else total + part
    return total


def flip_weight(flipped_ref, weight_ref):
    for tap_row in range(3):
        for tap_col in range(3):
            start = (3 * (2 - tap_row) + 2 - tap_col) * WIDTH
            flipped_ref[tap_row, tap_col * WIDTH : (tap_col + 1) * WIDTH, :] = weight_ref[
                :, start : start + WIDTH
            ]


def convolve_back(shifted_ref, index, flipped_ref):
    total = None
    for tap_row in range(3):
        part = dot(
            shifted_ref[index, tap_row * SIDE : tap_row * SIDE + PIXELS, :],
            flipped_ref[tap_row],
        )
        total = part if total is None else total + part
    return total


def pack_conv(shard):
    tail = shard[:, 3 * LANES :]
    parts = [shard[:, LANES * k : LANES * (k + 1)] for k in range(3)]
    parts.append(jnp.concatenate([tail[:48], tail[48:], jnp.zeros((48, 32), shard.dtype)], axis=1))
    return jnp.concatenate(parts, axis=0)


def pack_proj(qkv, proj):
    wide = jnp.concatenate([qkv, proj], axis=1)
    return jnp.concatenate([wide[:, LANES * k : LANES * (k + 1)] for k in range(3)], axis=0)


def pack_emb(shard):
    side = shard[:, LANES:]
    half = side.shape[0] // 2
    return jnp.concatenate(
        [shard[:, :LANES], jnp.concatenate([side[:half], side[half:]], axis=1)], axis=0
    )


def prepare_kernel(
    me_ref, region, bias_one, bias_two, gain_one, shift_one, gain_two, shift_two, gain_three,
    shift_three, proj_bias, q_bias, v_bias, emb_bias,
    params, qkv_bias, film_bias, region_col, region_row, grouping,
):
    vectors = (
        bias_one, bias_two, gain_one, shift_one, gain_two, shift_two, gain_three, shift_three,
        proj_bias,
    )
    for row, vector in enumerate(vectors):
        params[row : row + 1, :] = vector[...].reshape(1, WIDTH)
    queries, values = q_bias[...].reshape(1, WIDTH), v_bias[...].reshape(1, WIDTH)
    gap = jnp.zeros((1, LANES - HEAD_DIM), F32)
    for head in range(HEADS):
        part = slice(HEAD_DIM * head, HEAD_DIM * (head + 1))
        base = 3 * LANES * head
        qkv_bias[:, base : base + LANES] = jnp.concatenate([queries[:, part], gap], axis=1)
        qkv_bias[:, base + LANES : base + 2 * LANES] = jnp.zeros((1, LANES), F32)
        qkv_bias[:, base + 2 * LANES : base + 3 * LANES] = jnp.concatenate(
            [values[:, part], gap], axis=1
        )
    film_bias[...] = emb_bias[...].reshape(1, 2 * WIDTH)
    rows = region[...].astype(F32)
    home = me_ref[1] * MAPS
    turned = jnp.concatenate([rows, jnp.zeros((LANES - rows.shape[0], PIXELS), F32)], axis=0).T
    lane = lax.broadcasted_iota(jnp.int32, (PIXELS, LANES), 1)
    for m in range(MAPS):
        region_row[m] = region[pl.ds(home + m, 1)]
        region_col[m] = jnp.sum(
            jnp.where(lane == home + m, turned, 0.0), axis=1, keepdims=True
        ).astype(jnp.int32)
    down = lax.broadcasted_iota(jnp.int32, (WIDTH, WIDTH), 0)
    along = lax.broadcasted_iota(jnp.int32, (WIDTH, WIDTH), 1)
    grouping[...] = (down // GROUP_SIZE == along // GROUP_SIZE).astype(F32)


def pack_kernel(conv_one, conv_two, emb, qkv, proj, first, second, third):
    first[0] = pack_conv(conv_one[...].astype(F32)).astype(BF16)
    second[0, 0:CONV_PACK] = pack_conv(conv_two[...].astype(F32)).astype(BF16)
    second[0, CONV_PACK:] = pack_emb(emb[...].astype(F32)).astype(BF16)
    third[0] = pack_proj(qkv[...].astype(F32), proj[...].astype(F32)).astype(BF16)


def place_of(group, head, me_ref):
    far_group = group ^ me_ref[0]
    far_head = head ^ me_ref[1]
    bits = [far_group // 4, (far_group // 2) & 1, far_head // 2, far_group & 1]
    if head % 2 == 1:
        bits[2:] = bits[:1:-1]
    place = 16 * (far_head & 1)
    for position, bit in enumerate(bits):
        place = place + (1 << position) * bit
    return place


def place_of_own(group, over_x, me_ref):
    far_group = group ^ me_ref[0]
    far_x = over_x ^ (me_ref[1] // 2)
    far_y = far_group & 1
    odd = (me_ref[1] & 1) == 1
    place = far_group // 4 + 2 * ((far_group // 2) & 1)
    return place + jnp.where(odd, 4 * far_y + 8 * far_x, 4 * far_x + 8 * far_y)


def turn_halves(values, index, me_ref, kept, sent):
    odd = (me_ref[1] & 1) == 1
    turned = values.T
    place = pl.ds(index * PIXELS, PIXELS)
    for over_x in range(2):
        low = turned[2 * HEAD_DIM * over_x : 2 * HEAD_DIM * over_x + HEAD_DIM]
        high = turned[2 * HEAD_DIM * over_x + HEAD_DIM : 2 * HEAD_DIM * (over_x + 1)]
        rows = slice(HEAD_DIM * over_x, HEAD_DIM * (over_x + 1))
        kept[rows, place] = jnp.where(odd, high, low).astype(BF16)
        sent[rows, place] = jnp.where(odd, low, high).astype(BF16)


def unpack_conv(blocks, me_ref, weight_ref):
    for head in range(HEADS):
        pieces = []
        for group in range(BLOCK_GROUPS):
            block = blocks[place_of(group, head, me_ref), 0:CONV_PACK].astype(F32)
            pieces += [block[HEAD_DIM * k : HEAD_DIM * (k + 1)] for k in range(3)]
            pieces.append(jnp.concatenate([block[288:, :48], block[288:, 48:96]], axis=0))
        weight_ref[HEAD_DIM * head : HEAD_DIM * (head + 1), :] = jnp.concatenate(
            pieces, axis=1
        ).astype(BF16)


def unpack_emb(blocks, me_ref, emb_ref):
    for group in range(BLOCK_GROUPS):
        embs = []
        for head in range(HEADS):
            emb = blocks[place_of(group, head, me_ref), CONV_PACK:].astype(F32)
            side = jnp.concatenate([emb[64:96, :64], emb[64:96, 64:]], axis=0)
            embs.append(jnp.concatenate([emb[:64], side], axis=1))
        emb_ref[64 * group : 64 * group + 64] = jnp.concatenate(embs, axis=1).astype(BF16)


def unpack_proj(blocks, me_ref, qkv_ref, proj_ref):
    gap = jnp.zeros((48, LANES - HEAD_DIM), F32)
    for group in range(BLOCK_GROUPS):
        rows = slice(48 * group, 48 * group + 48)
        for head in range(HEADS):
            block = blocks[place_of(group, head, me_ref)].astype(F32)
            wide = jnp.concatenate([block[48 * k : 48 * k + 48] for k in range(3)], axis=1)
            for part in range(3):
                piece = wide[:, HEAD_DIM * part : HEAD_DIM * (part + 1)]
                slot = (3 * head + part) * LANES
                qkv_ref[rows, slot : slot + LANES] = jnp.concatenate([piece, gap], axis=1).astype(
                    BF16
                )
            proj_ref[rows, LANES * head : LANES * (head + 1)] = jnp.concatenate(
                [wide[:, 3 * HEAD_DIM :], gap], axis=1
            ).astype(BF16)


def norm_stats(sums, squares, cells, grouping):
    totals = group_total(jnp.concatenate([sums, squares], axis=0), grouping)
    mean = totals[:MAPS] / cells
    inverse = lax.rsqrt(totals[MAPS:] / cells - mean * mean + EPS)
    return jnp.concatenate([mean, inverse], axis=0)


def norm_one_kernel(inputs, region, params, grouping, shifted, stats):
    sums, squares = [], []
    for m in range(MAPS):
        values = inputs[m].astype(F32)
        masked = values * valid_of(region, m)
        sums.append(column_sum(masked))
        squares.append(column_sum(masked * values))
    stats[...] = norm_stats(
        jnp.concatenate(sums, axis=0),
        jnp.concatenate(squares, axis=0),
        cells_of(region),
        grouping[...],
    )
    for m in range(MAPS):
        hat = (inputs[m].astype(F32) - stats[m : m + 1]) * stats[MAPS + m : MAPS + m + 1]
        normed = hat * params[GAIN_ONE : GAIN_ONE + 1] + params[SHIFT_ONE : SHIFT_ONE + 1]
        store_shifted(shifted, m, normed * sigmoid(normed) * valid_of(region, m))


def conv_one_kernel(
    me_ref, shifted, region, params, grouping, blocks, weight, result, stats, sums
):
    blocks.collect()
    unpack_conv(blocks.ref, me_ref, weight)

    def one_map(m, carry):
        value = convolve(shifted, m, weight) + params[BIAS_ONE : BIAS_ONE + 1]
        result[m] = value
        masked = value * valid_of(region, m)
        sums[pl.ds(m, 1)] = column_sum(masked)
        sums[pl.ds(MAPS + m, 1)] = column_sum(masked * value)
        return carry

    lax.fori_loop(0, MAPS, one_map, 0)
    stats[...] = norm_stats(sums[:MAPS], sums[MAPS:], cells_of(region), grouping[...])


def modulate(value, stats, film, params, m):
    hat = (value - stats[pl.ds(m, 1)]) * stats[pl.ds(MAPS + m, 1)]
    modulated = hat * params[GAIN_TWO : GAIN_TWO + 1] + params[SHIFT_TWO : SHIFT_TWO + 1]
    scale = 1.0 + film[pl.ds(m, 1), :WIDTH]
    return hat, modulated, scale, modulated * scale + film[pl.ds(m, 1), WIDTH:]


def conv_two_kernel(
    me_ref, conv_out, stats_two, inputs, embedding, emb_bias, region, params, grouping, blocks,
    weight, emb_weight, hidden, shifted, residual, attend_in, stats, film,
    sums,
):
    blocks.collect()
    unpack_conv(blocks.ref, me_ref, weight)
    unpack_emb(blocks.ref, me_ref, emb_weight)
    embed = embedding[...].astype(F32)
    film[...] = dot((embed * sigmoid(embed)).astype(BF16), emb_weight[...]) + emb_bias[...]

    def one_map(m, carry):
        _, _, _, normed = modulate(conv_out[m], stats_two, film, params, m)
        valid = valid_of(region, m)
        active = normed * sigmoid(normed) * valid
        hidden[m] = active.astype(BF16)
        store_shifted(shifted, m, active)
        value = (
            inputs[m].astype(F32)
            + convolve(shifted, m, weight)
            + params[BIAS_TWO : BIAS_TWO + 1]
        )
        residual[m] = value
        sums[pl.ds(m, 1)] = column_sum(value * valid)
        sums[pl.ds(MAPS + m, 1)] = column_sum(value * value * valid)
        return carry

    lax.fori_loop(0, MAPS, one_map, 0)
    stats[...] = norm_stats(sums[:MAPS], sums[MAPS:], cells_of(region), grouping[...])
    for m in range(MAPS):
        hat = (residual[m] - stats[m : m + 1]) * stats[MAPS + m : MAPS + m + 1]
        attend_in[m] = (
            hat * params[GAIN_THREE : GAIN_THREE + 1] + params[SHIFT_THREE : SHIFT_THREE + 1]
        ).astype(BF16)


def norm_back(grad, hat, along, cross, inverse, valid, cells):
    return inverse * (grad - valid * (along + cross * hat) / cells)


def attend_kernel(
    me_ref, attend_in, qkv_bias, region, region_row, cotangent, residual, stats, params, blocks,
    output, grad_attend, bias_sums, sums,
    qkv_weight, proj_weight, columns, grad_columns, attended, terms,
):
    blocks.collect()
    unpack_proj(blocks.ref, me_ref, qkv_weight, proj_weight)

    def one_map(m, carry):
        rows = pl.ds(pl.multiple_of(m * PIXELS, PIXELS), PIXELS)
        columns[...] = (dot(attend_in[m], qkv_weight[...]) + qkv_bias[...]).astype(BF16)
        grad_attended = dot(cotangent[m], proj_weight[...]).astype(BF16)
        key_region = region[m]
        query_region = region_row[m]
        allowed = (key_region > 0) & ((key_region == query_region) | (query_region == 0))
        for head in range(HEADS):
            base = 3 * LANES * head
            queries = columns[:, base : base + LANES]
            keys = columns[:, base + LANES : base + 2 * LANES]
            values = columns[:, base + 2 * LANES : base + 3 * LANES]
            grad_out = grad_attended[:, LANES * head : LANES * (head + 1)]
            logits = jnp.where(allowed, dot(keys, queries, (1, 1)) * FACTOR, -1e30)
            raised = jnp.exp(logits - jnp.max(logits, axis=0, keepdims=True))
            weights = raised * (1.0 / jnp.sum(raised, axis=0, keepdims=True))
            weights_low = weights.astype(BF16)
            attended[rows, LANES * head : LANES * (head + 1)] = dot(
                weights_low, values, (0, 0)
            ).astype(BF16)
            grad_weights = dot(values, grad_out, (1, 1))
            inner = jnp.sum(grad_weights * weights, axis=0, keepdims=True)
            grad_logits = (weights * (grad_weights - inner)).astype(BF16)
            grad_columns[rows, base : base + LANES] = (
                dot(grad_logits, keys, (0, 0)) * FACTOR
            ).astype(BF16)
            grad_columns[rows, base + LANES : base + 2 * LANES] = (
                dot(grad_logits, queries) * FACTOR
            ).astype(BF16)
            grad_columns[rows, base + 2 * LANES : base + 3 * LANES] = dot(
                weights_low, grad_out
            ).astype(BF16)
        output[m] = (
            residual[m]
            + dot(attended[rows, :], proj_weight[...], (1, 1))
            + params[PROJ_BIAS : PROJ_BIAS + 1]
        ).astype(BF16)
        grad = dot(grad_columns[rows, :], qkv_weight[...], (1, 1))
        grad_attend[m] = grad
        hat = (residual[m] - stats[pl.ds(m, 1)]) * stats[pl.ds(MAPS + m, 1)]
        sums[pl.ds(m, 1)] = column_sum(grad)
        sums[pl.ds(MAPS + m, 1)] = column_sum(grad * hat)
        return carry

    lax.fori_loop(0, MAPS, one_map, 0)
    bias_sums[...] = column_sum(grad_columns[...].astype(F32))
    grad_qkv, grad_proj = None, None
    for m in range(MAPS):
        rows = slice(m * PIXELS, (m + 1) * PIXELS)
        qkv_part = dot(attend_in[m], grad_columns[rows, :], (0, 0))
        proj_part = dot(cotangent[m], attended[rows, :], (0, 0))
        grad_qkv = qkv_part if m == 0 else grad_qkv + qkv_part
        grad_proj = proj_part if m == 0 else grad_proj + proj_part
    for group in range(BLOCK_GROUPS):
        rows = slice(48 * group, 48 * group + 48)
        for head in range(HEADS):
            pieces = [
                grad_qkv[rows, slot * LANES : slot * LANES + HEAD_DIM]
                for slot in range(3 * head, 3 * head + 3)
            ]
            pieces.append(grad_proj[rows, head * LANES : head * LANES + HEAD_DIM])
            wide = jnp.concatenate(pieces, axis=1)
            terms[place_of(group, head, me_ref)] = jnp.concatenate(
                [wide[:, LANES * part : LANES * (part + 1)] for part in range(3)], axis=0
            ).astype(BF16)


def back_three_kernel(
    me_ref, grad_attend, sums, region, cotangent, residual, stats, params, grouping,
    grad_residual, grad_conv, kept, sent, small_sums,
):
    gain = params[GAIN_THREE : GAIN_THREE + 1]
    totals = group_total(sums[...] * gain, grouping[...])
    cells = cells_of(region)
    small_sums[...] = jnp.zeros_like(small_sums)
    small_sums[0:1] = column_sum(sums[MAPS:])
    small_sums[1:2] = column_sum(sums[:MAPS])
    top_sum = jnp.zeros((1, WIDTH), F32)
    low_sum = jnp.zeros((1, WIDTH), F32)
    for m in range(MAPS):
        inverse = stats[MAPS + m : MAPS + m + 1]
        hat = (residual[m] - stats[m : m + 1]) * inverse
        top = cotangent[m].astype(F32)
        grad = top + norm_back(
            grad_attend[m] * gain,
            hat,
            totals[m : m + 1],
            totals[MAPS + m : MAPS + m + 1],
            inverse,
            valid_of(region, m),
            cells[m : m + 1],
        )
        grad_residual[m] = grad
        low = grad.astype(BF16)
        grad_conv[m] = low
        turn_halves(low.astype(F32), m, me_ref, kept, sent)
        top_sum = top_sum + column_sum(top)
        low_sum = low_sum + column_sum(low.astype(F32))
    small_sums[2:3] = top_sum
    small_sums[3:4] = low_sum


def back_two_kernel(
    me_ref, grad_conv, weight, conv_out, stats, film, region, params, grouping,
    grad_low, kept, sent, grad_film, small_sums,
    flipped, shifted, grad_normed, sums,
):
    flip_weight(flipped, weight)

    def one_map(m, carry):
        store_shifted(shifted, m, grad_conv[m].astype(F32))
        hat, modulated, scale, normed = modulate(conv_out[m], stats, film, params, m)
        logistic = sigmoid(normed)
        slope = logistic * (1.0 + normed * (1.0 - logistic)) * valid_of(region, m)
        grad = convolve_back(shifted, m, flipped) * slope
        grad_film[pl.ds(m, 1), :WIDTH] = column_sum(grad * modulated)
        grad_film[pl.ds(m, 1), WIDTH:] = column_sum(grad)
        scaled = grad * scale
        grad_normed[m] = scaled
        sums[pl.ds(m, 1)] = column_sum(scaled)
        sums[pl.ds(MAPS + m, 1)] = column_sum(scaled * hat)
        return carry

    lax.fori_loop(0, MAPS, one_map, 0)
    gain = params[GAIN_TWO : GAIN_TWO + 1]
    totals = group_total(sums[...] * gain, grouping[...])
    cells = cells_of(region)
    small_sums[...] = jnp.zeros_like(small_sums)
    small_sums[0:1] = column_sum(sums[MAPS:])
    small_sums[1:2] = column_sum(sums[:MAPS])
    low_sum = jnp.zeros((1, WIDTH), F32)
    for m in range(MAPS):
        inverse = stats[MAPS + m : MAPS + m + 1]
        low = norm_back(
            grad_normed[m] * gain,
            (conv_out[m] - stats[m : m + 1]) * inverse,
            totals[m : m + 1],
            totals[MAPS + m : MAPS + m + 1],
            inverse,
            valid_of(region, m),
            cells[m : m + 1],
        ).astype(BF16)
        grad_low[m] = low
        turn_halves(low.astype(F32), m, me_ref, kept, sent)
        low_sum = low_sum + column_sum(low.astype(F32))
    small_sums[2:3] = low_sum


def back_film_kernel(embedding, emb_weight, grad_film, grad_embed):
    embed = embedding[...].astype(F32)
    logistic = sigmoid(embed)
    film_high = grad_film[...].astype(BF16)
    film_rest = (grad_film[...] - film_high.astype(F32)).astype(BF16)
    grad_embed[...] = (
        dot(film_high, emb_weight[...], (1, 1)) + dot(film_rest, emb_weight[...], (1, 1))
    ) * (logistic * (1.0 + embed * (1.0 - logistic)))


def back_one_kernel(
    grad_conv, weight, inputs, stats, grad_residual, region, params, grouping,
    grad_inputs, small_sums,
    flipped, shifted, grad_normed, sums,
):
    flip_weight(flipped, weight)
    gain = params[GAIN_ONE : GAIN_ONE + 1]

    def one_map(m, carry):
        store_shifted(shifted, m, grad_conv[m].astype(F32))
        hat = (inputs[m].astype(F32) - stats[pl.ds(m, 1)]) * stats[pl.ds(MAPS + m, 1)]
        normed = hat * gain + params[SHIFT_ONE : SHIFT_ONE + 1]
        logistic = sigmoid(normed)
        slope = logistic * (1.0 + normed * (1.0 - logistic)) * valid_of(region, m)
        grad = convolve_back(shifted, m, flipped) * slope
        grad_normed[m] = grad
        sums[pl.ds(m, 1)] = column_sum(grad)
        sums[pl.ds(MAPS + m, 1)] = column_sum(grad * hat)
        return carry

    lax.fori_loop(0, MAPS, one_map, 0)
    totals = group_total(sums[...] * gain, grouping[...])
    cells = cells_of(region)
    small_sums[...] = jnp.zeros_like(small_sums)
    small_sums[0:1] = column_sum(sums[MAPS:])
    small_sums[1:2] = column_sum(sums[:MAPS])
    for m in range(MAPS):
        inverse = stats[MAPS + m : MAPS + m + 1]
        grad_inputs[m] = (
            grad_residual[m]
            + norm_back(
                grad_normed[m] * gain,
                (inputs[m].astype(F32) - stats[m : m + 1]) * inverse,
                totals[m : m + 1],
                totals[MAPS + m : MAPS + m + 1],
                inverse,
                valid_of(region, m),
                cells[m : m + 1],
            )
        ).astype(BF16)


def conv_weight_grads(shifted, shifted_core, kept, came, total):
    def one_row(tap_row, carry):
        rows = pl.ds(pl.multiple_of(tap_row * SIDE, SIDE), PIXELS)
        part = None
        for turned, source in ((kept, shifted), (came, shifted_core)):
            for m in range(MAPS):
                term = dot(turned[:, m * PIXELS : (m + 1) * PIXELS], source[m, rows, :])
                part = term if part is None else part + term
        total[tap_row] = part
        return carry

    lax.fori_loop(0, 3, one_row, 0)


def pack_conv_grads(total, me_ref, blocks):
    for group in range(BLOCK_GROUPS):
        start, stop = group * CONV_ROWS, (group + 1) * CONV_ROWS
        pieces = []
        for tap_row in range(3):
            low, high = tap_row * 3 * WIDTH, (tap_row + 1) * 3 * WIDTH
            if max(low, start) < min(high, stop):
                pieces.append((tap_row, max(low, start) - low, min(high, stop) - low))
        for over_x in range(2):
            rows = slice(HEAD_DIM * over_x, HEAD_DIM * (over_x + 1))
            values = [total[tap_row, rows, a:b] for tap_row, a, b in pieces]
            block = values[0] if len(values) == 1 else jnp.concatenate(values, axis=1)
            place = place_of_own(group, over_x, me_ref)
            blocks[place, 0:CONV_PACK, :] = pack_conv(block).astype(BF16)


def grads_one_kernel(me_ref, kept, came, shifted, shifted_core, total, blocks):
    conv_weight_grads(shifted, shifted_core, kept, came, total)
    pack_conv_grads(total, me_ref, blocks)


def grads_two_kernel(
    me_ref, kept, came, shifted, hidden_core, near, far, near_came, far_came,
    total, shifted_core, blocks,
):
    for m in range(MAPS):
        store_shifted(shifted_core, m, hidden_core[m].astype(F32))
    conv_weight_grads(shifted, shifted_core, kept, came, total)
    pack_conv_grads(total, me_ref, blocks)
    for index, (mine, other) in enumerate(((near, near_came), (far, far_came))):
        blocks[8 * index : 8 * index + 8, CONV_PACK:, :] = (
            mine[...].astype(F32) + other[...].astype(F32)
        ).astype(BF16)


def unpack_conv_grad(block, result):
    for part in range(3):
        result[:, LANES * part : LANES * (part + 1)] = block[HEAD_DIM * part : HEAD_DIM * (part + 1)]
    result[:, 3 * LANES :] = jnp.concatenate([block[288:336, :48], block[288:336, 48:96]], axis=0)


def first_message_kernel(small_one, small_two, small_three, column_sums, grad_film, embedding, message):
    pieces = [small_one[0:1], small_one[1:2], small_two[0:1], small_two[1:2], small_two[2:3]]
    pieces += [small_three[row : row + 1] for row in range(4)]
    for part in (0, 2):
        slots = [(3 * head + part) * LANES for head in range(HEADS)]
        pieces.append(
            jnp.concatenate([column_sums[:, slot : slot + HEAD_DIM] for slot in slots], axis=1)
        )
    film = column_sum(grad_film[...])
    pieces.append(jnp.zeros((1, WIDTH), F32))
    rows = [jnp.concatenate(pieces[k : k + 2], axis=1) for k in range(0, 12, 2)]
    sums = jnp.concatenate(rows + [film, jnp.zeros((1, 2 * WIDTH), F32)], axis=0)
    embed = embedding[...].astype(F32)
    low = (embed * sigmoid(embed)).astype(BF16).astype(F32)
    wide = jnp.concatenate([low, jnp.zeros((MAPS, 2 * WIDTH - EMBED), F32)], axis=1)
    store_sums(sums, message)
    message[SUM_ROWS:, :] = jnp.concatenate([grad_film[...], wide], axis=0).astype(BF16)


def store_sums(sums, message):
    high = sums.astype(BF16).astype(F32)
    message[0:SUM_ROWS, :] = jnp.concatenate([high, sums - high], axis=0).astype(BF16)


def added_sums(parts):
    half = SUM_ROWS // 2
    total = None
    for part in parts:
        both = part[0:SUM_ROWS, :].astype(F32)
        both = both[:half] + both[half:]
        total = both if total is None else total + both
    return total


def next_message_kernel(*refs):
    parts, message = refs[:-1], refs[-1]
    store_sums(added_sums(parts), message)
    count = parts[0].shape[0] - SUM_ROWS
    for index, part in enumerate(parts):
        start = SUM_ROWS + count * index
        message[start : start + count, :] = part[SUM_ROWS:, :]


def finish_one_kernel(me_ref, mine, other, *refs):
    parts, result, emb, vectors = refs[:4], refs[4], refs[5], refs[6:]
    unpack_conv_grad(mine[0].astype(F32) + other[0].astype(F32), result)
    sums = added_sums(parts)
    for index, vector in enumerate(vectors[:11]):
        row, place = index // 2, (index % 2) * WIDTH
        vector[...] = sums[row, place : place + WIDTH]
    vectors[11][...] = sums[6]
    total = None
    for part in parts:
        for start in range(SUM_ROWS, part.shape[0], 2 * MAPS):
            films = part[start : start + MAPS, :].astype(F32)
            embeds = part[start + MAPS : start + 2 * MAPS, :EMBED].astype(F32)
            total = (films, embeds) if total is None else (
                jnp.concatenate([total[0], films], axis=0),
                jnp.concatenate([total[1], embeds], axis=0),
            )
    products = dot(total[1].astype(BF16), total[0].astype(BF16), (0, 0))
    rows, cols = emb.shape
    mine_rows = products[0:rows]
    for group in range(1, BLOCK_GROUPS):
        mine_rows = jnp.where(me_ref[0] == group, products[rows * group : rows * (group + 1)], mine_rows)
    mine_cols = mine_rows[:, 0:cols]
    for head in range(1, HEADS):
        mine_cols = jnp.where(me_ref[1] == head, mine_rows[:, cols * head : cols * (head + 1)], mine_cols)
    emb[...] = mine_cols


def finish_two_kernel(mine, other, result, qkv, proj):
    block = mine[0].astype(F32) + other[0].astype(F32)
    unpack_conv_grad(block, result)
    tiles = [block[CONV_PACK + 48 * k : CONV_PACK + 48 * k + 48] for k in range(3)]
    wide = jnp.concatenate(tiles, axis=1)
    qkv[...] = wide[:, : 3 * HEAD_DIM]
    proj[...] = wide[:, 3 * HEAD_DIM :]


def join_kernel(left, right, joined):
    count = left.shape[0]
    joined[:count] = left[...]
    joined[count:] = right[...]


def add_split_kernel(left, right, send, keep):
    half = keep.shape[0]
    send[...] = (left[half:].astype(F32) + right[half:].astype(F32)).astype(BF16)
    keep[...] = (left[:half].astype(F32) + right[:half].astype(F32)).astype(BF16)


def swap(values, masks, sizes):
    pairs = [(own, own ^ masks[own % 2]) for own in range(sizes[0] * sizes[1])]
    return lax.ppermute(values, AXES, pairs)


def stages_of(sizes):
    inner = sizes[0] // BLOCK_GROUPS
    group_bit = sizes[1] * inner
    over_x, over_y = 2, group_bit
    return ((4 * group_bit,) * 2, (2 * group_bit,) * 2, (over_x, over_y), (over_y, over_x))


def join(left, right):
    joined = shape_of((left.shape[0] + right.shape[0],) + left.shape[1:], left.dtype)
    return run_kernel(join_kernel, "join", (left, right), (joined,), room=8)[0]


def add_split(left, right):
    half = shape_of((left.shape[0] // 2,) + left.shape[1:], BF16)
    return run_kernel(add_split_kernel, "add_split", (left, right), (half, half), room=8)


def inner_groups(sizes):
    inner = sizes[0] // BLOCK_GROUPS
    return [[group * inner + k for k in range(inner)] for group in range(BLOCK_GROUPS)]


def inner_gather(shard, sizes):
    if sizes[0] == BLOCK_GROUPS:
        return shard
    return lax.all_gather(shard, "dp", axis=0, tiled=True, axis_index_groups=inner_groups(sizes))


def inner_scatter(grad, sizes):
    if sizes[0] == BLOCK_GROUPS:
        return grad
    return lax.psum_scatter(
        grad, "dp", scatter_dimension=0, tiled=True, axis_index_groups=inner_groups(sizes)
    )


def per_device(
    inputs, embedding, region, cotangent, conv_one, bias_one, conv_two, bias_two, emb_weight,
    emb_bias, qkv_weight, q_bias, v_bias, proj_weight, proj_bias, gain_one, shift_one, gain_two,
    shift_two, gain_three, shift_three,
):
    sizes = (lax.axis_size("dp"), lax.axis_size("head"))
    inner = sizes[0] // BLOCK_GROUPS
    dp_id, head_id = lax.axis_index("dp"), lax.axis_index("head")
    me = jnp.stack([dp_id // inner, head_id]).astype(jnp.int32)
    kernel = functools.partial
    map_shape = (MAPS, PIXELS, WIDTH)
    shifted_shape = (MAPS, PADDED, 3 * WIDTH)

    shards = [inner_gather(w, sizes) for w in (conv_one, conv_two, emb_weight, qkv_weight, proj_weight)]

    first, second, third, fourth = stages_of(sizes)
    core = (1, 1)

    def send(values, masks):
        return swap(values, masks, sizes)

    stats_shape = shape_of((2 * MAPS, WIDTH), F32)
    small_shape = shape_of((8, WIDTH), F32)
    sums_scratch = pltpu.VMEM((2 * MAPS, WIDTH), F32)
    pack_one, pack_two, pack_three = run_kernel(
        pack_kernel,
        "pack",
        (shards[0].T, shards[1].T, *shards[2:]),
        (
            shape_of((1, CONV_PACK, LANES), BF16),
            shape_of((1, SECOND_ROWS, LANES), BF16),
            shape_of((1, PROJ_PACK, LANES), BF16),
        ),
        room=62,
    )
    one = send(pack_one, first)
    two = send(pack_two, first)
    three = send(pack_three, first)
    params, qkv_bias, film_bias, region_col, region_row, grouping = run_kernel(
        prepare_kernel,
        "prepare",
        (
            me, after(region, pack_one), bias_one, bias_two, gain_one, shift_one, gain_two, shift_two,
            gain_three, shift_three, proj_bias, q_bias, v_bias, emb_bias,
        ),
        (
            shape_of((16, WIDTH), F32),
            shape_of((1, SLOTS), F32),
            shape_of((1, 2 * WIDTH), F32),
            shape_of((MAPS, PIXELS, 1), jnp.int32),
            shape_of((MAPS, 1, PIXELS), jnp.int32),
            shape_of((WIDTH, WIDTH), F32),
        ),
        room=62,
    )
    held_one = join(pack_one, one)
    one = send(held_one, second)
    held_two = join(pack_two, after(two, held_one))
    two = send(held_two, second)
    held_one = join(held_one, after(one, held_two, params))
    one = send(held_one, third)
    held_three = join(pack_three, after(three, held_one))
    three = send(held_three, second)
    held_one = join(held_one, after(one, held_three))
    far_one = send(held_one, fourth)
    near_core_one = send(held_one, core)
    held_two = join(held_two, after(two, held_one))
    two = send(held_two, third)
    shifted_one, stats_one = run_kernel(
        norm_one_kernel,
        "norm_one",
        (after(inputs, held_two), region_col, params, grouping),
        (shape_of(shifted_shape, BF16), stats_shape),
    )
    held_three = join(held_three, after(three, stats_one))
    three = send(held_three, third)
    held_two = join(held_two, after(two, held_three))
    far_two = send(held_two, fourth)
    near_core_two = send(held_two, core)
    far_one = after(far_one, held_two)
    far_core_one = send(far_one, core)
    shifted_core_one = send(shifted_one, core)
    held_three = join(held_three, after(three, held_two))
    far_three = send(held_three, fourth)
    near_core_three = send(held_three, core)
    weight_shape = shape_of((WIDTH, TAPS), BF16)
    weight_one, conv_out, stats_two = run_kernel(
        conv_one_kernel,
        "conv_one",
        (
            me, after(shifted_one, held_three), region_col, params, grouping,
            held_one, far_one, near_core_one, far_core_one,
        ),
        (weight_shape, shape_of(map_shape, F32), stats_shape),
        (sums_scratch,),
        blocks=(32, CONV_PACK, LANES),
    )
    far_three = after(far_three, conv_out)
    far_core_three = send(far_three, core)
    far_two = after(far_two, conv_out)
    far_core_two = send(far_two, core)
    weight_two, film_weight, hidden_two, shifted_two, residual, attend_in, stats_three, film = run_kernel(
        conv_two_kernel,
        "conv_two",
        (
            me, after(conv_out, far_three), stats_two, inputs, embedding, film_bias, region_col,
            params, grouping, held_two, far_two, near_core_two, far_core_two,
        ),
        (
            weight_shape,
            shape_of((EMBED, 2 * WIDTH), BF16),
            shape_of(map_shape, BF16),
            shape_of(shifted_shape, BF16),
            shape_of(map_shape, F32),
            shape_of(map_shape, BF16),
            stats_shape,
            shape_of((MAPS, 2 * WIDTH), F32),
        ),
        (sums_scratch,),
        blocks=(32, SECOND_ROWS, LANES),
    )
    proj_shape = shape_of((8, PROJ_PACK, LANES), BF16)
    output, grad_attend, column_sums, sums_three, *proj_terms = run_kernel(
        attend_kernel,
        "attend",
        (
            me, attend_in, qkv_bias, region_col, region_row, cotangent, residual, stats_three, params,
            held_three, far_three, near_core_three, far_core_three,
        ),
        (shape_of(map_shape, BF16), shape_of(map_shape, F32), shape_of((1, SLOTS), F32), stats_shape)
        + (proj_shape,) * 4,
        (
            pltpu.VMEM((WIDTH, SLOTS), BF16),
            pltpu.VMEM((WIDTH, HEADS * LANES), BF16),
            pltpu.VMEM((PIXELS, SLOTS), BF16),
            pltpu.VMEM((MAPS * PIXELS, SLOTS), BF16),
            pltpu.VMEM((MAPS * PIXELS, HEADS * LANES), BF16),
            pltpu.VMEM((32, PROJ_PACK, LANES), BF16),
        ),
        blocks=(32, PROJ_PACK, LANES),
        terms=4,
    )
    near_proj, far_proj, near_came, far_came = proj_terms
    near_came, far_came = send(near_came, core), send(far_came, core)
    hidden_core_two = send(after(hidden_two, output), core)
    turned_shape = shape_of((2 * HEAD_DIM, MAPS * PIXELS), BF16)
    grad_residual, grad_conv_two, kept, sent, small_three = run_kernel(
        back_three_kernel,
        "back_three",
        (
            me, grad_attend, sums_three, region_col, cotangent, residual, stats_three, params, grouping,
        ),
        (shape_of(map_shape, F32), shape_of(map_shape, BF16), turned_shape, turned_shape, small_shape),
    )
    came = send(after(sent, near_came, far_came, hidden_core_two), core)
    grads_scratch = pltpu.VMEM((3, 2 * HEAD_DIM, 3 * WIDTH), F32)
    grads_rows = CONV_PACK + PROJ_PACK
    near_two, far_two = run_kernel(
        grads_two_kernel,
        "weight_grads_two",
        (me, kept, came, shifted_two, hidden_core_two, near_proj, far_proj, near_came, far_came),
        (shape_of((8, grads_rows, LANES), BF16),) * 2,
        (
            grads_scratch,
            pltpu.VMEM(shifted_shape, BF16),
            pltpu.VMEM((16, grads_rows, LANES), BF16),
        ),
        terms=2,
    )
    two = send(far_two, fourth)
    back_scratch = (
        pltpu.VMEM((3, 3 * WIDTH, WIDTH), BF16),
        pltpu.VMEM(shifted_shape, BF16),
        pltpu.VMEM(map_shape, F32),
        sums_scratch,
    )
    grad_conv_one, kept, sent, grad_film, small_two = run_kernel(
        back_two_kernel,
        "back_two",
        (
            me, after(grad_conv_two, near_two, shifted_core_one), weight_two, conv_out, stats_two, film,
            region_col, params, grouping,
        ),
        (
            shape_of(map_shape, BF16),
            turned_shape,
            turned_shape,
            shape_of((MAPS, 2 * WIDTH), F32),
            small_shape,
        ),
        back_scratch,
    )
    came = send(sent, core)
    far_two, near_two = add_split(near_two, after(two, kept))
    two = send(far_two, third)
    near_one, far_one = run_kernel(
        grads_one_kernel,
        "weight_grads_one",
        (me, kept, after(came, far_two), shifted_one, shifted_core_one),
        (shape_of((8, CONV_PACK, LANES), BF16),) * 2,
        (grads_scratch, pltpu.VMEM((16, CONV_PACK, LANES), BF16)),
        terms=2,
    )
    one = send(far_one, fourth)
    far_two, near_two = add_split(near_two, after(two, near_one))
    two = send(far_two, second)
    (grad_embedding,) = run_kernel(
        back_film_kernel,
        "back_film",
        (embedding, film_weight, after(grad_film, far_two)),
        (shape_of((MAPS, EMBED), F32),),
    )
    grad_inputs, small_one = run_kernel(
        back_one_kernel,
        "back_one",
        (
            after(grad_conv_one, grad_embedding, far_two), weight_one, inputs, stats_one, grad_residual,
            region_col, params, grouping,
        ),
        (shape_of(map_shape, BF16), small_shape),
        back_scratch,
    )
    far_one, near_one = add_split(near_one, after(one, small_one))
    one = send(far_one, third)
    far_two, near_two = add_split(near_two, after(two, far_one))
    two = send(far_two, first)

    def both(left, right):
        return tuple(a ^ b for a, b in zip(left, right))

    def message(count):
        return (shape_of((SUM_ROWS + 2 * MAPS * count, 2 * WIDTH), BF16),)

    (rows,) = run_kernel(
        first_message_kernel,
        "first_message",
        (after(small_one, far_two), small_two, small_three, column_sums, grad_film, embedding),
        message(1),
        room=8,
    )
    came = (rows, send(rows, core))
    far_one, near_one = add_split(near_one, after(one, came[1]))
    one = send(far_one, second)
    (rows,) = run_kernel(
        next_message_kernel, "next_message", (after(came[0], far_one), came[1]), message(2), room=8
    )
    came = [rows] + [send(rows, masks) for masks in (first, second, both(first, second))]
    conv_grad_shape = shape_of((HEAD_DIM, CONV_ROWS), F32)
    grad_weight_two, grad_qkv_weight, grad_proj_weight = run_kernel(
        finish_two_kernel,
        "finish_two",
        (near_two, after(two, rows)),
        (conv_grad_shape, shape_of((48, 3 * HEAD_DIM), F32), shape_of((48, HEAD_DIM), F32)),
        room=8,
    )
    far_one, near_one = add_split(near_one, after(one, grad_weight_two))
    one = send(far_one, first)
    (rows,) = run_kernel(
        next_message_kernel,
        "next_message",
        (after(came[0], far_one), *came[1:]),
        message(8),
        room=8,
    )
    came = [rows] + [send(rows, masks) for masks in (third, fourth, both(third, fourth))]
    vector = shape_of((WIDTH,), F32)
    grad_weight_one, grad_emb_weight, *vectors = run_kernel(
        finish_one_kernel,
        "finish_one",
        (me, near_one, one, *came),
        (conv_grad_shape, shape_of((EMBED // BLOCK_GROUPS, 2 * WIDTH // HEADS), F32))
        + (vector,) * 11
        + (shape_of((2 * WIDTH,), F32),),
        room=8,
    )
    finals = [
        inner_scatter(grad, sizes)
        for grad in (
            grad_weight_one.T, grad_weight_two.T, grad_emb_weight, grad_qkv_weight, grad_proj_weight,
        )
    ]
    return (
        output,
        grad_inputs,
        grad_embedding,
        *finals,
        vectors[4],
        vectors[8],
        vectors[11],
        vectors[9],
        vectors[10],
        vectors[7],
        vectors[0],
        vectors[1],
        vectors[2],
        vectors[3],
        vectors[5],
        vectors[6],
    )


def solution(mesh):
    own = P(AXES)
    split = P("dp", "head")
    whole = P()
    in_specs = (own, own, P("dp"), own, split, whole, split, whole, split, whole, split) + (
        (whole, whole, split) + (whole,) * 7
    )
    out_specs = (own,) * 3 + (split,) * 5 + (whole,) * 12
    return jax.shard_map(
        per_device, mesh=mesh, in_specs=in_specs, out_specs=out_specs, check_vma=False
    )
```

```python
import functools

import jax
import jax.numpy as jnp
from jax import lax
from jax.experimental import pallas as pl
from jax.experimental.pallas import tpu as pltpu
from jax.sharding import PartitionSpec as P

WIDTH = 384
EMBED = 512
HEADS = 4
HEAD_DIM = 96
GROUP_SIZE = 12
SIDE = 16
PIXELS = 256
MAPS = 4
LANES = 128
TAPS = 9 * WIDTH
PADDED = PIXELS + 2 * SIDE
SLOTS = 3 * HEADS * LANES
FACTOR = HEAD_DIM ** (-0.5)
EPS = 1e-05
AXES = ("dp", "head")

BLOCK_GROUPS = 8
CONV_ROWS = TAPS // BLOCK_GROUPS
CONV_PACK = 336
EMB_PACK = 96
SUM_ROWS = 16
PROJ_PACK = 144
SECOND_ROWS = CONV_PACK + EMB_PACK
ROOM = 28
FLOPS_PER_US = 1.15e9
DURATIONS = {
    "norm_one": 2.4,
    "conv_one": 6,
    "conv_two": 8,
    "attend": 15,
    "back_three": 2.5,
    "own_grads": 3.5,
    "weight_grads_two": 4.5,
    "back_two": 7.5,
    "back_film": 1.1,
    "weight_grads_one": 4,
    "back_one": 7,
}

F32 = jnp.float32
BF16 = jnp.bfloat16
BIAS_ONE, BIAS_TWO, GAIN_ONE, SHIFT_ONE, GAIN_TWO, SHIFT_TWO, GAIN_THREE, SHIFT_THREE, PROJ_BIAS = (
    range(9)
)

VMEM = pl.BlockSpec(memory_space=pltpu.VMEM)
SMEM = pl.BlockSpec(memory_space=pltpu.SMEM)


def after(value, *others):
    return lax.optimization_barrier((value, *others))[0]


class Parts:
    def __init__(self, parts, ref):
        self.parts, self.ref = parts, ref

    def collect(self):
        first = self.ref.shape[1] - self.parts[0].shape[1]
        for index, part in enumerate(self.parts):
            self.ref[8 * index : 8 * index + 8, first:] = part[...]


def run_kernel(kernel, name, operands, outs, scratch=(), room=ROOM, blocks=None, terms=0):
    operands = tuple(operands)
    plain = len(operands) - (blocks[0] // 8 if blocks else 0)
    direct = len(outs) - terms
    in_specs = [SMEM if value.dtype == jnp.int32 and value.ndim == 1 else VMEM for value in operands]
    scratch = list(scratch)
    own = len(scratch)
    if blocks:
        scratch.append(pltpu.VMEM(blocks, BF16))

    def body(*refs):
        ins = refs[: len(operands)]
        results = refs[len(operands) : len(operands) + len(outs)]
        given = refs[len(operands) + len(outs) :]
        held = [Parts(ins[plain:], given[own])] if blocks else []
        kernel(*ins[:plain], *held, *results[:direct], *given[:own])
        for k in range(terms):
            results[direct + k][...] = given[own - 1][8 * k : 8 * k + 8]

    return pl.pallas_call(
        body,
        out_shape=list(outs),
        in_specs=in_specs,
        out_specs=[VMEM] * len(outs),
        scratch_shapes=scratch,
        compiler_params=pltpu.CompilerParams(vmem_limit_bytes=room * 2**20),
        cost_estimate=pl.CostEstimate(
            flops=int(FLOPS_PER_US * DURATIONS.get(name, 0.5)), bytes_accessed=0, transcendentals=0
        ),
        name=name,
    )(*operands)


def shape_of(shape, dtype):
    return jax.ShapeDtypeStruct(shape, dtype)


def dot(left, right, dims=(1, 0)):
    return lax.dot_general(
        left, right, (((dims[0],), (dims[1],)), ((), ())), preferred_element_type=F32
    )


def group_total(rows, grouping):
    return lax.dot_general(
        rows,
        grouping,
        (((1,), (0,)), ((), ())),
        preferred_element_type=F32,
        precision=lax.Precision.HIGHEST,
    )


def sigmoid(values):
    return 1.0 / (1.0 + jnp.exp(-values))


def valid_of(region_ref, index):
    return (region_ref[index] > 0).astype(F32)


def cells_of(region_ref):
    counts = [jnp.sum(valid_of(region_ref, m), axis=0, keepdims=True) for m in range(MAPS)]
    return jnp.concatenate(counts, axis=0) * float(GROUP_SIZE)


def column_sum(values):
    return jnp.sum(values, axis=0, keepdims=True)


def store_shifted(target_ref, index, values):
    column = lax.broadcasted_iota(jnp.int32, (PIXELS, 1), 0) % SIDE
    left = jnp.where(column == 0, 0.0, pltpu.roll(values, 1, 0))
    right = jnp.where(column == SIDE - 1, 0.0, pltpu.roll(values, PIXELS - 1, 0))
    border = jnp.zeros((SIDE, 3 * WIDTH), BF16)
    target_ref[index, 0:SIDE, :] = border
    target_ref[index, SIDE + PIXELS : PADDED, :] = border
    for position, part in enumerate((left, values, right)):
        target_ref[index, SIDE : SIDE + PIXELS, position * WIDTH : (position + 1) * WIDTH] = (
            part.astype(BF16)
        )


def convolve(shifted_ref, index, weight_ref):
    total = None
    for tap_row in range(3):
        part = dot(
            shifted_ref[index, tap_row * SIDE : tap_row * SIDE + PIXELS, :],
            weight_ref[:, tap_row * 3 * WIDTH : (tap_row + 1) * 3 * WIDTH],
            (1, 1),
        )
        total = part if total is None else total + part
    return total


def flip_weight(flipped_ref, weight_ref):
    for tap_row in range(3):
        for tap_col in range(3):
            start = (3 * (2 - tap_row) + 2 - tap_col) * WIDTH
            flipped_ref[tap_row, tap_col * WIDTH : (tap_col + 1) * WIDTH, :] = weight_ref[
                :, start : start + WIDTH
            ]


def convolve_back(shifted_ref, index, flipped_ref):
    total = None
    for tap_row in range(3):
        part = dot(
            shifted_ref[index, tap_row * SIDE : tap_row * SIDE + PIXELS, :],
            flipped_ref[tap_row],
        )
        total = part if total is None else total + part
    return total


def pack_conv(shard):
    tail = shard[:, 3 * LANES :]
    parts = [shard[:, LANES * k : LANES * (k + 1)] for k in range(3)]
    parts.append(jnp.concatenate([tail[:48], tail[48:], jnp.zeros((48, 32), shard.dtype)], axis=1))
    return jnp.concatenate(parts, axis=0)


def pack_proj(qkv, proj):
    wide = jnp.concatenate([qkv, proj], axis=1)
    return jnp.concatenate([wide[:, LANES * k : LANES * (k + 1)] for k in range(3)], axis=0)


def pack_emb(shard):
    side = shard[:, LANES:]
    half = side.shape[0] // 2
    return jnp.concatenate(
        [shard[:, :LANES], jnp.concatenate([side[:half], side[half:]], axis=1)], axis=0
    )


def prepare_kernel(
    me_ref, region, bias_one, bias_two, gain_one, shift_one, gain_two, shift_two, gain_three,
    shift_three, proj_bias, q_bias, v_bias, emb_bias,
    params, qkv_bias, film_bias, region_col, region_row, grouping,
):
    vectors = (
        bias_one, bias_two, gain_one, shift_one, gain_two, shift_two, gain_three, shift_three,
        proj_bias,
    )
    for row, vector in enumerate(vectors):
        params[row : row + 1, :] = vector[...].reshape(1, WIDTH)
    queries, values = q_bias[...].reshape(1, WIDTH), v_bias[...].reshape(1, WIDTH)
    gap = jnp.zeros((1, LANES - HEAD_DIM), F32)
    for head in range(HEADS):
        part = slice(HEAD_DIM * head, HEAD_DIM * (head + 1))
        base = 3 * LANES * head
        qkv_bias[:, base : base + LANES] = jnp.concatenate([queries[:, part], gap], axis=1)
        qkv_bias[:, base + LANES : base + 2 * LANES] = jnp.zeros((1, LANES), F32)
        qkv_bias[:, base + 2 * LANES : base + 3 * LANES] = jnp.concatenate(
            [values[:, part], gap], axis=1
        )
    film_bias[...] = emb_bias[...].reshape(1, 2 * WIDTH)
    rows = region[...].astype(F32)
    home = me_ref[1] * MAPS
    turned = jnp.concatenate([rows, jnp.zeros((LANES - rows.shape[0], PIXELS), F32)], axis=0).T
    lane = lax.broadcasted_iota(jnp.int32, (PIXELS, LANES), 1)
    for m in range(MAPS):
        region_row[m] = region[pl.ds(home + m, 1)]
        region_col[m] = jnp.sum(
            jnp.where(lane == home + m, turned, 0.0), axis=1, keepdims=True
        ).astype(jnp.int32)
    down = lax.broadcasted_iota(jnp.int32, (WIDTH, WIDTH), 0)
    along = lax.broadcasted_iota(jnp.int32, (WIDTH, WIDTH), 1)
    grouping[...] = (down // GROUP_SIZE == along // GROUP_SIZE).astype(F32)


def pack_kernel(conv_one, conv_two, emb, qkv, proj, first, second):
    first[0] = pack_conv(conv_one[...].astype(F32)).astype(BF16)
    second[0, 0:CONV_PACK] = pack_conv(conv_two[...].astype(F32)).astype(BF16)
    second[0, CONV_PACK:SECOND_ROWS] = pack_emb(emb[...].astype(F32)).astype(BF16)
    second[0, SECOND_ROWS:] = pack_proj(qkv[...].astype(F32), proj[...].astype(F32)).astype(BF16)


def place_of(group, head, me_ref):
    far_group = group ^ me_ref[0]
    far_head = head ^ me_ref[1]
    bits = [far_group // 4, (far_group // 2) & 1, far_head // 2, far_group & 1]
    if head % 2 == 1:
        bits[2:] = bits[:1:-1]
    place = 16 * (far_head & 1)
    for position, bit in enumerate(bits):
        place = place + (1 << position) * bit
    return place


def place_of_own(group, over_x, me_ref):
    far_group = group ^ me_ref[0]
    far_x = over_x ^ (me_ref[1] // 2)
    far_y = far_group & 1
    odd = (me_ref[1] & 1) == 1
    place = far_group // 4 + 2 * ((far_group // 2) & 1)
    return place + jnp.where(odd, 4 * far_y + 8 * far_x, 4 * far_x + 8 * far_y)


def turn_halves(values, index, me_ref, kept, sent):
    odd = (me_ref[1] & 1) == 1
    turned = values.T
    place = pl.ds(index * PIXELS, PIXELS)
    for over_x in range(2):
        low = turned[2 * HEAD_DIM * over_x : 2 * HEAD_DIM * over_x + HEAD_DIM]
        high = turned[2 * HEAD_DIM * over_x + HEAD_DIM : 2 * HEAD_DIM * (over_x + 1)]
        rows = slice(HEAD_DIM * over_x, HEAD_DIM * (over_x + 1))
        kept[rows, place] = jnp.where(odd, high, low).astype(BF16)
        sent[rows, place] = jnp.where(odd, low, high).astype(BF16)


def repeat(count, step):
    def body(index, carry):
        step(index)
        return carry

    lax.fori_loop(0, count, body, 0)


def rows_of(index, size):
    return pl.ds(pl.multiple_of(index * size, 16), size)


def unpack_conv(blocks, me_ref, weight_ref):
    for head in range(HEADS):
        pieces = []
        for group in range(BLOCK_GROUPS):
            block = blocks[place_of(group, head, me_ref), 0:CONV_PACK].astype(F32)
            pieces += [block[HEAD_DIM * k : HEAD_DIM * (k + 1)] for k in range(3)]
            pieces.append(jnp.concatenate([block[288:, :48], block[288:, 48:96]], axis=0))
        weight_ref[HEAD_DIM * head : HEAD_DIM * (head + 1), :] = jnp.concatenate(
            pieces, axis=1
        ).astype(BF16)


def unpack_emb(blocks, me_ref, emb_ref):
    for group in range(BLOCK_GROUPS):
        embs = []
        for head in range(HEADS):
            emb = blocks[place_of(group, head, me_ref), CONV_PACK:].astype(F32)
            side = jnp.concatenate([emb[64:96, :64], emb[64:96, 64:]], axis=0)
            embs.append(jnp.concatenate([emb[:64], side], axis=1))
        emb_ref[64 * group : 64 * group + 64] = jnp.concatenate(embs, axis=1).astype(BF16)


def unpack_proj(blocks, me_ref, qkv_ref, proj_ref):
    gap = jnp.zeros((48, LANES - HEAD_DIM), F32)
    for group in range(BLOCK_GROUPS):
        rows = slice(48 * group, 48 * group + 48)
        for head in range(HEADS):
            block = blocks[place_of(group, head, me_ref)].astype(F32)
            wide = jnp.concatenate([block[48 * k : 48 * k + 48] for k in range(3)], axis=1)
            for part in range(3):
                piece = wide[:, HEAD_DIM * part : HEAD_DIM * (part + 1)]
                slot = (3 * head + part) * LANES
                qkv_ref[rows, slot : slot + LANES] = jnp.concatenate([piece, gap], axis=1).astype(
                    BF16
                )
            proj_ref[rows, LANES * head : LANES * (head + 1)] = jnp.concatenate(
                [wide[:, 3 * HEAD_DIM :], gap], axis=1
            ).astype(BF16)


def norm_stats(sums, squares, cells, grouping):
    totals = group_total(jnp.concatenate([sums, squares], axis=0), grouping)
    mean = totals[:MAPS] / cells
    inverse = lax.rsqrt(totals[MAPS:] / cells - mean * mean + EPS)
    return jnp.concatenate([mean, inverse], axis=0)


def norm_one_kernel(inputs, region, params, grouping, shifted, stats, sums):
    def add_map(m):
        values = inputs[m].astype(F32)
        masked = values * valid_of(region, m)
        sums[pl.ds(m, 1)] = column_sum(masked)
        sums[pl.ds(MAPS + m, 1)] = column_sum(masked * values)

    def one_map(m):
        hat = (inputs[m].astype(F32) - stats[pl.ds(m, 1)]) * stats[pl.ds(MAPS + m, 1)]
        normed = hat * params[GAIN_ONE : GAIN_ONE + 1] + params[SHIFT_ONE : SHIFT_ONE + 1]
        store_shifted(shifted, m, normed * sigmoid(normed) * valid_of(region, m))

    repeat(MAPS, add_map)
    stats[...] = norm_stats(sums[:MAPS], sums[MAPS:], cells_of(region), grouping[...])
    repeat(MAPS, one_map)


def conv_one_kernel(
    me_ref, shifted, region, params, grouping, blocks, weight, result, stats, sums
):
    blocks.collect()
    unpack_conv(blocks.ref, me_ref, weight)

    def one_map(m, carry):
        value = convolve(shifted, m, weight) + params[BIAS_ONE : BIAS_ONE + 1]
        result[m] = value
        masked = value * valid_of(region, m)
        sums[pl.ds(m, 1)] = column_sum(masked)
        sums[pl.ds(MAPS + m, 1)] = column_sum(masked * value)
        return carry

    lax.fori_loop(0, MAPS, one_map, 0, unroll=True)
    stats[...] = norm_stats(sums[:MAPS], sums[MAPS:], cells_of(region), grouping[...])


def modulate(value, stats, film, params, m):
    hat = (value - stats[pl.ds(m, 1)]) * stats[pl.ds(MAPS + m, 1)]
    modulated = hat * params[GAIN_TWO : GAIN_TWO + 1] + params[SHIFT_TWO : SHIFT_TWO + 1]
    scale = 1.0 + film[pl.ds(m, 1), :WIDTH]
    return hat, modulated, scale, modulated * scale + film[pl.ds(m, 1), WIDTH:]


def conv_two_kernel(
    me_ref, conv_out, stats_two, inputs, embedding, emb_bias, region, params, grouping, blocks,
    weight, emb_weight, hidden, shifted, residual, attend_in, stats, film,
    sums,
):
    blocks.collect()
    unpack_conv(blocks.ref, me_ref, weight)
    unpack_emb(blocks.ref, me_ref, emb_weight)
    embed = embedding[...].astype(F32)
    film[...] = dot((embed * sigmoid(embed)).astype(BF16), emb_weight[...]) + emb_bias[...]

    def one_map(m, carry):
        _, _, _, normed = modulate(conv_out[m], stats_two, film, params, m)
        valid = valid_of(region, m)
        active = normed * sigmoid(normed) * valid
        hidden[m] = active.astype(BF16)
        store_shifted(shifted, m, active)
        value = (
            inputs[m].astype(F32)
            + convolve(shifted, m, weight)
            + params[BIAS_TWO : BIAS_TWO + 1]
        )
        residual[m] = value
        sums[pl.ds(m, 1)] = column_sum(value * valid)
        sums[pl.ds(MAPS + m, 1)] = column_sum(value * value * valid)
        return carry

    lax.fori_loop(0, MAPS, one_map, 0, unroll=True)
    stats[...] = norm_stats(sums[:MAPS], sums[MAPS:], cells_of(region), grouping[...])
    for m in range(MAPS):
        hat = (residual[m] - stats[m : m + 1]) * stats[MAPS + m : MAPS + m + 1]
        attend_in[m] = (
            hat * params[GAIN_THREE : GAIN_THREE + 1] + params[SHIFT_THREE : SHIFT_THREE + 1]
        ).astype(BF16)


def norm_back(grad, hat, along, cross, inverse, valid, cells):
    return inverse * (grad - valid * (along + cross * hat) / cells)


def attend_kernel(
    me_ref, attend_in, qkv_bias, region, region_row, cotangent, residual, stats, params, blocks,
    output, grad_attend, bias_sums, sums,
    qkv_weight, proj_weight, columns, grad_columns, attended, terms,
):
    blocks.collect()
    unpack_proj(blocks.ref, me_ref, qkv_weight, proj_weight)

    def one_map(m, carry):
        rows = pl.ds(pl.multiple_of(m * PIXELS, PIXELS), PIXELS)
        columns[...] = (dot(attend_in[m], qkv_weight[...]) + qkv_bias[...]).astype(BF16)
        grad_attended = dot(cotangent[m], proj_weight[...]).astype(BF16)
        key_region = region[m]
        query_region = region_row[m]
        allowed = (key_region > 0) & ((key_region == query_region) | (query_region == 0))
        for head in range(HEADS):
            base = 3 * LANES * head
            queries = columns[:, base : base + LANES]
            keys = columns[:, base + LANES : base + 2 * LANES]
            values = columns[:, base + 2 * LANES : base + 3 * LANES]
            grad_out = grad_attended[:, LANES * head : LANES * (head + 1)]
            logits = jnp.where(allowed, dot(keys, queries, (1, 1)) * FACTOR, -1e30)
            raised = jnp.exp(logits - jnp.max(logits, axis=0, keepdims=True))
            weights = raised * (1.0 / jnp.sum(raised, axis=0, keepdims=True))
            weights_low = weights.astype(BF16)
            attended[rows, LANES * head : LANES * (head + 1)] = dot(
                weights_low, values, (0, 0)
            ).astype(BF16)
            grad_weights = dot(values, grad_out, (1, 1))
            inner = jnp.sum(grad_weights * weights, axis=0, keepdims=True)
            grad_logits = (weights * (grad_weights - inner)).astype(BF16)
            grad_columns[rows, base : base + LANES] = (
                dot(grad_logits, keys, (0, 0)) * FACTOR
            ).astype(BF16)
            grad_columns[rows, base + LANES : base + 2 * LANES] = (
                dot(grad_logits, queries) * FACTOR
            ).astype(BF16)
            grad_columns[rows, base + 2 * LANES : base + 3 * LANES] = dot(
                weights_low, grad_out
            ).astype(BF16)
        output[m] = (
            residual[m]
            + dot(attended[rows, :], proj_weight[...], (1, 1))
            + params[PROJ_BIAS : PROJ_BIAS + 1]
        ).astype(BF16)
        grad = dot(grad_columns[rows, :], qkv_weight[...], (1, 1))
        grad_attend[m] = grad
        hat = (residual[m] - stats[pl.ds(m, 1)]) * stats[pl.ds(MAPS + m, 1)]
        sums[pl.ds(m, 1)] = column_sum(grad)
        sums[pl.ds(MAPS + m, 1)] = column_sum(grad * hat)
        return carry

    lax.fori_loop(0, MAPS, one_map, 0)
    bias_sums[...] = column_sum(grad_columns[...].astype(F32))
    grad_qkv, grad_proj = None, None
    for m in range(MAPS):
        rows = slice(m * PIXELS, (m + 1) * PIXELS)
        qkv_part = dot(attend_in[m], grad_columns[rows, :], (0, 0))
        proj_part = dot(cotangent[m], attended[rows, :], (0, 0))
        grad_qkv = qkv_part if m == 0 else grad_qkv + qkv_part
        grad_proj = proj_part if m == 0 else grad_proj + proj_part
    for group in range(BLOCK_GROUPS):
        rows = slice(48 * group, 48 * group + 48)
        for head in range(HEADS):
            pieces = [
                grad_qkv[rows, slot * LANES : slot * LANES + HEAD_DIM]
                for slot in range(3 * head, 3 * head + 3)
            ]
            pieces.append(grad_proj[rows, head * LANES : head * LANES + HEAD_DIM])
            wide = jnp.concatenate(pieces, axis=1)
            terms[place_of(group, head, me_ref)] = jnp.concatenate(
                [wide[:, LANES * part : LANES * (part + 1)] for part in range(3)], axis=0
            ).astype(BF16)


def back_three_kernel(
    me_ref, grad_attend, sums, region, cotangent, residual, stats, params, grouping,
    grad_residual, grad_conv, kept, sent, small_sums,
):
    gain = params[GAIN_THREE : GAIN_THREE + 1]
    totals = group_total(sums[...] * gain, grouping[...])
    cells = cells_of(region)
    small_sums[...] = jnp.zeros_like(small_sums)
    small_sums[0:1] = column_sum(sums[MAPS:])
    small_sums[1:2] = column_sum(sums[:MAPS])
    top_sum = jnp.zeros((1, WIDTH), F32)
    low_sum = jnp.zeros((1, WIDTH), F32)
    for m in range(MAPS):
        inverse = stats[MAPS + m : MAPS + m + 1]
        hat = (residual[m] - stats[m : m + 1]) * inverse
        top = cotangent[m].astype(F32)
        grad = top + norm_back(
            grad_attend[m] * gain,
            hat,
            totals[m : m + 1],
            totals[MAPS + m : MAPS + m + 1],
            inverse,
            valid_of(region, m),
            cells[m : m + 1],
        )
        grad_residual[m] = grad
        low = grad.astype(BF16)
        grad_conv[m] = low
        turn_halves(low.astype(F32), m, me_ref, kept, sent)
        top_sum = top_sum + column_sum(top)
        low_sum = low_sum + column_sum(low.astype(F32))
    small_sums[2:3] = top_sum
    small_sums[3:4] = low_sum


def back_two_kernel(
    me_ref, grad_conv, weight, conv_out, stats, film, region, params, grouping,
    grad_low, kept, sent, grad_film, small_sums,
    flipped, shifted, grad_normed, sums,
):
    flip_weight(flipped, weight)

    def one_map(m, carry):
        store_shifted(shifted, m, grad_conv[m].astype(F32))
        hat, modulated, scale, normed = modulate(conv_out[m], stats, film, params, m)
        logistic = sigmoid(normed)
        slope = logistic * (1.0 + normed * (1.0 - logistic)) * valid_of(region, m)
        grad = convolve_back(shifted, m, flipped) * slope
        grad_film[pl.ds(m, 1), :WIDTH] = column_sum(grad * modulated)
        grad_film[pl.ds(m, 1), WIDTH:] = column_sum(grad)
        scaled = grad * scale
        grad_normed[m] = scaled
        sums[pl.ds(m, 1)] = column_sum(scaled)
        sums[pl.ds(MAPS + m, 1)] = column_sum(scaled * hat)
        return carry

    lax.fori_loop(0, MAPS, one_map, 0)
    gain = params[GAIN_TWO : GAIN_TWO + 1]
    totals = group_total(sums[...] * gain, grouping[...])
    cells = cells_of(region)
    small_sums[...] = jnp.zeros_like(small_sums)
    small_sums[0:1] = column_sum(sums[MAPS:])
    small_sums[1:2] = column_sum(sums[:MAPS])
    low_sum = jnp.zeros((1, WIDTH), F32)
    for m in range(MAPS):
        inverse = stats[MAPS + m : MAPS + m + 1]
        low = norm_back(
            grad_normed[m] * gain,
            (conv_out[m] - stats[m : m + 1]) * inverse,
            totals[m : m + 1],
            totals[MAPS + m : MAPS + m + 1],
            inverse,
            valid_of(region, m),
            cells[m : m + 1],
        ).astype(BF16)
        grad_low[m] = low
        turn_halves(low.astype(F32), m, me_ref, kept, sent)
        low_sum = low_sum + column_sum(low.astype(F32))
    small_sums[2:3] = low_sum


def back_film_kernel(embedding, emb_weight, grad_film, grad_embed):
    embed = embedding[...].astype(F32)
    logistic = sigmoid(embed)
    film_high = grad_film[...].astype(BF16)
    film_rest = (grad_film[...] - film_high.astype(F32)).astype(BF16)
    grad_embed[...] = (
        dot(film_high, emb_weight[...], (1, 1)) + dot(film_rest, emb_weight[...], (1, 1))
    ) * (logistic * (1.0 + embed * (1.0 - logistic)))


def back_one_kernel(
    grad_conv, weight, inputs, stats, grad_residual, region, params, grouping,
    grad_inputs, small_sums,
    flipped, shifted, grad_normed, sums,
):
    flip_weight(flipped, weight)
    gain = params[GAIN_ONE : GAIN_ONE + 1]

    def one_map(m, carry):
        store_shifted(shifted, m, grad_conv[m].astype(F32))
        hat = (inputs[m].astype(F32) - stats[pl.ds(m, 1)]) * stats[pl.ds(MAPS + m, 1)]
        normed = hat * gain + params[SHIFT_ONE : SHIFT_ONE + 1]
        logistic = sigmoid(normed)
        slope = logistic * (1.0 + normed * (1.0 - logistic)) * valid_of(region, m)
        grad = convolve_back(shifted, m, flipped) * slope
        grad_normed[m] = grad
        sums[pl.ds(m, 1)] = column_sum(grad)
        sums[pl.ds(MAPS + m, 1)] = column_sum(grad * hat)
        return carry

    lax.fori_loop(0, MAPS, one_map, 0)
    totals = group_total(sums[...] * gain, grouping[...])
    cells = cells_of(region)
    small_sums[...] = jnp.zeros_like(small_sums)
    small_sums[0:1] = column_sum(sums[MAPS:])
    small_sums[1:2] = column_sum(sums[:MAPS])
    for m in range(MAPS):
        inverse = stats[MAPS + m : MAPS + m + 1]
        grad_inputs[m] = (
            grad_residual[m]
            + norm_back(
                grad_normed[m] * gain,
                (inputs[m].astype(F32) - stats[m : m + 1]) * inverse,
                totals[m : m + 1],
                totals[MAPS + m : MAPS + m + 1],
                inverse,
                valid_of(region, m),
                cells[m : m + 1],
            )
        ).astype(BF16)


def conv_weight_grads(shifted, turned, total, begun=None):
    def one_row(tap_row, carry):
        rows = pl.ds(pl.multiple_of(tap_row * SIDE, SIDE), PIXELS)
        part = None if begun is None else begun[tap_row]
        for m in range(MAPS):
            term = dot(turned[:, m * PIXELS : (m + 1) * PIXELS], shifted[m, rows, :])
            part = term if part is None else part + term
        total[tap_row] = part
        return carry

    lax.fori_loop(0, 3, one_row, 0)


def own_grads_kernel(kept, shifted, total):
    conv_weight_grads(shifted, kept, total)


def pack_conv_grads(total, me_ref, blocks):
    def one_half(over_x):
        rows = rows_of(over_x, HEAD_DIM)
        for group in range(BLOCK_GROUPS):
            start, stop = group * CONV_ROWS, (group + 1) * CONV_ROWS
            values = []
            for tap_row in range(3):
                low, high = tap_row * 3 * WIDTH, (tap_row + 1) * 3 * WIDTH
                if max(low, start) < min(high, stop):
                    values.append(total[tap_row, rows, max(low, start) - low : min(high, stop) - low])
            block = values[0] if len(values) == 1 else jnp.concatenate(values, axis=1)
            place = place_of_own(group, over_x, me_ref)
            blocks[place, 0:CONV_PACK, :] = pack_conv(block).astype(BF16)

    repeat(2, one_half)


def grads_one_kernel(me_ref, came, shifted_core, begun, total, blocks):
    conv_weight_grads(shifted_core, came, total, begun)
    pack_conv_grads(total, me_ref, blocks)


def grads_two_kernel(
    me_ref, came, hidden_core, begun, near, far, near_came, far_came, total, shifted_core, blocks
):
    for m in range(MAPS):
        store_shifted(shifted_core, m, hidden_core[m].astype(F32))
    conv_weight_grads(shifted_core, came, total, begun)
    pack_conv_grads(total, me_ref, blocks)
    for index, (mine, other) in enumerate(((near, near_came), (far, far_came))):
        blocks[8 * index : 8 * index + 8, CONV_PACK:, :] = (
            mine[...].astype(F32) + other[...].astype(F32)
        ).astype(BF16)


def unpack_conv_grad(block, result):
    for part in range(3):
        result[:, LANES * part : LANES * (part + 1)] = block[HEAD_DIM * part : HEAD_DIM * (part + 1)]
    result[:, 3 * LANES :] = jnp.concatenate([block[288:336, :48], block[288:336, 48:96]], axis=0)


def first_message_kernel(small_one, small_two, small_three, column_sums, grad_film, embedding, message):
    pieces = [small_one[0:1], small_one[1:2], small_two[0:1], small_two[1:2], small_two[2:3]]
    pieces += [small_three[row : row + 1] for row in range(4)]
    for part in (0, 2):
        slots = [(3 * head + part) * LANES for head in range(HEADS)]
        pieces.append(
            jnp.concatenate([column_sums[:, slot : slot + HEAD_DIM] for slot in slots], axis=1)
        )
    film = column_sum(grad_film[...])
    pieces.append(jnp.zeros((1, WIDTH), F32))
    rows = [jnp.concatenate(pieces[k : k + 2], axis=1) for k in range(0, 12, 2)]
    sums = jnp.concatenate(rows + [film, jnp.zeros((1, 2 * WIDTH), F32)], axis=0)
    embed = embedding[...].astype(F32)
    low = (embed * sigmoid(embed)).astype(BF16).astype(F32)
    wide = jnp.concatenate([low, jnp.zeros((MAPS, 2 * WIDTH - EMBED), F32)], axis=1)
    store_sums(sums, message)
    message[SUM_ROWS:, :] = jnp.concatenate([grad_film[...], wide], axis=0).astype(BF16)


def store_sums(sums, message):
    high = sums.astype(BF16).astype(F32)
    message[0:SUM_ROWS, :] = jnp.concatenate([high, sums - high], axis=0).astype(BF16)


def added_sums(parts):
    half = SUM_ROWS // 2
    total = None
    for part in parts:
        both = part[0:SUM_ROWS, :].astype(F32)
        both = both[:half] + both[half:]
        total = both if total is None else total + both
    return total


def next_message_kernel(*refs):
    parts, message = refs[:-1], refs[-1]
    store_sums(added_sums(parts), message)
    count = parts[0].shape[0] - SUM_ROWS
    for index, part in enumerate(parts):
        start = SUM_ROWS + count * index
        message[start : start + count, :] = part[SUM_ROWS:, :]


def finish_one_kernel(mine, other, result):
    unpack_conv_grad(mine[0].astype(F32) + other[0].astype(F32), result)


def finish_rows_kernel(me_ref, *refs):
    parts, emb, vectors = refs[:2], refs[2], refs[3:]
    sums = added_sums(parts)
    for index, vector in enumerate(vectors[:11]):
        row, place = index // 2, (index % 2) * WIDTH
        vector[...] = sums[row, place : place + WIDTH]
    vectors[11][...] = sums[6]
    total = None
    for part in parts:
        for start in range(SUM_ROWS, part.shape[0], 2 * MAPS):
            films = part[start : start + MAPS, :].astype(F32)
            embeds = part[start + MAPS : start + 2 * MAPS, :EMBED].astype(F32)
            total = (films, embeds) if total is None else (
                jnp.concatenate([total[0], films], axis=0),
                jnp.concatenate([total[1], embeds], axis=0),
            )
    products = dot(total[1].astype(BF16), total[0].astype(BF16), (0, 0))
    rows, cols = emb.shape
    mine_rows = products[0:rows]
    for group in range(1, BLOCK_GROUPS):
        mine_rows = jnp.where(me_ref[0] == group, products[rows * group : rows * (group + 1)], mine_rows)
    mine_cols = mine_rows[:, 0:cols]
    for head in range(1, HEADS):
        mine_cols = jnp.where(me_ref[1] == head, mine_rows[:, cols * head : cols * (head + 1)], mine_cols)
    emb[...] = mine_cols


def finish_two_kernel(mine, other, result, qkv, proj):
    block = mine[0].astype(F32) + other[0].astype(F32)
    unpack_conv_grad(block, result)
    tiles = [block[CONV_PACK + 48 * k : CONV_PACK + 48 * k + 48] for k in range(3)]
    wide = jnp.concatenate(tiles, axis=1)
    qkv[...] = wide[:, : 3 * HEAD_DIM]
    proj[...] = wide[:, 3 * HEAD_DIM :]


def join_kernel(left, right, joined):
    count = left.shape[0]
    joined[:count] = left[...]
    joined[count:] = right[...]


def join_split_kernel(left, right, joined, joined_last):
    count = left.shape[0]
    for index, part in enumerate((left, right)):
        joined[count * index : count * index + count] = part[:, :SECOND_ROWS]
        joined_last[count * index : count * index + count] = part[:, SECOND_ROWS:]


def add_split_kernel(left, right, send, keep):
    half = keep.shape[0]
    send[...] = (left[half:].astype(F32) + right[half:].astype(F32)).astype(BF16)
    keep[...] = (left[:half].astype(F32) + right[:half].astype(F32)).astype(BF16)


def swap(values, masks, sizes):
    pairs = [(own, own ^ masks[own % 2]) for own in range(sizes[0] * sizes[1])]
    return lax.ppermute(values, AXES, pairs)


def stages_of(sizes):
    inner = sizes[0] // BLOCK_GROUPS
    group_bit = sizes[1] * inner
    over_x, over_y = 2, group_bit
    return ((4 * group_bit,) * 2, (2 * group_bit,) * 2, (over_x, over_y), (over_y, over_x))


def join(left, right):
    joined = shape_of((left.shape[0] + right.shape[0],) + left.shape[1:], left.dtype)
    return run_kernel(join_kernel, "join", (left, right), (joined,), room=8)[0]


def add_split(left, right):
    half = shape_of((left.shape[0] // 2,) + left.shape[1:], BF16)
    return run_kernel(add_split_kernel, "add_split", (left, right), (half, half), room=8)


def inner_groups(sizes):
    inner = sizes[0] // BLOCK_GROUPS
    return [[group * inner + k for k in range(inner)] for group in range(BLOCK_GROUPS)]


def inner_gather(shard, sizes):
    if sizes[0] == BLOCK_GROUPS:
        return shard
    return lax.all_gather(shard, "dp", axis=0, tiled=True, axis_index_groups=inner_groups(sizes))


def inner_scatter(grad, sizes):
    if sizes[0] == BLOCK_GROUPS:
        return grad
    return lax.psum_scatter(
        grad, "dp", scatter_dimension=0, tiled=True, axis_index_groups=inner_groups(sizes)
    )


def per_device(
    inputs, embedding, region, cotangent, conv_one, bias_one, conv_two, bias_two, emb_weight,
    emb_bias, qkv_weight, q_bias, v_bias, proj_weight, proj_bias, gain_one, shift_one, gain_two,
    shift_two, gain_three, shift_three,
):
    sizes = (lax.axis_size("dp"), lax.axis_size("head"))
    inner = sizes[0] // BLOCK_GROUPS
    dp_id, head_id = lax.axis_index("dp"), lax.axis_index("head")
    me = jnp.stack([dp_id // inner, head_id]).astype(jnp.int32)
    kernel = functools.partial
    map_shape = (MAPS, PIXELS, WIDTH)
    shifted_shape = (MAPS, PADDED, 3 * WIDTH)

    shards = [inner_gather(w, sizes) for w in (conv_one, conv_two, emb_weight, qkv_weight, proj_weight)]

    first, second, third, fourth = stages_of(sizes)
    core = (1, 1)

    def send(values, masks):
        return swap(values, masks, sizes)

    stats_shape = shape_of((2 * MAPS, WIDTH), F32)
    small_shape = shape_of((8, WIDTH), F32)
    sums_scratch = pltpu.VMEM((2 * MAPS, WIDTH), F32)
    pack_one, pack_two = run_kernel(
        pack_kernel,
        "pack",
        (shards[0].T, shards[1].T, *shards[2:]),
        (
            shape_of((1, CONV_PACK, LANES), BF16),
            shape_of((1, SECOND_ROWS + PROJ_PACK, LANES), BF16),
        ),
        room=62,
    )
    one = send(pack_one, first)
    two = send(pack_two, first)
    params, qkv_bias, film_bias, region_col, region_row, grouping = run_kernel(
        prepare_kernel,
        "prepare",
        (
            me, after(region, pack_one), bias_one, bias_two, gain_one, shift_one, gain_two, shift_two,
            gain_three, shift_three, proj_bias, q_bias, v_bias, emb_bias,
        ),
        (
            shape_of((16, WIDTH), F32),
            shape_of((1, SLOTS), F32),
            shape_of((1, 2 * WIDTH), F32),
            shape_of((MAPS, PIXELS, 1), jnp.int32),
            shape_of((MAPS, 1, PIXELS), jnp.int32),
            shape_of((WIDTH, WIDTH), F32),
        ),
        room=62,
    )
    held_one = join(pack_one, one)
    one = send(held_one, second)
    held_two = join(pack_two, after(two, held_one))
    two = send(held_two, second)
    held_one = join(held_one, after(one, held_two, params))
    one = send(held_one, third)
    held_two = join(held_two, after(two, held_one))
    two = send(held_two, third)
    held_one = join(held_one, after(one, held_two))
    far_one = send(held_one, fourth)
    near_core_one = send(held_one, core)
    shifted_one, stats_one = run_kernel(
        norm_one_kernel,
        "norm_one",
        (after(inputs, held_one), region_col, params, grouping),
        (shape_of(shifted_shape, BF16), stats_shape),
        (sums_scratch,),
    )
    held_two, held_three = run_kernel(
        join_split_kernel,
        "join",
        (held_two, after(two, stats_one)),
        (shape_of((8, SECOND_ROWS, LANES), BF16), shape_of((8, PROJ_PACK, LANES), BF16)),
        room=8,
    )
    far_two = send(held_two, fourth)
    near_core_two = send(held_two, core)
    far_one = after(far_one, held_two)
    far_core_one = send(far_one, core)
    shifted_core_one = send(shifted_one, core)
    weight_shape = shape_of((WIDTH, TAPS), BF16)
    weight_one, conv_out, stats_two = run_kernel(
        conv_one_kernel,
        "conv_one",
        (
            me, after(shifted_one, held_two), region_col, params, grouping,
            held_one, far_one, near_core_one, far_core_one,
        ),
        (weight_shape, shape_of(map_shape, F32), stats_shape),
        (sums_scratch,),
        blocks=(32, CONV_PACK, LANES),
    )
    far_three = send(after(held_three, conv_out), fourth)
    near_core_three = send(held_three, core)
    far_two = after(far_two, conv_out)
    far_core_two = send(far_two, core)
    weight_two, film_weight, hidden_two, shifted_two, residual, attend_in, stats_three, film = run_kernel(
        conv_two_kernel,
        "conv_two",
        (
            me, conv_out, stats_two, inputs, embedding, film_bias, region_col,
            params, grouping, held_two, far_two, near_core_two, far_core_two,
        ),
        (
            weight_shape,
            shape_of((EMBED, 2 * WIDTH), BF16),
            shape_of(map_shape, BF16),
            shape_of(shifted_shape, BF16),
            shape_of(map_shape, F32),
            shape_of(map_shape, BF16),
            stats_shape,
            shape_of((MAPS, 2 * WIDTH), F32),
        ),
        (sums_scratch,),
        blocks=(32, SECOND_ROWS, LANES),
    )
    far_three = after(far_three, attend_in)
    far_core_three = send(far_three, core)
    proj_shape = shape_of((8, PROJ_PACK, LANES), BF16)
    output, grad_attend, column_sums, sums_three, *proj_terms = run_kernel(
        attend_kernel,
        "attend",
        (
            me, attend_in, qkv_bias, region_col, region_row, cotangent, residual, stats_three, params,
            held_three, far_three, near_core_three, far_core_three,
        ),
        (shape_of(map_shape, BF16), shape_of(map_shape, F32), shape_of((1, SLOTS), F32), stats_shape)
        + (proj_shape,) * 4,
        (
            pltpu.VMEM((WIDTH, SLOTS), BF16),
            pltpu.VMEM((WIDTH, HEADS * LANES), BF16),
            pltpu.VMEM((PIXELS, SLOTS), BF16),
            pltpu.VMEM((MAPS * PIXELS, SLOTS), BF16),
            pltpu.VMEM((MAPS * PIXELS, HEADS * LANES), BF16),
            pltpu.VMEM((32, PROJ_PACK, LANES), BF16),
        ),
        blocks=(32, PROJ_PACK, LANES),
        terms=4,
    )
    near_proj, far_proj, near_came, far_came = proj_terms
    near_came, far_came = send(near_came, core), send(far_came, core)
    hidden_core_two = send(after(hidden_two, output), core)
    turned_shape = shape_of((2 * HEAD_DIM, MAPS * PIXELS), BF16)
    grad_residual, grad_conv_two, kept, sent, small_three = run_kernel(
        back_three_kernel,
        "back_three",
        (
            me, grad_attend, sums_three, region_col, cotangent, residual, stats_three, params, grouping,
        ),
        (shape_of(map_shape, F32), shape_of(map_shape, BF16), turned_shape, turned_shape, small_shape),
    )
    came = send(after(sent, near_came, far_came, hidden_core_two), core)
    total_shape = (3, 2 * HEAD_DIM, 3 * WIDTH)
    grads_scratch = pltpu.VMEM(total_shape, F32)
    (begun,) = run_kernel(
        own_grads_kernel, "own_grads", (kept, shifted_two), (shape_of(total_shape, F32),)
    )
    grads_rows = CONV_PACK + PROJ_PACK
    near_two, far_two = run_kernel(
        grads_two_kernel,
        "weight_grads_two",
        (me, after(came, begun), hidden_core_two, begun, near_proj, far_proj, near_came, far_came),
        (shape_of((8, grads_rows, LANES), BF16),) * 2,
        (
            grads_scratch,
            pltpu.VMEM(shifted_shape, BF16),
            pltpu.VMEM((16, grads_rows, LANES), BF16),
        ),
        terms=2,
    )
    two = send(far_two, fourth)
    back_scratch = (
        pltpu.VMEM((3, 3 * WIDTH, WIDTH), BF16),
        pltpu.VMEM(shifted_shape, BF16),
        pltpu.VMEM(map_shape, F32),
        sums_scratch,
    )
    grad_conv_one, kept, sent, grad_film, small_two = run_kernel(
        back_two_kernel,
        "back_two",
        (
            me, after(grad_conv_two, near_two, shifted_core_one), weight_two, conv_out, stats_two, film,
            region_col, params, grouping,
        ),
        (
            shape_of(map_shape, BF16),
            turned_shape,
            turned_shape,
            shape_of((MAPS, 2 * WIDTH), F32),
            small_shape,
        ),
        back_scratch,
    )
    came = send(sent, core)
    (begun,) = run_kernel(
        own_grads_kernel, "own_grads", (kept, shifted_one), (shape_of(total_shape, F32),)
    )
    (grad_embedding,) = run_kernel(
        back_film_kernel,
        "back_film",
        (embedding, film_weight, after(grad_film, begun)),
        (shape_of((MAPS, EMBED), F32),),
    )
    far_two, near_two = add_split(near_two, after(two, grad_embedding))
    two = send(far_two, third)
    near_one, far_one = run_kernel(
        grads_one_kernel,
        "weight_grads_one",
        (me, after(came, far_two), shifted_core_one, begun),
        (shape_of((8, CONV_PACK, LANES), BF16),) * 2,
        (grads_scratch, pltpu.VMEM((16, CONV_PACK, LANES), BF16)),
        terms=2,
    )
    one = send(far_one, fourth)
    grad_inputs, small_one = run_kernel(
        back_one_kernel,
        "back_one",
        (
            after(grad_conv_one, near_one), weight_one, inputs, stats_one, grad_residual,
            region_col, params, grouping,
        ),
        (shape_of(map_shape, BF16), small_shape),
        back_scratch,
    )
    far_two, near_two = add_split(near_two, after(two, small_one))
    two = send(far_two, second)

    def message(count):
        return (shape_of((SUM_ROWS + 2 * MAPS * count, 2 * WIDTH), BF16),)

    def next_message(parts, count):
        return run_kernel(next_message_kernel, "next_message", parts, message(count), room=8)[0]

    (rows,) = run_kernel(
        first_message_kernel,
        "first_message",
        (after(small_one, far_two), small_two, small_three, column_sums, grad_film, embedding),
        message(1),
        room=8,
    )
    came = send(rows, second)
    far_one, near_one = add_split(near_one, after(one, rows))
    one = send(far_one, third)
    rows = next_message((rows, after(came, far_one)), 2)
    came = send(rows, first)
    far_two, near_two = add_split(near_two, after(two, rows))
    two = send(far_two, first)
    rows = next_message((rows, after(came, far_two)), 4)
    came = send(rows, third)
    far_one, near_one = add_split(near_one, after(one, rows))
    one = send(far_one, second)
    rows = next_message((rows, after(came, far_one)), 8)
    came = send(rows, fourth)
    conv_grad_shape = shape_of((HEAD_DIM, CONV_ROWS), F32)
    grad_weight_two, grad_qkv_weight, grad_proj_weight = run_kernel(
        finish_two_kernel,
        "finish_two",
        (near_two, after(two, rows)),
        (conv_grad_shape, shape_of((48, 3 * HEAD_DIM), F32), shape_of((48, HEAD_DIM), F32)),
        room=8,
    )
    far_one, near_one = add_split(near_one, after(one, grad_weight_two))
    one = send(far_one, first)
    rows = next_message((rows, after(came, far_one)), 16)
    came = (rows, send(rows, core))
    vector = shape_of((WIDTH,), F32)
    grad_emb_weight, *vectors = run_kernel(
        finish_rows_kernel,
        "finish_rows",
        (me, *came),
        (shape_of((EMBED // BLOCK_GROUPS, 2 * WIDTH // HEADS), F32),)
        + (vector,) * 11
        + (shape_of((2 * WIDTH,), F32),),
        room=8,
    )
    (grad_weight_one,) = run_kernel(
        finish_one_kernel,
        "finish_one",
        (near_one, after(one, grad_emb_weight)),
        (conv_grad_shape,),
        room=8,
    )
    finals = [
        inner_scatter(grad, sizes)
        for grad in (
            grad_weight_one.T, grad_weight_two.T, grad_emb_weight, grad_qkv_weight, grad_proj_weight,
        )
    ]
    return (
        output,
        grad_inputs,
        grad_embedding,
        *finals,
        vectors[4],
        vectors[8],
        vectors[11],
        vectors[9],
        vectors[10],
        vectors[7],
        vectors[0],
        vectors[1],
        vectors[2],
        vectors[3],
        vectors[5],
        vectors[6],
    )


def solution(mesh):
    own = P(AXES)
    split = P("dp", "head")
    whole = P()
    in_specs = (own, own, P("dp"), own, split, whole, split, whole, split, whole, split) + (
        (whole, whole, split) + (whole,) * 7
    )
    out_specs = (own,) * 3 + (split,) * 5 + (whole,) * 12
    return jax.shard_map(
        per_device, mesh=mesh, in_specs=in_specs, out_specs=out_specs, check_vma=False
    )
```

```python
import functools

import jax
import jax.numpy as jnp
from jax import lax
from jax.experimental import pallas as pl
from jax.experimental.pallas import tpu as pltpu
from jax.sharding import PartitionSpec as P

WIDTH = 384
EMBED = 512
HEADS = 4
HEAD_DIM = 96
GROUP_SIZE = 12
SIDE = 16
PIXELS = 256
MAPS = 4
LANES = 128
TAPS = 9 * WIDTH
PADDED = PIXELS + 2 * SIDE
SLOTS = 3 * HEADS * LANES
FACTOR = HEAD_DIM ** (-0.5)
EPS = 1e-05
AXES = ("dp", "head")

BLOCK_GROUPS = 8
CONV_ROWS = TAPS // BLOCK_GROUPS
CONV_PACK = 336
EMB_PACK = 96
SUM_ROWS = 16
PROJ_PACK = 144
SECOND_ROWS = CONV_PACK + EMB_PACK
ROOM = 28
FLOPS_PER_US = 1.5e9
DURATIONS = {
    "norm_one": 2.4,
    "conv_one": 6,
    "conv_two": 8,
    "attend": 15,
    "back_three": 2.5,
    "own_grads": 3.5,
    "weight_grads_two": 4.5,
    "back_two": 7.5,
    "back_film": 1.1,
    "weight_grads_one": 4,
    "back_one": 7,
}

F32 = jnp.float32
BF16 = jnp.bfloat16
BIAS_ONE, BIAS_TWO, GAIN_ONE, SHIFT_ONE, GAIN_TWO, SHIFT_TWO, GAIN_THREE, SHIFT_THREE, PROJ_BIAS = (
    range(9)
)

VMEM = pl.BlockSpec(memory_space=pltpu.VMEM)
SMEM = pl.BlockSpec(memory_space=pltpu.SMEM)


def after(value, *others):
    return lax.optimization_barrier((value, *others))[0]


class Parts:
    def __init__(self, parts, ref):
        self.parts, self.ref = parts, ref

    def collect(self):
        first = self.ref.shape[1] - self.parts[0].shape[1]
        for index, part in enumerate(self.parts):
            self.ref[8 * index : 8 * index + 8, first:] = part[...]


def run_kernel(kernel, name, operands, outs, scratch=(), room=ROOM, blocks=None, terms=0):
    operands = tuple(operands)
    plain = len(operands) - (blocks[0] // 8 if blocks else 0)
    direct = len(outs) - terms
    in_specs = [SMEM if value.dtype == jnp.int32 and value.ndim == 1 else VMEM for value in operands]
    scratch = list(scratch)
    own = len(scratch)
    if blocks:
        scratch.append(pltpu.VMEM(blocks, BF16))

    def body(*refs):
        ins = refs[: len(operands)]
        results = refs[len(operands) : len(operands) + len(outs)]
        given = refs[len(operands) + len(outs) :]
        held = [Parts(ins[plain:], given[own])] if blocks else []
        kernel(*ins[:plain], *held, *results[:direct], *given[:own])
        for k in range(terms):
            results[direct + k][...] = given[own - 1][8 * k : 8 * k + 8]

    return pl.pallas_call(
        body,
        out_shape=list(outs),
        in_specs=in_specs,
        out_specs=[VMEM] * len(outs),
        scratch_shapes=scratch,
        compiler_params=pltpu.CompilerParams(vmem_limit_bytes=room * 2**20),
        cost_estimate=pl.CostEstimate(
            flops=int(FLOPS_PER_US * DURATIONS.get(name, 0.5)), bytes_accessed=0, transcendentals=0
        ),
        name=name,
    )(*operands)


def shape_of(shape, dtype):
    return jax.ShapeDtypeStruct(shape, dtype)


def dot(left, right, dims=(1, 0)):
    return lax.dot_general(
        left, right, (((dims[0],), (dims[1],)), ((), ())), preferred_element_type=F32
    )


def group_total(rows, grouping):
    return lax.dot_general(
        rows,
        grouping,
        (((1,), (0,)), ((), ())),
        preferred_element_type=F32,
        precision=lax.Precision.HIGHEST,
    )


def sigmoid(values):
    return 1.0 / (1.0 + jnp.exp(-values))


def valid_of(region_ref, index):
    return (region_ref[index] > 0).astype(F32)


def cells_of(region_ref):
    counts = [jnp.sum(valid_of(region_ref, m), axis=0, keepdims=True) for m in range(MAPS)]
    return jnp.concatenate(counts, axis=0) * float(GROUP_SIZE)


def column_sum(values):
    return jnp.sum(values, axis=0, keepdims=True)


def store_shifted(target_ref, index, values):
    column = lax.broadcasted_iota(jnp.int32, (PIXELS, 1), 0) % SIDE
    left = jnp.where(column == 0, 0.0, pltpu.roll(values, 1, 0))
    right = jnp.where(column == SIDE - 1, 0.0, pltpu.roll(values, PIXELS - 1, 0))
    border = jnp.zeros((SIDE, 3 * WIDTH), BF16)
    target_ref[index, 0:SIDE, :] = border
    target_ref[index, SIDE + PIXELS : PADDED, :] = border
    for position, part in enumerate((left, values, right)):
        target_ref[index, SIDE : SIDE + PIXELS, position * WIDTH : (position + 1) * WIDTH] = (
            part.astype(BF16)
        )


def convolve(shifted_ref, index, weight_ref):
    total = None
    for tap_row in range(3):
        part = dot(
            shifted_ref[index, tap_row * SIDE : tap_row * SIDE + PIXELS, :],
            weight_ref[:, tap_row * 3 * WIDTH : (tap_row + 1) * 3 * WIDTH],
            (1, 1),
        )
        total = part if total is None else total + part
    return total


def flip_weight(flipped_ref, weight_ref):
    for tap_row in range(3):
        for tap_col in range(3):
            start = (3 * (2 - tap_row) + 2 - tap_col) * WIDTH
            flipped_ref[tap_row, tap_col * WIDTH : (tap_col + 1) * WIDTH, :] = weight_ref[
                :, start : start + WIDTH
            ]


def convolve_back(shifted_ref, index, flipped_ref):
    total = None
    for tap_row in range(3):
        part = dot(
            shifted_ref[index, tap_row * SIDE : tap_row * SIDE + PIXELS, :],
            flipped_ref[tap_row],
        )
        total = part if total is None else total + part
    return total


def pack_conv(shard):
    tail = shard[:, 3 * LANES :]
    parts = [shard[:, LANES * k : LANES * (k + 1)] for k in range(3)]
    parts.append(jnp.concatenate([tail[:48], tail[48:], jnp.zeros((48, 32), shard.dtype)], axis=1))
    return jnp.concatenate(parts, axis=0)


def pack_proj(qkv, proj):
    wide = jnp.concatenate([qkv, proj], axis=1)
    return jnp.concatenate([wide[:, LANES * k : LANES * (k + 1)] for k in range(3)], axis=0)


def pack_emb(shard):
    side = shard[:, LANES:]
    half = side.shape[0] // 2
    return jnp.concatenate(
        [shard[:, :LANES], jnp.concatenate([side[:half], side[half:]], axis=1)], axis=0
    )


def prepare_kernel(
    me_ref, region, bias_one, bias_two, gain_one, shift_one, gain_two, shift_two, gain_three,
    shift_three, proj_bias, q_bias, v_bias, emb_bias,
    params, qkv_bias, film_bias, region_col, region_row, grouping,
):
    vectors = (
        bias_one, bias_two, gain_one, shift_one, gain_two, shift_two, gain_three, shift_three,
        proj_bias,
    )
    for row, vector in enumerate(vectors):
        params[row : row + 1, :] = vector[...].reshape(1, WIDTH)
    queries, values = q_bias[...].reshape(1, WIDTH), v_bias[...].reshape(1, WIDTH)
    gap = jnp.zeros((1, LANES - HEAD_DIM), F32)
    for head in range(HEADS):
        part = slice(HEAD_DIM * head, HEAD_DIM * (head + 1))
        base = 3 * LANES * head
        qkv_bias[:, base : base + LANES] = jnp.concatenate([queries[:, part], gap], axis=1)
        qkv_bias[:, base + LANES : base + 2 * LANES] = jnp.zeros((1, LANES), F32)
        qkv_bias[:, base + 2 * LANES : base + 3 * LANES] = jnp.concatenate(
            [values[:, part], gap], axis=1
        )
    film_bias[...] = emb_bias[...].reshape(1, 2 * WIDTH)
    rows = region[...].astype(F32)
    home = me_ref[1] * MAPS
    turned = jnp.concatenate([rows, jnp.zeros((LANES - rows.shape[0], PIXELS), F32)], axis=0).T
    lane = lax.broadcasted_iota(jnp.int32, (PIXELS, LANES), 1)
    for m in range(MAPS):
        region_row[m] = region[pl.ds(home + m, 1)]
        region_col[m] = jnp.sum(
            jnp.where(lane == home + m, turned, 0.0), axis=1, keepdims=True
        ).astype(jnp.int32)
    down = lax.broadcasted_iota(jnp.int32, (WIDTH, WIDTH), 0)
    along = lax.broadcasted_iota(jnp.int32, (WIDTH, WIDTH), 1)
    grouping[...] = (down // GROUP_SIZE == along // GROUP_SIZE).astype(F32)


def pack_kernel(conv_one, conv_two, emb, qkv, proj, first, second):
    first[0] = pack_conv(conv_one[...].astype(F32)).astype(BF16)
    second[0, 0:CONV_PACK] = pack_conv(conv_two[...].astype(F32)).astype(BF16)
    second[0, CONV_PACK:SECOND_ROWS] = pack_emb(emb[...].astype(F32)).astype(BF16)
    second[0, SECOND_ROWS:] = pack_proj(qkv[...].astype(F32), proj[...].astype(F32)).astype(BF16)


def place_of(group, head, me_ref):
    far_group = group ^ me_ref[0]
    far_head = head ^ me_ref[1]
    bits = [far_group // 4, (far_group // 2) & 1, far_head // 2, far_group & 1]
    if head % 2 == 1:
        bits[2:] = bits[:1:-1]
    place = 16 * (far_head & 1)
    for position, bit in enumerate(bits):
        place = place + (1 << position) * bit
    return place


def place_of_own(group, over_x, me_ref):
    far_group = group ^ me_ref[0]
    far_x = over_x ^ (me_ref[1] // 2)
    far_y = far_group & 1
    odd = (me_ref[1] & 1) == 1
    place = far_group // 4 + 2 * ((far_group // 2) & 1)
    return place + jnp.where(odd, 4 * far_y + 8 * far_x, 4 * far_x + 8 * far_y)


def turn_halves(values, index, me_ref, kept, sent):
    odd = (me_ref[1] & 1) == 1
    turned = values.T
    place = pl.ds(index * PIXELS, PIXELS)
    for over_x in range(2):
        low = turned[2 * HEAD_DIM * over_x : 2 * HEAD_DIM * over_x + HEAD_DIM]
        high = turned[2 * HEAD_DIM * over_x + HEAD_DIM : 2 * HEAD_DIM * (over_x + 1)]
        rows = slice(HEAD_DIM * over_x, HEAD_DIM * (over_x + 1))
        kept[rows, place] = jnp.where(odd, high, low).astype(BF16)
        sent[rows, place] = jnp.where(odd, low, high).astype(BF16)


def repeat(count, step):
    def body(index, carry):
        step(index)
        return carry

    lax.fori_loop(0, count, body, 0)


def rows_of(index, size):
    return pl.ds(pl.multiple_of(index * size, 16), size)


def unpack_conv(blocks, me_ref, weight_ref):
    for head in range(HEADS):
        pieces = []
        for group in range(BLOCK_GROUPS):
            block = blocks[place_of(group, head, me_ref), 0:CONV_PACK]
            pieces += [block[HEAD_DIM * k : HEAD_DIM * (k + 1)] for k in range(3)]
            pieces.append(jnp.concatenate([block[288:, :48], block[288:, 48:96]], axis=0))
        weight_ref[HEAD_DIM * head : HEAD_DIM * (head + 1), :] = jnp.concatenate(
            pieces, axis=1
        )


def unpack_emb(blocks, me_ref, emb_ref):
    for group in range(BLOCK_GROUPS):
        embs = []
        for head in range(HEADS):
            emb = blocks[place_of(group, head, me_ref), CONV_PACK:].astype(F32)
            side = jnp.concatenate([emb[64:96, :64], emb[64:96, 64:]], axis=0)
            embs.append(jnp.concatenate([emb[:64], side], axis=1))
        emb_ref[64 * group : 64 * group + 64] = jnp.concatenate(embs, axis=1).astype(BF16)


def unpack_proj(blocks, me_ref, qkv_ref, proj_ref):
    gap = jnp.zeros((48, LANES - HEAD_DIM), F32)
    for group in range(BLOCK_GROUPS):
        rows = slice(48 * group, 48 * group + 48)
        for head in range(HEADS):
            block = blocks[place_of(group, head, me_ref)].astype(F32)
            wide = jnp.concatenate([block[48 * k : 48 * k + 48] for k in range(3)], axis=1)
            for part in range(3):
                piece = wide[:, HEAD_DIM * part : HEAD_DIM * (part + 1)]
                slot = (3 * head + part) * LANES
                qkv_ref[rows, slot : slot + LANES] = jnp.concatenate([piece, gap], axis=1).astype(
                    BF16
                )
            proj_ref[rows, LANES * head : LANES * (head + 1)] = jnp.concatenate(
                [wide[:, 3 * HEAD_DIM :], gap], axis=1
            ).astype(BF16)


def norm_stats(sums, squares, cells, grouping):
    totals = group_total(jnp.concatenate([sums, squares], axis=0), grouping)
    mean = totals[:MAPS] / cells
    inverse = lax.rsqrt(totals[MAPS:] / cells - mean * mean + EPS)
    return jnp.concatenate([mean, inverse], axis=0)


def norm_one_kernel(inputs, region, params, grouping, shifted, stats, sums):
    def add_map(m):
        values = inputs[m].astype(F32)
        masked = values * valid_of(region, m)
        sums[pl.ds(m, 1)] = column_sum(masked)
        sums[pl.ds(MAPS + m, 1)] = column_sum(masked * values)

    def one_map(m):
        hat = (inputs[m].astype(F32) - stats[pl.ds(m, 1)]) * stats[pl.ds(MAPS + m, 1)]
        normed = hat * params[GAIN_ONE : GAIN_ONE + 1] + params[SHIFT_ONE : SHIFT_ONE + 1]
        store_shifted(shifted, m, normed * sigmoid(normed) * valid_of(region, m))

    repeat(MAPS, add_map)
    stats[...] = norm_stats(sums[:MAPS], sums[MAPS:], cells_of(region), grouping[...])
    repeat(MAPS, one_map)


def conv_one_kernel(
    me_ref, shifted, region, params, grouping, blocks, weight, result, stats, sums
):
    blocks.collect()
    unpack_conv(blocks.ref, me_ref, weight)

    def one_map(m, carry):
        value = convolve(shifted, m, weight) + params[BIAS_ONE : BIAS_ONE + 1]
        result[m] = value
        masked = value * valid_of(region, m)
        sums[pl.ds(m, 1)] = column_sum(masked)
        sums[pl.ds(MAPS + m, 1)] = column_sum(masked * value)
        return carry

    lax.fori_loop(0, MAPS, one_map, 0, unroll=True)
    stats[...] = norm_stats(sums[:MAPS], sums[MAPS:], cells_of(region), grouping[...])


def modulate(value, stats, film, params, m):
    hat = (value - stats[pl.ds(m, 1)]) * stats[pl.ds(MAPS + m, 1)]
    modulated = hat * params[GAIN_TWO : GAIN_TWO + 1] + params[SHIFT_TWO : SHIFT_TWO + 1]
    scale = 1.0 + film[pl.ds(m, 1), :WIDTH]
    return hat, modulated, scale, modulated * scale + film[pl.ds(m, 1), WIDTH:]


def conv_two_kernel(
    me_ref, conv_out, stats_two, inputs, embedding, emb_bias, region, params, grouping, blocks,
    weight, emb_weight, hidden, shifted, residual, attend_in, stats, film,
    sums,
):
    blocks.collect()
    unpack_conv(blocks.ref, me_ref, weight)
    unpack_emb(blocks.ref, me_ref, emb_weight)
    embed = embedding[...].astype(F32)
    film[...] = dot((embed * sigmoid(embed)).astype(BF16), emb_weight[...]) + emb_bias[...]

    def one_map(m, carry):
        _, _, _, normed = modulate(conv_out[m], stats_two, film, params, m)
        valid = valid_of(region, m)
        active = normed * sigmoid(normed) * valid
        hidden[m] = active.astype(BF16)
        store_shifted(shifted, m, active)
        value = (
            inputs[m].astype(F32)
            + convolve(shifted, m, weight)
            + params[BIAS_TWO : BIAS_TWO + 1]
        )
        residual[m] = value
        sums[pl.ds(m, 1)] = column_sum(value * valid)
        sums[pl.ds(MAPS + m, 1)] = column_sum(value * value * valid)
        return carry

    lax.fori_loop(0, MAPS, one_map, 0, unroll=True)
    stats[...] = norm_stats(sums[:MAPS], sums[MAPS:], cells_of(region), grouping[...])
    for m in range(MAPS):
        hat = (residual[m] - stats[m : m + 1]) * stats[MAPS + m : MAPS + m + 1]
        attend_in[m] = (
            hat * params[GAIN_THREE : GAIN_THREE + 1] + params[SHIFT_THREE : SHIFT_THREE + 1]
        ).astype(BF16)


def norm_back(grad, hat, along, cross, inverse, valid, cells):
    return inverse * (grad - valid * (along + cross * hat) / cells)


def attend_kernel(
    me_ref, attend_in, qkv_bias, region, region_row, cotangent, residual, stats, params, blocks,
    output, grad_attend, bias_sums, sums,
    qkv_weight, proj_weight, columns, grad_columns, attended, terms,
):
    blocks.collect()
    unpack_proj(blocks.ref, me_ref, qkv_weight, proj_weight)

    def one_map(m, carry):
        rows = pl.ds(pl.multiple_of(m * PIXELS, PIXELS), PIXELS)
        columns[...] = (dot(attend_in[m], qkv_weight[...]) + qkv_bias[...]).astype(BF16)
        grad_attended = dot(cotangent[m], proj_weight[...]).astype(BF16)
        key_region = region[m]
        query_region = region_row[m]
        allowed = (key_region > 0) & ((key_region == query_region) | (query_region == 0))
        for head in range(HEADS):
            base = 3 * LANES * head
            queries = columns[:, base : base + LANES]
            keys = columns[:, base + LANES : base + 2 * LANES]
            values = columns[:, base + 2 * LANES : base + 3 * LANES]
            grad_out = grad_attended[:, LANES * head : LANES * (head + 1)]
            logits = jnp.where(allowed, dot(keys, queries, (1, 1)) * FACTOR, -1e30)
            raised = jnp.exp(logits - jnp.max(logits, axis=0, keepdims=True))
            weights = raised * (1.0 / jnp.sum(raised, axis=0, keepdims=True))
            weights_low = weights.astype(BF16)
            attended[rows, LANES * head : LANES * (head + 1)] = dot(
                weights_low, values, (0, 0)
            ).astype(BF16)
            grad_weights = dot(values, grad_out, (1, 1))
            inner = jnp.sum(grad_weights * weights, axis=0, keepdims=True)
            grad_logits = (weights * (grad_weights - inner)).astype(BF16)
            grad_columns[rows, base : base + LANES] = (
                dot(grad_logits, keys, (0, 0)) * FACTOR
            ).astype(BF16)
            grad_columns[rows, base + LANES : base + 2 * LANES] = (
                dot(grad_logits, queries) * FACTOR
            ).astype(BF16)
            grad_columns[rows, base + 2 * LANES : base + 3 * LANES] = dot(
                weights_low, grad_out
            ).astype(BF16)
        output[m] = (
            residual[m]
            + dot(attended[rows, :], proj_weight[...], (1, 1))
            + params[PROJ_BIAS : PROJ_BIAS + 1]
        ).astype(BF16)
        grad = dot(grad_columns[rows, :], qkv_weight[...], (1, 1))
        grad_attend[m] = grad
        hat = (residual[m] - stats[pl.ds(m, 1)]) * stats[pl.ds(MAPS + m, 1)]
        sums[pl.ds(m, 1)] = column_sum(grad)
        sums[pl.ds(MAPS + m, 1)] = column_sum(grad * hat)
        return carry

    lax.fori_loop(0, MAPS, one_map, 0)
    bias_sums[...] = column_sum(grad_columns[...].astype(F32))
    grad_qkv, grad_proj = None, None
    for m in range(MAPS):
        rows = slice(m * PIXELS, (m + 1) * PIXELS)
        qkv_part = dot(attend_in[m], grad_columns[rows, :], (0, 0))
        proj_part = dot(cotangent[m], attended[rows, :], (0, 0))
        grad_qkv = qkv_part if m == 0 else grad_qkv + qkv_part
        grad_proj = proj_part if m == 0 else grad_proj + proj_part
    for group in range(BLOCK_GROUPS):
        rows = slice(48 * group, 48 * group + 48)
        for head in range(HEADS):
            pieces = [
                grad_qkv[rows, slot * LANES : slot * LANES + HEAD_DIM]
                for slot in range(3 * head, 3 * head + 3)
            ]
            pieces.append(grad_proj[rows, head * LANES : head * LANES + HEAD_DIM])
            wide = jnp.concatenate(pieces, axis=1)
            terms[place_of(group, head, me_ref)] = jnp.concatenate(
                [wide[:, LANES * part : LANES * (part + 1)] for part in range(3)], axis=0
            ).astype(BF16)


def back_three_kernel(
    me_ref, grad_attend, sums, region, cotangent, residual, stats, params, grouping,
    grad_residual, grad_conv, kept, sent, small_sums,
):
    gain = params[GAIN_THREE : GAIN_THREE + 1]
    totals = group_total(sums[...] * gain, grouping[...])
    cells = cells_of(region)
    small_sums[...] = jnp.zeros_like(small_sums)
    small_sums[0:1] = column_sum(sums[MAPS:])
    small_sums[1:2] = column_sum(sums[:MAPS])
    top_sum = jnp.zeros((1, WIDTH), F32)
    low_sum = jnp.zeros((1, WIDTH), F32)
    for m in range(MAPS):
        inverse = stats[MAPS + m : MAPS + m + 1]
        hat = (residual[m] - stats[m : m + 1]) * inverse
        top = cotangent[m].astype(F32)
        grad = top + norm_back(
            grad_attend[m] * gain,
            hat,
            totals[m : m + 1],
            totals[MAPS + m : MAPS + m + 1],
            inverse,
            valid_of(region, m),
            cells[m : m + 1],
        )
        grad_residual[m] = grad
        low = grad.astype(BF16)
        grad_conv[m] = low
        turn_halves(low.astype(F32), m, me_ref, kept, sent)
        top_sum = top_sum + column_sum(top)
        low_sum = low_sum + column_sum(low.astype(F32))
    small_sums[2:3] = top_sum
    small_sums[3:4] = low_sum


def back_two_kernel(
    me_ref, grad_conv, weight, conv_out, stats, film, region, params, grouping,
    grad_low, kept, sent, grad_film, small_sums,
    flipped, shifted, grad_normed, sums,
):
    flip_weight(flipped, weight)

    def one_map(m, carry):
        store_shifted(shifted, m, grad_conv[m].astype(F32))
        hat, modulated, scale, normed = modulate(conv_out[m], stats, film, params, m)
        logistic = sigmoid(normed)
        slope = logistic * (1.0 + normed * (1.0 - logistic)) * valid_of(region, m)
        grad = convolve_back(shifted, m, flipped) * slope
        grad_film[pl.ds(m, 1), :WIDTH] = column_sum(grad * modulated)
        grad_film[pl.ds(m, 1), WIDTH:] = column_sum(grad)
        scaled = grad * scale
        grad_normed[m] = scaled
        sums[pl.ds(m, 1)] = column_sum(scaled)
        sums[pl.ds(MAPS + m, 1)] = column_sum(scaled * hat)
        return carry

    lax.fori_loop(0, MAPS, one_map, 0)
    gain = params[GAIN_TWO : GAIN_TWO + 1]
    totals = group_total(sums[...] * gain, grouping[...])
    cells = cells_of(region)
    small_sums[...] = jnp.zeros_like(small_sums)
    small_sums[0:1] = column_sum(sums[MAPS:])
    small_sums[1:2] = column_sum(sums[:MAPS])
    low_sum = jnp.zeros((1, WIDTH), F32)
    for m in range(MAPS):
        inverse = stats[MAPS + m : MAPS + m + 1]
        low = norm_back(
            grad_normed[m] * gain,
            (conv_out[m] - stats[m : m + 1]) * inverse,
            totals[m : m + 1],
            totals[MAPS + m : MAPS + m + 1],
            inverse,
            valid_of(region, m),
            cells[m : m + 1],
        ).astype(BF16)
        grad_low[m] = low
        turn_halves(low.astype(F32), m, me_ref, kept, sent)
        low_sum = low_sum + column_sum(low.astype(F32))
    small_sums[2:3] = low_sum


def back_film_kernel(embedding, emb_weight, grad_film, grad_embed):
    embed = embedding[...].astype(F32)
    logistic = sigmoid(embed)
    film_high = grad_film[...].astype(BF16)
    film_rest = (grad_film[...] - film_high.astype(F32)).astype(BF16)
    grad_embed[...] = (
        dot(film_high, emb_weight[...], (1, 1)) + dot(film_rest, emb_weight[...], (1, 1))
    ) * (logistic * (1.0 + embed * (1.0 - logistic)))


def back_one_kernel(
    grad_conv, weight, inputs, stats, grad_residual, region, params, grouping,
    grad_inputs, small_sums,
    flipped, shifted, grad_normed, sums,
):
    flip_weight(flipped, weight)
    gain = params[GAIN_ONE : GAIN_ONE + 1]

    def one_map(m, carry):
        store_shifted(shifted, m, grad_conv[m].astype(F32))
        hat = (inputs[m].astype(F32) - stats[pl.ds(m, 1)]) * stats[pl.ds(MAPS + m, 1)]
        normed = hat * gain + params[SHIFT_ONE : SHIFT_ONE + 1]
        logistic = sigmoid(normed)
        slope = logistic * (1.0 + normed * (1.0 - logistic)) * valid_of(region, m)
        grad = convolve_back(shifted, m, flipped) * slope
        grad_normed[m] = grad
        sums[pl.ds(m, 1)] = column_sum(grad)
        sums[pl.ds(MAPS + m, 1)] = column_sum(grad * hat)
        return carry

    lax.fori_loop(0, MAPS, one_map, 0)
    totals = group_total(sums[...] * gain, grouping[...])
    cells = cells_of(region)
    small_sums[...] = jnp.zeros_like(small_sums)
    small_sums[0:1] = column_sum(sums[MAPS:])
    small_sums[1:2] = column_sum(sums[:MAPS])
    for m in range(MAPS):
        inverse = stats[MAPS + m : MAPS + m + 1]
        grad_inputs[m] = (
            grad_residual[m]
            + norm_back(
                grad_normed[m] * gain,
                (inputs[m].astype(F32) - stats[m : m + 1]) * inverse,
                totals[m : m + 1],
                totals[MAPS + m : MAPS + m + 1],
                inverse,
                valid_of(region, m),
                cells[m : m + 1],
            )
        ).astype(BF16)


def conv_weight_grads(shifted, turned, total, begun=None):
    def one_row(tap_row, carry):
        rows = pl.ds(pl.multiple_of(tap_row * SIDE, SIDE), PIXELS)
        part = None if begun is None else begun[tap_row]
        for m in range(MAPS):
            term = dot(turned[:, m * PIXELS : (m + 1) * PIXELS], shifted[m, rows, :])
            part = term if part is None else part + term
        total[tap_row] = part
        return carry

    lax.fori_loop(0, 3, one_row, 0)


def own_grads_kernel(kept, shifted, total):
    conv_weight_grads(shifted, kept, total)


def pack_conv_grads(total, me_ref, blocks):
    def one_half(over_x):
        rows = rows_of(over_x, HEAD_DIM)
        for group in range(BLOCK_GROUPS):
            start, stop = group * CONV_ROWS, (group + 1) * CONV_ROWS
            values = []
            for tap_row in range(3):
                low, high = tap_row * 3 * WIDTH, (tap_row + 1) * 3 * WIDTH
                if max(low, start) < min(high, stop):
                    values.append(total[tap_row, rows, max(low, start) - low : min(high, stop) - low])
            block = values[0] if len(values) == 1 else jnp.concatenate(values, axis=1)
            place = place_of_own(group, over_x, me_ref)
            blocks[place, 0:CONV_PACK, :] = pack_conv(block.astype(BF16))

    repeat(2, one_half)


def grads_one_kernel(me_ref, came, shifted_core, begun, total, blocks):
    conv_weight_grads(shifted_core, came, total, begun)
    pack_conv_grads(total, me_ref, blocks)


def grads_two_kernel(
    me_ref, came, hidden_core, begun, near, far, near_came, far_came, total, shifted_core, blocks
):
    for m in range(MAPS):
        store_shifted(shifted_core, m, hidden_core[m].astype(F32))
    conv_weight_grads(shifted_core, came, total, begun)
    pack_conv_grads(total, me_ref, blocks)
    for index, (mine, other) in enumerate(((near, near_came), (far, far_came))):
        blocks[8 * index : 8 * index + 8, CONV_PACK:, :] = (
            mine[...].astype(F32) + other[...].astype(F32)
        ).astype(BF16)


def unpack_conv_grad(block, result):
    for part in range(3):
        result[:, LANES * part : LANES * (part + 1)] = block[HEAD_DIM * part : HEAD_DIM * (part + 1)]
    result[:, 3 * LANES :] = jnp.concatenate([block[288:336, :48], block[288:336, 48:96]], axis=0)


def first_message_kernel(small_one, small_two, small_three, column_sums, grad_film, embedding, message):
    pieces = [small_one[0:1], small_one[1:2], small_two[0:1], small_two[1:2], small_two[2:3]]
    pieces += [small_three[row : row + 1] for row in range(4)]
    for part in (0, 2):
        slots = [(3 * head + part) * LANES for head in range(HEADS)]
        pieces.append(
            jnp.concatenate([column_sums[:, slot : slot + HEAD_DIM] for slot in slots], axis=1)
        )
    film = column_sum(grad_film[...])
    pieces.append(jnp.zeros((1, WIDTH), F32))
    rows = [jnp.concatenate(pieces[k : k + 2], axis=1) for k in range(0, 12, 2)]
    sums = jnp.concatenate(rows + [film, jnp.zeros((1, 2 * WIDTH), F32)], axis=0)
    embed = embedding[...].astype(F32)
    low = (embed * sigmoid(embed)).astype(BF16).astype(F32)
    wide = jnp.concatenate([low, jnp.zeros((MAPS, 2 * WIDTH - EMBED), F32)], axis=1)
    store_sums(sums, message)
    message[SUM_ROWS:, :] = jnp.concatenate([grad_film[...], wide], axis=0).astype(BF16)


def store_sums(sums, message):
    high = sums.astype(BF16).astype(F32)
    message[0:SUM_ROWS, :] = jnp.concatenate([high, sums - high], axis=0).astype(BF16)


def added_sums(parts):
    half = SUM_ROWS // 2
    total = None
    for part in parts:
        both = part[0:SUM_ROWS, :].astype(F32)
        both = both[:half] + both[half:]
        total = both if total is None else total + both
    return total


def next_message_kernel(*refs):
    parts, message = refs[:-1], refs[-1]
    store_sums(added_sums(parts), message)
    count = parts[0].shape[0] - SUM_ROWS
    for index, part in enumerate(parts):
        start = SUM_ROWS + count * index
        message[start : start + count, :] = part[SUM_ROWS:, :]


def finish_one_kernel(mine, other, result):
    unpack_conv_grad(mine[0].astype(F32) + other[0].astype(F32), result)


def finish_rows_kernel(me_ref, *refs):
    parts, emb, vectors = refs[:2], refs[2], refs[3:]
    sums = added_sums(parts)
    for index, vector in enumerate(vectors[:11]):
        row, place = index // 2, (index % 2) * WIDTH
        vector[...] = sums[row, place : place + WIDTH]
    vectors[11][...] = sums[6]
    total = None
    for part in parts:
        for start in range(SUM_ROWS, part.shape[0], 2 * MAPS):
            films = part[start : start + MAPS, :].astype(F32)
            embeds = part[start + MAPS : start + 2 * MAPS, :EMBED].astype(F32)
            total = (films, embeds) if total is None else (
                jnp.concatenate([total[0], films], axis=0),
                jnp.concatenate([total[1], embeds], axis=0),
            )
    products = dot(total[1].astype(BF16), total[0].astype(BF16), (0, 0))
    rows, cols = emb.shape
    mine_rows = products[0:rows]
    for group in range(1, BLOCK_GROUPS):
        mine_rows = jnp.where(me_ref[0] == group, products[rows * group : rows * (group + 1)], mine_rows)
    mine_cols = mine_rows[:, 0:cols]
    for head in range(1, HEADS):
        mine_cols = jnp.where(me_ref[1] == head, mine_rows[:, cols * head : cols * (head + 1)], mine_cols)
    emb[...] = mine_cols


def finish_two_kernel(mine, other, result, qkv, proj):
    block = mine[0].astype(F32) + other[0].astype(F32)
    unpack_conv_grad(block, result)
    tiles = [block[CONV_PACK + 48 * k : CONV_PACK + 48 * k + 48] for k in range(3)]
    wide = jnp.concatenate(tiles, axis=1)
    qkv[...] = wide[:, : 3 * HEAD_DIM]
    proj[...] = wide[:, 3 * HEAD_DIM :]


def join_kernel(left, right, joined):
    count = left.shape[0]
    joined[:count] = left[...]
    joined[count:] = right[...]


def join_split_kernel(left, right, joined, joined_last):
    count = left.shape[0]
    for index, part in enumerate((left, right)):
        joined[count * index : count * index + count] = part[:, :SECOND_ROWS]
        joined_last[count * index : count * index + count] = part[:, SECOND_ROWS:]


def add_split_kernel(left, right, send, keep):
    half = keep.shape[0]
    send[...] = (left[half:].astype(F32) + right[half:].astype(F32)).astype(BF16)
    keep[...] = (left[:half].astype(F32) + right[:half].astype(F32)).astype(BF16)


def swap(values, masks, sizes):
    pairs = [(own, own ^ masks[own % 2]) for own in range(sizes[0] * sizes[1])]
    return lax.ppermute(values, AXES, pairs)


def stages_of(sizes):
    inner = sizes[0] // BLOCK_GROUPS
    group_bit = sizes[1] * inner
    over_x, over_y = 2, group_bit
    return ((4 * group_bit,) * 2, (2 * group_bit,) * 2, (over_x, over_y), (over_y, over_x))


def join(left, right):
    joined = shape_of((left.shape[0] + right.shape[0],) + left.shape[1:], left.dtype)
    return run_kernel(join_kernel, "join", (left, right), (joined,), room=8)[0]


def add_split(left, right):
    half = shape_of((left.shape[0] // 2,) + left.shape[1:], BF16)
    return run_kernel(add_split_kernel, "add_split", (left, right), (half, half), room=8)


def inner_groups(sizes):
    inner = sizes[0] // BLOCK_GROUPS
    return [[group * inner + k for k in range(inner)] for group in range(BLOCK_GROUPS)]


def inner_gather(shard, sizes):
    if sizes[0] == BLOCK_GROUPS:
        return shard
    return lax.all_gather(shard, "dp", axis=0, tiled=True, axis_index_groups=inner_groups(sizes))


def inner_scatter(grad, sizes):
    if sizes[0] == BLOCK_GROUPS:
        return grad
    return lax.psum_scatter(
        grad, "dp", scatter_dimension=0, tiled=True, axis_index_groups=inner_groups(sizes)
    )


def inner_sum(vector, sizes):
    if sizes[0] == BLOCK_GROUPS:
        return vector
    return jnp.sum(lax.all_gather(vector, "dp", axis_index_groups=inner_groups(sizes)), axis=0)


def per_device(
    inputs, embedding, region, cotangent, conv_one, bias_one, conv_two, bias_two, emb_weight,
    emb_bias, qkv_weight, q_bias, v_bias, proj_weight, proj_bias, gain_one, shift_one, gain_two,
    shift_two, gain_three, shift_three,
):
    sizes = (lax.axis_size("dp"), lax.axis_size("head"))
    inner = sizes[0] // BLOCK_GROUPS
    dp_id, head_id = lax.axis_index("dp"), lax.axis_index("head")
    me = jnp.stack([dp_id // inner, head_id]).astype(jnp.int32)
    kernel = functools.partial
    map_shape = (MAPS, PIXELS, WIDTH)
    shifted_shape = (MAPS, PADDED, 3 * WIDTH)

    shards = [inner_gather(w, sizes) for w in (conv_one, conv_two, emb_weight, qkv_weight, proj_weight)]

    first, second, third, fourth = stages_of(sizes)
    core = (1, 1)

    def send(values, masks):
        return swap(values, masks, sizes)

    stats_shape = shape_of((2 * MAPS, WIDTH), F32)
    small_shape = shape_of((8, WIDTH), F32)
    sums_scratch = pltpu.VMEM((2 * MAPS, WIDTH), F32)
    pack_one, pack_two = run_kernel(
        pack_kernel,
        "pack",
        (shards[0].T, shards[1].T, *shards[2:]),
        (
            shape_of((1, CONV_PACK, LANES), BF16),
            shape_of((1, SECOND_ROWS + PROJ_PACK, LANES), BF16),
        ),
        room=62,
    )
    one = send(pack_one, first)
    two = send(pack_two, first)
    params, qkv_bias, film_bias, region_col, region_row, grouping = run_kernel(
        prepare_kernel,
        "prepare",
        (
            me, after(region, pack_one), bias_one, bias_two, gain_one, shift_one, gain_two, shift_two,
            gain_three, shift_three, proj_bias, q_bias, v_bias, emb_bias,
        ),
        (
            shape_of((16, WIDTH), F32),
            shape_of((1, SLOTS), F32),
            shape_of((1, 2 * WIDTH), F32),
            shape_of((MAPS, PIXELS, 1), jnp.int32),
            shape_of((MAPS, 1, PIXELS), jnp.int32),
            shape_of((WIDTH, WIDTH), F32),
        ),
        room=62,
    )
    held_one = join(pack_one, one)
    one = send(held_one, second)
    held_two = join(pack_two, after(two, held_one))
    two = send(held_two, second)
    held_one = join(held_one, after(one, held_two, params))
    one = send(held_one, third)
    held_two = join(held_two, after(two, held_one))
    two = send(held_two, third)
    held_one = join(held_one, after(one, held_two))
    far_one = send(held_one, fourth)
    near_core_one = send(held_one, core)
    shifted_one, stats_one = run_kernel(
        norm_one_kernel,
        "norm_one",
        (after(inputs, held_one), region_col, params, grouping),
        (shape_of(shifted_shape, BF16), stats_shape),
        (sums_scratch,),
    )
    held_two, held_three = run_kernel(
        join_split_kernel,
        "join",
        (held_two, after(two, stats_one)),
        (shape_of((8, SECOND_ROWS, LANES), BF16), shape_of((8, PROJ_PACK, LANES), BF16)),
        room=8,
    )
    far_two = send(held_two, fourth)
    near_core_two = send(held_two, core)
    far_one = after(far_one, held_two)
    far_core_one = send(far_one, core)
    shifted_core_one = send(shifted_one, core)
    weight_shape = shape_of((WIDTH, TAPS), BF16)
    weight_one, conv_out, stats_two = run_kernel(
        conv_one_kernel,
        "conv_one",
        (
            me, after(shifted_one, held_two), region_col, params, grouping,
            held_one, far_one, near_core_one, far_core_one,
        ),
        (weight_shape, shape_of(map_shape, F32), stats_shape),
        (sums_scratch,),
        blocks=(32, CONV_PACK, LANES),
    )
    far_three = send(after(held_three, conv_out), fourth)
    near_core_three = send(held_three, core)
    far_two = after(far_two, conv_out)
    far_core_two = send(far_two, core)
    weight_two, film_weight, hidden_two, shifted_two, residual, attend_in, stats_three, film = run_kernel(
        conv_two_kernel,
        "conv_two",
        (
            me, conv_out, stats_two, inputs, embedding, film_bias, region_col,
            params, grouping, held_two, far_two, near_core_two, far_core_two,
        ),
        (
            weight_shape,
            shape_of((EMBED, 2 * WIDTH), BF16),
            shape_of(map_shape, BF16),
            shape_of(shifted_shape, BF16),
            shape_of(map_shape, F32),
            shape_of(map_shape, BF16),
            stats_shape,
            shape_of((MAPS, 2 * WIDTH), F32),
        ),
        (sums_scratch,),
        blocks=(32, SECOND_ROWS, LANES),
    )
    far_three = after(far_three, attend_in)
    far_core_three = send(far_three, core)
    proj_shape = shape_of((8, PROJ_PACK, LANES), BF16)
    output, grad_attend, column_sums, sums_three, *proj_terms = run_kernel(
        attend_kernel,
        "attend",
        (
            me, attend_in, qkv_bias, region_col, region_row, cotangent, residual, stats_three, params,
            held_three, far_three, near_core_three, far_core_three,
        ),
        (shape_of(map_shape, BF16), shape_of(map_shape, F32), shape_of((1, SLOTS), F32), stats_shape)
        + (proj_shape,) * 4,
        (
            pltpu.VMEM((WIDTH, SLOTS), BF16),
            pltpu.VMEM((WIDTH, HEADS * LANES), BF16),
            pltpu.VMEM((PIXELS, SLOTS), BF16),
            pltpu.VMEM((MAPS * PIXELS, SLOTS), BF16),
            pltpu.VMEM((MAPS * PIXELS, HEADS * LANES), BF16),
            pltpu.VMEM((32, PROJ_PACK, LANES), BF16),
        ),
        blocks=(32, PROJ_PACK, LANES),
        terms=4,
    )
    near_proj, far_proj, near_came, far_came = proj_terms
    near_came, far_came = send(near_came, core), send(far_came, core)
    hidden_core_two = send(after(hidden_two, output), core)
    turned_shape = shape_of((2 * HEAD_DIM, MAPS * PIXELS), BF16)
    grad_residual, grad_conv_two, kept, sent, small_three = run_kernel(
        back_three_kernel,
        "back_three",
        (
            me, grad_attend, sums_three, region_col, cotangent, residual, stats_three, params, grouping,
        ),
        (shape_of(map_shape, F32), shape_of(map_shape, BF16), turned_shape, turned_shape, small_shape),
    )
    came = send(after(sent, near_came, far_came, hidden_core_two), core)
    total_shape = (3, 2 * HEAD_DIM, 3 * WIDTH)
    grads_scratch = pltpu.VMEM(total_shape, F32)
    (begun,) = run_kernel(
        own_grads_kernel, "own_grads", (kept, shifted_two), (shape_of(total_shape, F32),)
    )
    grads_rows = CONV_PACK + PROJ_PACK
    near_two, far_two = run_kernel(
        grads_two_kernel,
        "weight_grads_two",
        (me, after(came, begun), hidden_core_two, begun, near_proj, far_proj, near_came, far_came),
        (shape_of((8, grads_rows, LANES), BF16),) * 2,
        (
            grads_scratch,
            pltpu.VMEM(shifted_shape, BF16),
            pltpu.VMEM((16, grads_rows, LANES), BF16),
        ),
        terms=2,
    )
    two = send(far_two, fourth)
    back_scratch = (
        pltpu.VMEM((3, 3 * WIDTH, WIDTH), BF16),
        pltpu.VMEM(shifted_shape, BF16),
        pltpu.VMEM(map_shape, F32),
        sums_scratch,
    )
    grad_conv_one, kept, sent, grad_film, small_two = run_kernel(
        back_two_kernel,
        "back_two",
        (
            me, after(grad_conv_two, near_two, shifted_core_one), weight_two, conv_out, stats_two, film,
            region_col, params, grouping,
        ),
        (
            shape_of(map_shape, BF16),
            turned_shape,
            turned_shape,
            shape_of((MAPS, 2 * WIDTH), F32),
            small_shape,
        ),
        back_scratch,
    )
    came = send(sent, core)
    (begun,) = run_kernel(
        own_grads_kernel, "own_grads", (kept, shifted_one), (shape_of(total_shape, F32),)
    )
    (grad_embedding,) = run_kernel(
        back_film_kernel,
        "back_film",
        (embedding, film_weight, after(grad_film, begun)),
        (shape_of((MAPS, EMBED), F32),),
    )
    far_two, near_two = add_split(near_two, after(two, grad_embedding))
    two = send(far_two, third)
    near_one, far_one = run_kernel(
        grads_one_kernel,
        "weight_grads_one",
        (me, after(came, far_two), shifted_core_one, begun),
        (shape_of((8, CONV_PACK, LANES), BF16),) * 2,
        (grads_scratch, pltpu.VMEM((16, CONV_PACK, LANES), BF16)),
        terms=2,
    )
    one = send(far_one, fourth)
    grad_inputs, small_one = run_kernel(
        back_one_kernel,
        "back_one",
        (
            after(grad_conv_one, near_one), weight_one, inputs, stats_one, grad_residual,
            region_col, params, grouping,
        ),
        (shape_of(map_shape, BF16), small_shape),
        back_scratch,
    )
    far_two, near_two = add_split(near_two, after(two, small_one))
    two = send(far_two, second)

    def message(count):
        return (shape_of((SUM_ROWS + 2 * MAPS * count, 2 * WIDTH), BF16),)

    def next_message(parts, count):
        return run_kernel(next_message_kernel, "next_message", parts, message(count), room=8)[0]

    (rows,) = run_kernel(
        first_message_kernel,
        "first_message",
        (after(small_one, far_two), small_two, small_three, column_sums, grad_film, embedding),
        message(1),
        room=8,
    )
    came = send(rows, second)
    far_one, near_one = add_split(near_one, after(one, rows))
    one = send(far_one, third)
    rows = next_message((rows, after(came, far_one)), 2)
    came = send(rows, first)
    far_two, near_two = add_split(near_two, after(two, rows))
    two = send(far_two, first)
    rows = next_message((rows, after(came, far_two)), 4)
    came = send(rows, third)
    far_one, near_one = add_split(near_one, after(one, rows))
    one = send(far_one, second)
    rows = next_message((rows, after(came, far_one)), 8)
    came = send(rows, fourth)
    conv_grad_shape = shape_of((HEAD_DIM, CONV_ROWS), F32)
    grad_weight_two, grad_qkv_weight, grad_proj_weight = run_kernel(
        finish_two_kernel,
        "finish_two",
        (near_two, after(two, rows)),
        (conv_grad_shape, shape_of((48, 3 * HEAD_DIM), F32), shape_of((48, HEAD_DIM), F32)),
        room=8,
    )
    far_one, near_one = add_split(near_one, after(one, grad_weight_two))
    one = send(far_one, first)
    rows = next_message((rows, after(came, far_one)), 16)
    came = (rows, send(rows, core))
    vector = shape_of((WIDTH,), F32)
    grad_emb_weight, *vectors = run_kernel(
        finish_rows_kernel,
        "finish_rows",
        (me, *came),
        (shape_of((EMBED // BLOCK_GROUPS, 2 * WIDTH // HEADS), F32),)
        + (vector,) * 11
        + (shape_of((2 * WIDTH,), F32),),
        room=8,
    )
    (grad_weight_one,) = run_kernel(
        finish_one_kernel,
        "finish_one",
        (near_one, after(one, grad_emb_weight)),
        (conv_grad_shape,),
        room=8,
    )
    finals = [
        inner_scatter(grad, sizes)
        for grad in (
            grad_weight_one.T, grad_weight_two.T, grad_emb_weight, grad_qkv_weight, grad_proj_weight,
        )
    ]
    vectors = [inner_sum(vector, sizes) for vector in vectors]
    return (
        output,
        grad_inputs,
        grad_embedding,
        *finals,
        vectors[4],
        vectors[8],
        vectors[11],
        vectors[9],
        vectors[10],
        vectors[7],
        vectors[0],
        vectors[1],
        vectors[2],
        vectors[3],
        vectors[5],
        vectors[6],
    )


def solution(mesh):
    own = P(AXES)
    split = P("dp", "head")
    whole = P()
    in_specs = (own, own, P("dp"), own, split, whole, split, whole, split, whole, split) + (
        (whole, whole, split) + (whole,) * 7
    )
    out_specs = (own,) * 3 + (split,) * 5 + (whole,) * 12
    return jax.shard_map(
        per_device, mesh=mesh, in_specs=in_specs, out_specs=out_specs, check_vma=False
    )
```

```python
import functools

import jax
import jax.numpy as jnp
from jax import lax
from jax.experimental import pallas as pl
from jax.experimental.pallas import tpu as pltpu
from jax.sharding import PartitionSpec as P

WIDTH = 384
EMBED = 512
HEADS = 4
HEAD_DIM = 96
GROUP_SIZE = 12
SIDE = 16
PIXELS = 256
MAPS = 4
LANES = 128
TAPS = 9 * WIDTH
PADDED = PIXELS + 2 * SIDE
SLOTS = 3 * HEADS * LANES
FACTOR = HEAD_DIM ** (-0.5)
EPS = 1e-05
AXES = ("dp", "head")

BLOCK_GROUPS = 8
CONV_ROWS = TAPS // BLOCK_GROUPS
CONV_PACK = 336
EMB_PACK = 96
SUM_ROWS = 16
PROJ_PACK = 144
SECOND_ROWS = CONV_PACK + EMB_PACK
THIRD_ROWS = PROJ_PACK + 16
ROOM = 28
FLOPS_PER_US = 1.5e9
DURATIONS = {
    "norm_one": 2.4,
    "conv_one": 6,
    "conv_two": 8,
    "attend": 15,
    "back_three": 2.5,
    "own_grads": 3.5,
    "weight_grads_two": 4.5,
    "back_two": 7.5,
    "back_film": 1.1,
    "weight_grads_one": 4,
    "back_one": 7,
}

F32 = jnp.float32
BF16 = jnp.bfloat16
BIAS_ONE, BIAS_TWO, GAIN_ONE, SHIFT_ONE, GAIN_TWO, SHIFT_TWO, GAIN_THREE, SHIFT_THREE, PROJ_BIAS = (
    range(9)
)

VMEM = pl.BlockSpec(memory_space=pltpu.VMEM)
SMEM = pl.BlockSpec(memory_space=pltpu.SMEM)


def after(value, *others):
    return lax.optimization_barrier((value, *others))[0]


class Parts:
    def __init__(self, parts, ref):
        self.parts, self.ref = parts, ref

    def collect(self):
        first = self.ref.shape[1] - self.parts[0].shape[1]
        for index, part in enumerate(self.parts):
            self.ref[8 * index : 8 * index + 8, first:] = part[...]


def run_kernel(kernel, name, operands, outs, scratch=(), room=ROOM, blocks=None, terms=0):
    operands = tuple(operands)
    plain = len(operands) - (blocks[0] // 8 if blocks else 0)
    direct = len(outs) - terms
    in_specs = [SMEM if value.dtype == jnp.int32 and value.ndim == 1 else VMEM for value in operands]
    scratch = list(scratch)
    own = len(scratch)
    if blocks:
        scratch.append(pltpu.VMEM(blocks, BF16))

    def body(*refs):
        ins = refs[: len(operands)]
        results = refs[len(operands) : len(operands) + len(outs)]
        given = refs[len(operands) + len(outs) :]
        held = [Parts(ins[plain:], given[own])] if blocks else []
        kernel(*ins[:plain], *held, *results[:direct], *given[:own])
        for k in range(terms):
            results[direct + k][...] = given[own - 1][8 * k : 8 * k + 8]

    return pl.pallas_call(
        body,
        out_shape=list(outs),
        in_specs=in_specs,
        out_specs=[VMEM] * len(outs),
        scratch_shapes=scratch,
        compiler_params=pltpu.CompilerParams(vmem_limit_bytes=room * 2**20),
        cost_estimate=pl.CostEstimate(
            flops=int(FLOPS_PER_US * DURATIONS.get(name, 0.5)), bytes_accessed=0, transcendentals=0
        ),
        name=name,
    )(*operands)


def shape_of(shape, dtype):
    return jax.ShapeDtypeStruct(shape, dtype)


def dot(left, right, dims=(1, 0)):
    return lax.dot_general(
        left, right, (((dims[0],), (dims[1],)), ((), ())), preferred_element_type=F32
    )


def group_total(rows, grouping):
    return lax.dot_general(
        rows,
        grouping,
        (((1,), (0,)), ((), ())),
        preferred_element_type=F32,
        precision=lax.Precision.HIGHEST,
    )


def sigmoid(values):
    return 1.0 / (1.0 + jnp.exp(-values))


def valid_of(region_ref, index):
    return (region_ref[index] > 0).astype(F32)


def cells_of(region_ref):
    counts = [jnp.sum(valid_of(region_ref, m), axis=0, keepdims=True) for m in range(MAPS)]
    return jnp.concatenate(counts, axis=0) * float(GROUP_SIZE)


def column_sum(values):
    return jnp.sum(values, axis=0, keepdims=True)


def store_shifted(target_ref, index, values):
    column = lax.broadcasted_iota(jnp.int32, (PIXELS, 1), 0) % SIDE
    left = jnp.where(column == 0, 0.0, pltpu.roll(values, 1, 0))
    right = jnp.where(column == SIDE - 1, 0.0, pltpu.roll(values, PIXELS - 1, 0))
    border = jnp.zeros((SIDE, 3 * WIDTH), BF16)
    target_ref[index, 0:SIDE, :] = border
    target_ref[index, SIDE + PIXELS : PADDED, :] = border
    for position, part in enumerate((left, values, right)):
        target_ref[index, SIDE : SIDE + PIXELS, position * WIDTH : (position + 1) * WIDTH] = (
            part.astype(BF16)
        )


def convolve(shifted_ref, index, weight_ref):
    total = None
    for tap_row in range(3):
        part = dot(
            shifted_ref[index, tap_row * SIDE : tap_row * SIDE + PIXELS, :],
            weight_ref[:, tap_row * 3 * WIDTH : (tap_row + 1) * 3 * WIDTH],
            (1, 1),
        )
        total = part if total is None else total + part
    return total


def flip_weight(flipped_ref, weight_ref):
    for tap_row in range(3):
        for tap_col in range(3):
            start = (3 * (2 - tap_row) + 2 - tap_col) * WIDTH
            flipped_ref[tap_row, tap_col * WIDTH : (tap_col + 1) * WIDTH, :] = weight_ref[
                :, start : start + WIDTH
            ]


def convolve_back(shifted_ref, index, flipped_ref):
    total = None
    for tap_row in range(3):
        part = dot(
            shifted_ref[index, tap_row * SIDE : tap_row * SIDE + PIXELS, :],
            flipped_ref[tap_row],
        )
        total = part if total is None else total + part
    return total


def pack_conv(shard):
    tail = shard[:, 3 * LANES :]
    parts = [shard[:, LANES * k : LANES * (k + 1)] for k in range(3)]
    parts.append(jnp.concatenate([tail[:48], tail[48:], jnp.zeros((48, 32), shard.dtype)], axis=1))
    return jnp.concatenate(parts, axis=0)


def pack_proj(qkv, proj):
    wide = jnp.concatenate([qkv, proj], axis=1)
    return jnp.concatenate([wide[:, LANES * k : LANES * (k + 1)] for k in range(3)], axis=0)


def pack_emb(shard):
    side = shard[:, LANES:]
    half = side.shape[0] // 2
    return jnp.concatenate(
        [shard[:, :LANES], jnp.concatenate([side[:half], side[half:]], axis=1)], axis=0
    )


def prepare_kernel(
    me_ref, region, bias_one, bias_two, gain_one, shift_one, gain_two, shift_two, gain_three,
    shift_three, proj_bias, q_bias, v_bias, emb_bias,
    params, qkv_bias, film_bias, region_col, region_row, grouping,
):
    vectors = (
        bias_one, bias_two, gain_one, shift_one, gain_two, shift_two, gain_three, shift_three,
        proj_bias,
    )
    for row, vector in enumerate(vectors):
        params[row : row + 1, :] = vector[...].reshape(1, WIDTH)
    queries, values = q_bias[...].reshape(1, WIDTH), v_bias[...].reshape(1, WIDTH)
    gap = jnp.zeros((1, LANES - HEAD_DIM), F32)
    for head in range(HEADS):
        part = slice(HEAD_DIM * head, HEAD_DIM * (head + 1))
        base = 3 * LANES * head
        qkv_bias[:, base : base + LANES] = jnp.concatenate([queries[:, part], gap], axis=1)
        qkv_bias[:, base + LANES : base + 2 * LANES] = jnp.zeros((1, LANES), F32)
        qkv_bias[:, base + 2 * LANES : base + 3 * LANES] = jnp.concatenate(
            [values[:, part], gap], axis=1
        )
    film_bias[...] = emb_bias[...].reshape(1, 2 * WIDTH)
    rows = region[...].astype(F32)
    home = me_ref[1] * MAPS
    turned = jnp.concatenate([rows, jnp.zeros((LANES - rows.shape[0], PIXELS), F32)], axis=0).T
    lane = lax.broadcasted_iota(jnp.int32, (PIXELS, LANES), 1)
    for m in range(MAPS):
        region_row[m] = region[pl.ds(home + m, 1)]
        region_col[m] = jnp.sum(
            jnp.where(lane == home + m, turned, 0.0), axis=1, keepdims=True
        ).astype(jnp.int32)
    down = lax.broadcasted_iota(jnp.int32, (WIDTH, WIDTH), 0)
    along = lax.broadcasted_iota(jnp.int32, (WIDTH, WIDTH), 1)
    grouping[...] = (down // GROUP_SIZE == along // GROUP_SIZE).astype(F32)


def pack_kernel(conv_one, conv_two, emb, qkv, proj, embedding, first, second, third):
    first[0] = pack_conv(conv_one[...].astype(F32)).astype(BF16)
    second[0, 0:CONV_PACK] = pack_conv(conv_two[...].astype(F32)).astype(BF16)
    second[0, CONV_PACK:] = pack_emb(emb[...].astype(F32)).astype(BF16)
    third[0, 0:PROJ_PACK] = pack_proj(qkv[...].astype(F32), proj[...].astype(F32)).astype(BF16)
    embed = embedding[...].astype(F32)
    low = embed * sigmoid(embed)
    third[0, PROJ_PACK:] = jnp.concatenate(
        [low[:, LANES * k : LANES * (k + 1)] for k in range(EMBED // LANES)], axis=0
    ).astype(BF16)


def place_of(group, head, me_ref):
    far_group = group ^ me_ref[0]
    far_head = head ^ me_ref[1]
    bits = [far_group // 4, (far_group // 2) & 1, far_head // 2, far_group & 1]
    if head % 2 == 1:
        bits[2:] = bits[:1:-1]
    place = 16 * (far_head & 1)
    for position, bit in enumerate(bits):
        place = place + (1 << position) * bit
    return place


def place_of_own(group, over_x, me_ref):
    far_group = group ^ me_ref[0]
    far_x = over_x ^ (me_ref[1] // 2)
    far_y = far_group & 1
    odd = (me_ref[1] & 1) == 1
    place = far_group // 4 + 2 * ((far_group // 2) & 1)
    return place + jnp.where(odd, 4 * far_y + 8 * far_x, 4 * far_x + 8 * far_y)


def turn_halves(values, index, me_ref, kept, sent):
    odd = (me_ref[1] & 1) == 1
    turned = values.T
    place = pl.ds(index * PIXELS, PIXELS)
    for over_x in range(2):
        low = turned[2 * HEAD_DIM * over_x : 2 * HEAD_DIM * over_x + HEAD_DIM]
        high = turned[2 * HEAD_DIM * over_x + HEAD_DIM : 2 * HEAD_DIM * (over_x + 1)]
        rows = slice(HEAD_DIM * over_x, HEAD_DIM * (over_x + 1))
        kept[rows, place] = jnp.where(odd, high, low).astype(BF16)
        sent[rows, place] = jnp.where(odd, low, high).astype(BF16)


def repeat(count, step):
    def body(index, carry):
        step(index)
        return carry

    lax.fori_loop(0, count, body, 0)


def rows_of(index, size):
    return pl.ds(pl.multiple_of(index * size, 16), size)


def unpack_conv(blocks, me_ref, weight_ref):
    for head in range(HEADS):
        pieces = []
        for group in range(BLOCK_GROUPS):
            block = blocks[place_of(group, head, me_ref), 0:CONV_PACK]
            pieces += [block[HEAD_DIM * k : HEAD_DIM * (k + 1)] for k in range(3)]
            pieces.append(jnp.concatenate([block[288:, :48], block[288:, 48:96]], axis=0))
        weight_ref[HEAD_DIM * head : HEAD_DIM * (head + 1), :] = jnp.concatenate(
            pieces, axis=1
        )


def unpack_emb(blocks, me_ref, emb_ref):
    for group in range(BLOCK_GROUPS):
        embs = []
        for head in range(HEADS):
            emb = blocks[place_of(group, head, me_ref), CONV_PACK:].astype(F32)
            side = jnp.concatenate([emb[64:96, :64], emb[64:96, 64:]], axis=0)
            embs.append(jnp.concatenate([emb[:64], side], axis=1))
        emb_ref[64 * group : 64 * group + 64] = jnp.concatenate(embs, axis=1).astype(BF16)


def unpack_proj(blocks, me_ref, qkv_ref, proj_ref):
    gap = jnp.zeros((48, LANES - HEAD_DIM), F32)
    for group in range(BLOCK_GROUPS):
        rows = slice(48 * group, 48 * group + 48)
        for head in range(HEADS):
            block = blocks[place_of(group, head, me_ref)].astype(F32)
            wide = jnp.concatenate([block[48 * k : 48 * k + 48] for k in range(3)], axis=1)
            for part in range(3):
                piece = wide[:, HEAD_DIM * part : HEAD_DIM * (part + 1)]
                slot = (3 * head + part) * LANES
                qkv_ref[rows, slot : slot + LANES] = jnp.concatenate([piece, gap], axis=1).astype(
                    BF16
                )
            proj_ref[rows, LANES * head : LANES * (head + 1)] = jnp.concatenate(
                [wide[:, 3 * HEAD_DIM :], gap], axis=1
            ).astype(BF16)


def norm_stats(sums, squares, cells, grouping):
    totals = group_total(jnp.concatenate([sums, squares], axis=0), grouping)
    mean = totals[:MAPS] / cells
    inverse = lax.rsqrt(totals[MAPS:] / cells - mean * mean + EPS)
    return jnp.concatenate([mean, inverse], axis=0)


def norm_one_kernel(inputs, region, params, grouping, shifted, stats, sums):
    def add_map(m):
        values = inputs[m].astype(F32)
        masked = values * valid_of(region, m)
        sums[pl.ds(m, 1)] = column_sum(masked)
        sums[pl.ds(MAPS + m, 1)] = column_sum(masked * values)

    def one_map(m):
        hat = (inputs[m].astype(F32) - stats[pl.ds(m, 1)]) * stats[pl.ds(MAPS + m, 1)]
        normed = hat * params[GAIN_ONE : GAIN_ONE + 1] + params[SHIFT_ONE : SHIFT_ONE + 1]
        store_shifted(shifted, m, normed * sigmoid(normed) * valid_of(region, m))

    repeat(MAPS, add_map)
    stats[...] = norm_stats(sums[:MAPS], sums[MAPS:], cells_of(region), grouping[...])
    repeat(MAPS, one_map)


def conv_one_kernel(
    me_ref, shifted, region, params, grouping, blocks, weight, result, stats, sums
):
    blocks.collect()
    unpack_conv(blocks.ref, me_ref, weight)

    def one_map(m, carry):
        value = convolve(shifted, m, weight) + params[BIAS_ONE : BIAS_ONE + 1]
        result[m] = value
        masked = value * valid_of(region, m)
        sums[pl.ds(m, 1)] = column_sum(masked)
        sums[pl.ds(MAPS + m, 1)] = column_sum(masked * value)
        return carry

    lax.fori_loop(0, MAPS, one_map, 0, unroll=True)
    stats[...] = norm_stats(sums[:MAPS], sums[MAPS:], cells_of(region), grouping[...])


def modulate(value, stats, film, params, m):
    hat = (value - stats[pl.ds(m, 1)]) * stats[pl.ds(MAPS + m, 1)]
    modulated = hat * params[GAIN_TWO : GAIN_TWO + 1] + params[SHIFT_TWO : SHIFT_TWO + 1]
    scale = 1.0 + film[pl.ds(m, 1), :WIDTH]
    return hat, modulated, scale, modulated * scale + film[pl.ds(m, 1), WIDTH:]


def conv_two_kernel(
    me_ref, conv_out, stats_two, inputs, embedding, emb_bias, region, params, grouping, blocks,
    weight, emb_weight, hidden, shifted, residual, attend_in, stats, film,
    sums,
):
    blocks.collect()
    unpack_conv(blocks.ref, me_ref, weight)
    unpack_emb(blocks.ref, me_ref, emb_weight)
    embed = embedding[...].astype(F32)
    film[...] = dot((embed * sigmoid(embed)).astype(BF16), emb_weight[...]) + emb_bias[...]

    def one_map(m, carry):
        _, _, _, normed = modulate(conv_out[m], stats_two, film, params, m)
        valid = valid_of(region, m)
        active = normed * sigmoid(normed) * valid
        hidden[m] = active.astype(BF16)
        store_shifted(shifted, m, active)
        value = (
            inputs[m].astype(F32)
            + convolve(shifted, m, weight)
            + params[BIAS_TWO : BIAS_TWO + 1]
        )
        residual[m] = value
        sums[pl.ds(m, 1)] = column_sum(value * valid)
        sums[pl.ds(MAPS + m, 1)] = column_sum(value * value * valid)
        return carry

    lax.fori_loop(0, MAPS, one_map, 0, unroll=True)
    stats[...] = norm_stats(sums[:MAPS], sums[MAPS:], cells_of(region), grouping[...])
    for m in range(MAPS):
        hat = (residual[m] - stats[m : m + 1]) * stats[MAPS + m : MAPS + m + 1]
        attend_in[m] = (
            hat * params[GAIN_THREE : GAIN_THREE + 1] + params[SHIFT_THREE : SHIFT_THREE + 1]
        ).astype(BF16)


def norm_back(grad, hat, along, cross, inverse, valid, cells):
    return inverse * (grad - valid * (along + cross * hat) / cells)


def attend_kernel(
    me_ref, attend_in, qkv_bias, region, region_row, cotangent, residual, stats, params, blocks,
    output, grad_attend, bias_sums, sums, embeds,
    qkv_weight, proj_weight, columns, grad_columns, attended, terms,
):
    blocks.collect()
    unpack_proj(blocks.ref, me_ref, qkv_weight, proj_weight)

    def two_devices(pair):
        rows = []
        for index in (2 * pair, 2 * pair + 1):
            low = ((index >> 1) & 1) + 2 * (index & 1)
            block = blocks.ref[low + 4 * (index >> 2), PROJ_PACK:, :].astype(F32)
            tiles = [block[MAPS * k : MAPS * (k + 1)] for k in range(EMBED // LANES)]
            rows.append(jnp.concatenate(tiles, axis=1))
        embeds[pl.ds(pl.multiple_of(2 * MAPS * pair, 8), 2 * MAPS)] = jnp.concatenate(rows, axis=0)

    repeat(16, two_devices)

    def one_map(m, carry):
        rows = pl.ds(pl.multiple_of(m * PIXELS, PIXELS), PIXELS)
        columns[...] = (dot(attend_in[m], qkv_weight[...]) + qkv_bias[...]).astype(BF16)
        grad_attended = dot(cotangent[m], proj_weight[...]).astype(BF16)
        key_region = region[m]
        query_region = region_row[m]
        allowed = (key_region > 0) & ((key_region == query_region) | (query_region == 0))
        for head in range(HEADS):
            base = 3 * LANES * head
            queries = columns[:, base : base + LANES]
            keys = columns[:, base + LANES : base + 2 * LANES]
            values = columns[:, base + 2 * LANES : base + 3 * LANES]
            grad_out = grad_attended[:, LANES * head : LANES * (head + 1)]
            logits = jnp.where(allowed, dot(keys, queries, (1, 1)) * FACTOR, -1e30)
            raised = jnp.exp(logits - jnp.max(logits, axis=0, keepdims=True))
            weights = raised * (1.0 / jnp.sum(raised, axis=0, keepdims=True))
            weights_low = weights.astype(BF16)
            attended[rows, LANES * head : LANES * (head + 1)] = dot(
                weights_low, values, (0, 0)
            ).astype(BF16)
            grad_weights = dot(values, grad_out, (1, 1))
            inner = jnp.sum(grad_weights * weights, axis=0, keepdims=True)
            grad_logits = (weights * (grad_weights - inner)).astype(BF16)
            grad_columns[rows, base : base + LANES] = (
                dot(grad_logits, keys, (0, 0)) * FACTOR
            ).astype(BF16)
            grad_columns[rows, base + LANES : base + 2 * LANES] = (
                dot(grad_logits, queries) * FACTOR
            ).astype(BF16)
            grad_columns[rows, base + 2 * LANES : base + 3 * LANES] = dot(
                weights_low, grad_out
            ).astype(BF16)
        output[m] = (
            residual[m]
            + dot(attended[rows, :], proj_weight[...], (1, 1))
            + params[PROJ_BIAS : PROJ_BIAS + 1]
        ).astype(BF16)
        grad = dot(grad_columns[rows, :], qkv_weight[...], (1, 1))
        grad_attend[m] = grad
        hat = (residual[m] - stats[pl.ds(m, 1)]) * stats[pl.ds(MAPS + m, 1)]
        sums[pl.ds(m, 1)] = column_sum(grad)
        sums[pl.ds(MAPS + m, 1)] = column_sum(grad * hat)
        return carry

    lax.fori_loop(0, MAPS, one_map, 0)
    bias_sums[...] = column_sum(grad_columns[...].astype(F32))
    grad_qkv, grad_proj = None, None
    for m in range(MAPS):
        rows = slice(m * PIXELS, (m + 1) * PIXELS)
        qkv_part = dot(attend_in[m], grad_columns[rows, :], (0, 0))
        proj_part = dot(cotangent[m], attended[rows, :], (0, 0))
        grad_qkv = qkv_part if m == 0 else grad_qkv + qkv_part
        grad_proj = proj_part if m == 0 else grad_proj + proj_part
    for group in range(BLOCK_GROUPS):
        rows = slice(48 * group, 48 * group + 48)
        for head in range(HEADS):
            pieces = [
                grad_qkv[rows, slot * LANES : slot * LANES + HEAD_DIM]
                for slot in range(3 * head, 3 * head + 3)
            ]
            pieces.append(grad_proj[rows, head * LANES : head * LANES + HEAD_DIM])
            wide = jnp.concatenate(pieces, axis=1)
            terms[place_of(group, head, me_ref)] = jnp.concatenate(
                [wide[:, LANES * part : LANES * (part + 1)] for part in range(3)], axis=0
            ).astype(BF16)


def back_three_kernel(
    me_ref, grad_attend, sums, region, cotangent, residual, stats, params, grouping,
    grad_residual, grad_conv, kept, sent, small_sums,
):
    gain = params[GAIN_THREE : GAIN_THREE + 1]
    totals = group_total(sums[...] * gain, grouping[...])
    cells = cells_of(region)
    small_sums[...] = jnp.zeros_like(small_sums)
    small_sums[0:1] = column_sum(sums[MAPS:])
    small_sums[1:2] = column_sum(sums[:MAPS])
    top_sum = jnp.zeros((1, WIDTH), F32)
    low_sum = jnp.zeros((1, WIDTH), F32)
    for m in range(MAPS):
        inverse = stats[MAPS + m : MAPS + m + 1]
        hat = (residual[m] - stats[m : m + 1]) * inverse
        top = cotangent[m].astype(F32)
        grad = top + norm_back(
            grad_attend[m] * gain,
            hat,
            totals[m : m + 1],
            totals[MAPS + m : MAPS + m + 1],
            inverse,
            valid_of(region, m),
            cells[m : m + 1],
        )
        grad_residual[m] = grad
        low = grad.astype(BF16)
        grad_conv[m] = low
        turn_halves(low.astype(F32), m, me_ref, kept, sent)
        top_sum = top_sum + column_sum(top)
        low_sum = low_sum + column_sum(low.astype(F32))
    small_sums[2:3] = top_sum
    small_sums[3:4] = low_sum


def back_two_kernel(
    me_ref, grad_conv, weight, conv_out, stats, film, region, params, grouping,
    grad_low, kept, sent, grad_film, small_sums,
    flipped, shifted, grad_normed, sums,
):
    flip_weight(flipped, weight)

    def one_map(m, carry):
        store_shifted(shifted, m, grad_conv[m].astype(F32))
        hat, modulated, scale, normed = modulate(conv_out[m], stats, film, params, m)
        logistic = sigmoid(normed)
        slope = logistic * (1.0 + normed * (1.0 - logistic)) * valid_of(region, m)
        grad = convolve_back(shifted, m, flipped) * slope
        grad_film[pl.ds(m, 1), :WIDTH] = column_sum(grad * modulated)
        grad_film[pl.ds(m, 1), WIDTH:] = column_sum(grad)
        scaled = grad * scale
        grad_normed[m] = scaled
        sums[pl.ds(m, 1)] = column_sum(scaled)
        sums[pl.ds(MAPS + m, 1)] = column_sum(scaled * hat)
        return carry

    lax.fori_loop(0, MAPS, one_map, 0, unroll=2)
    gain = params[GAIN_TWO : GAIN_TWO + 1]
    totals = group_total(sums[...] * gain, grouping[...])
    cells = cells_of(region)
    small_sums[...] = jnp.zeros_like(small_sums)
    small_sums[0:1] = column_sum(sums[MAPS:])
    small_sums[1:2] = column_sum(sums[:MAPS])
    low_sum = jnp.zeros((1, WIDTH), F32)
    for m in range(MAPS):
        inverse = stats[MAPS + m : MAPS + m + 1]
        low = norm_back(
            grad_normed[m] * gain,
            (conv_out[m] - stats[m : m + 1]) * inverse,
            totals[m : m + 1],
            totals[MAPS + m : MAPS + m + 1],
            inverse,
            valid_of(region, m),
            cells[m : m + 1],
        ).astype(BF16)
        grad_low[m] = low
        turn_halves(low.astype(F32), m, me_ref, kept, sent)
        low_sum = low_sum + column_sum(low.astype(F32))
    small_sums[2:3] = low_sum


def back_film_kernel(embedding, emb_weight, grad_film, grad_embed):
    embed = embedding[...].astype(F32)
    logistic = sigmoid(embed)
    film_high = grad_film[...].astype(BF16)
    film_rest = (grad_film[...] - film_high.astype(F32)).astype(BF16)
    grad_embed[...] = (
        dot(film_high, emb_weight[...], (1, 1)) + dot(film_rest, emb_weight[...], (1, 1))
    ) * (logistic * (1.0 + embed * (1.0 - logistic)))


def back_one_kernel(
    grad_conv, weight, inputs, stats, grad_residual, region, params, grouping,
    grad_inputs, small_sums,
    flipped, shifted, grad_normed, sums,
):
    flip_weight(flipped, weight)
    gain = params[GAIN_ONE : GAIN_ONE + 1]

    def one_map(m, carry):
        store_shifted(shifted, m, grad_conv[m].astype(F32))
        hat = (inputs[m].astype(F32) - stats[pl.ds(m, 1)]) * stats[pl.ds(MAPS + m, 1)]
        normed = hat * gain + params[SHIFT_ONE : SHIFT_ONE + 1]
        logistic = sigmoid(normed)
        slope = logistic * (1.0 + normed * (1.0 - logistic)) * valid_of(region, m)
        grad = convolve_back(shifted, m, flipped) * slope
        grad_normed[m] = grad
        sums[pl.ds(m, 1)] = column_sum(grad)
        sums[pl.ds(MAPS + m, 1)] = column_sum(grad * hat)
        return carry

    lax.fori_loop(0, MAPS, one_map, 0)
    totals = group_total(sums[...] * gain, grouping[...])
    cells = cells_of(region)
    small_sums[...] = jnp.zeros_like(small_sums)
    small_sums[0:1] = column_sum(sums[MAPS:])
    small_sums[1:2] = column_sum(sums[:MAPS])
    for m in range(MAPS):
        inverse = stats[MAPS + m : MAPS + m + 1]
        grad_inputs[m] = (
            grad_residual[m]
            + norm_back(
                grad_normed[m] * gain,
                (inputs[m].astype(F32) - stats[m : m + 1]) * inverse,
                totals[m : m + 1],
                totals[MAPS + m : MAPS + m + 1],
                inverse,
                valid_of(region, m),
                cells[m : m + 1],
            )
        ).astype(BF16)


def conv_weight_grads(shifted, turned, total, begun=None):
    def one_row(tap_row, carry):
        rows = pl.ds(pl.multiple_of(tap_row * SIDE, SIDE), PIXELS)
        part = None if begun is None else begun[tap_row]
        for m in range(MAPS):
            term = dot(turned[:, m * PIXELS : (m + 1) * PIXELS], shifted[m, rows, :])
            part = term if part is None else part + term
        total[tap_row] = part
        return carry

    lax.fori_loop(0, 3, one_row, 0)


def own_grads_kernel(kept, shifted, total):
    conv_weight_grads(shifted, kept, total)


def pack_conv_grads(total, me_ref, blocks):
    def one_half(over_x):
        rows = rows_of(over_x, HEAD_DIM)
        for group in range(BLOCK_GROUPS):
            start, stop = group * CONV_ROWS, (group + 1) * CONV_ROWS
            values = []
            for tap_row in range(3):
                low, high = tap_row * 3 * WIDTH, (tap_row + 1) * 3 * WIDTH
                if max(low, start) < min(high, stop):
                    values.append(total[tap_row, rows, max(low, start) - low : min(high, stop) - low])
            block = values[0] if len(values) == 1 else jnp.concatenate(values, axis=1)
            place = place_of_own(group, over_x, me_ref)
            blocks[place, 0:CONV_PACK, :] = pack_conv(block.astype(BF16))

    repeat(2, one_half)


def grads_one_kernel(me_ref, came, shifted_core, begun, total, blocks):
    conv_weight_grads(shifted_core, came, total, begun)
    pack_conv_grads(total, me_ref, blocks)


def grads_two_kernel(
    me_ref, came, hidden_core, begun, near, far, near_came, far_came, total, shifted_core, blocks
):
    for m in range(MAPS):
        store_shifted(shifted_core, m, hidden_core[m].astype(F32))
    conv_weight_grads(shifted_core, came, total, begun)
    pack_conv_grads(total, me_ref, blocks)
    for index, (mine, other) in enumerate(((near, near_came), (far, far_came))):
        blocks[8 * index : 8 * index + 8, CONV_PACK:, :] = (
            mine[...].astype(F32) + other[...].astype(F32)
        ).astype(BF16)


def unpack_conv_grad(block, result):
    for part in range(3):
        result[:, LANES * part : LANES * (part + 1)] = block[HEAD_DIM * part : HEAD_DIM * (part + 1)]
    result[:, 3 * LANES :] = jnp.concatenate([block[288:336, :48], block[288:336, 48:96]], axis=0)


def first_message_kernel(small_one, small_two, small_three, column_sums, grad_film, message):
    pieces = [small_one[0:1], small_one[1:2], small_two[0:1], small_two[1:2], small_two[2:3]]
    pieces += [small_three[row : row + 1] for row in range(4)]
    for part in (0, 2):
        slots = [(3 * head + part) * LANES for head in range(HEADS)]
        pieces.append(
            jnp.concatenate([column_sums[:, slot : slot + HEAD_DIM] for slot in slots], axis=1)
        )
    film = column_sum(grad_film[...])
    pieces.append(jnp.zeros((1, WIDTH), F32))
    rows = [jnp.concatenate(pieces[k : k + 2], axis=1) for k in range(0, 12, 2)]
    sums = jnp.concatenate(rows + [film, jnp.zeros((1, 2 * WIDTH), F32)], axis=0)
    store_message(sums, [grad_film[...]], message)


def store_message(sums, films, message):
    high = sums.astype(BF16).astype(F32)
    message[...] = jnp.concatenate([high, sums - high, *films], axis=0).astype(BF16)


def added_sums(parts):
    half = SUM_ROWS // 2
    total = None
    for part in parts:
        both = part[:half] + part[half:SUM_ROWS]
        total = both if total is None else total + both
    return total


def next_message_kernel(left, right, message):
    parts = [left[...].astype(F32), right[...].astype(F32)]
    store_message(added_sums(parts), [part[SUM_ROWS:] for part in parts], message)


def finish_one_kernel(mine, other, result):
    unpack_conv_grad(mine[0].astype(F32) + other[0].astype(F32), result)


def finish_rows_kernel(me_ref, embeds, left, right, emb, *vectors):
    parts = [left[...].astype(F32), right[...].astype(F32)]
    sums = added_sums(parts)
    for index, vector in enumerate(vectors[:11]):
        row, place = index // 2, (index % 2) * WIDTH
        vector[...] = sums[row, place : place + WIDTH]
    vectors[11][...] = sums[6]
    films = jnp.concatenate([part[SUM_ROWS:] for part in parts], axis=0)
    rows, cols = emb.shape
    mine = films[:, 0:cols]
    for head in range(1, HEADS):
        mine = jnp.where(me_ref[1] == head, films[:, cols * head : cols * (head + 1)], mine)
    products = dot(embeds[...].astype(BF16), mine.astype(BF16), (0, 0))
    total = products[0:rows]
    for group in range(1, BLOCK_GROUPS):
        total = jnp.where(me_ref[0] == group, products[rows * group : rows * (group + 1)], total)
    emb[...] = total


def finish_two_kernel(mine, other, result, qkv, proj):
    block = mine[0].astype(F32) + other[0].astype(F32)
    unpack_conv_grad(block, result)
    tiles = [block[CONV_PACK + 48 * k : CONV_PACK + 48 * k + 48] for k in range(3)]
    wide = jnp.concatenate(tiles, axis=1)
    qkv[...] = wide[:, : 3 * HEAD_DIM]
    proj[...] = wide[:, 3 * HEAD_DIM :]


def join_kernel(left, right, joined):
    count = left.shape[0]
    joined[:count] = left[...]
    joined[count:] = right[...]


def add_split_kernel(left, right, send, keep):
    half = keep.shape[0]
    send[...] = (left[half:].astype(F32) + right[half:].astype(F32)).astype(BF16)
    keep[...] = (left[:half].astype(F32) + right[:half].astype(F32)).astype(BF16)


def swap(values, masks, sizes):
    pairs = [(own, own ^ masks[own % 2]) for own in range(sizes[0] * sizes[1])]
    return lax.ppermute(values, AXES, pairs)


def stages_of(sizes):
    inner = sizes[0] // BLOCK_GROUPS
    group_bit = sizes[1] * inner
    over_x, over_y = 2, group_bit
    return ((4 * group_bit,) * 2, (2 * group_bit,) * 2, (over_x, over_y), (over_y, over_x))


def join(left, right):
    joined = shape_of((left.shape[0] + right.shape[0],) + left.shape[1:], left.dtype)
    return run_kernel(join_kernel, "join", (left, right), (joined,), room=8)[0]


def add_split(left, right):
    half = shape_of((left.shape[0] // 2,) + left.shape[1:], BF16)
    return run_kernel(add_split_kernel, "add_split", (left, right), (half, half), room=8)


def inner_groups(sizes):
    inner = sizes[0] // BLOCK_GROUPS
    return [[group * inner + k for k in range(inner)] for group in range(BLOCK_GROUPS)]


def inner_gather(shard, sizes):
    if sizes[0] == BLOCK_GROUPS:
        return shard
    return lax.all_gather(shard, "dp", axis=0, tiled=True, axis_index_groups=inner_groups(sizes))


def inner_scatter(grad, sizes):
    if sizes[0] == BLOCK_GROUPS:
        return grad
    return lax.psum_scatter(
        grad, "dp", scatter_dimension=0, tiled=True, axis_index_groups=inner_groups(sizes)
    )


def inner_sum(vector, sizes):
    if sizes[0] == BLOCK_GROUPS:
        return vector
    return jnp.sum(lax.all_gather(vector, "dp", axis_index_groups=inner_groups(sizes)), axis=0)


def per_device(
    inputs, embedding, region, cotangent, conv_one, bias_one, conv_two, bias_two, emb_weight,
    emb_bias, qkv_weight, q_bias, v_bias, proj_weight, proj_bias, gain_one, shift_one, gain_two,
    shift_two, gain_three, shift_three,
):
    sizes = (lax.axis_size("dp"), lax.axis_size("head"))
    inner = sizes[0] // BLOCK_GROUPS
    dp_id, head_id = lax.axis_index("dp"), lax.axis_index("head")
    me = jnp.stack([dp_id // inner, head_id]).astype(jnp.int32)
    kernel = functools.partial
    map_shape = (MAPS, PIXELS, WIDTH)
    shifted_shape = (MAPS, PADDED, 3 * WIDTH)

    shards = [inner_gather(w, sizes) for w in (conv_one, conv_two, emb_weight, qkv_weight, proj_weight)]

    first, second, third, fourth = stages_of(sizes)
    core = (1, 1)

    def send(values, masks):
        return swap(values, masks, sizes)

    stats_shape = shape_of((2 * MAPS, WIDTH), F32)
    small_shape = shape_of((8, WIDTH), F32)
    sums_scratch = pltpu.VMEM((2 * MAPS, WIDTH), F32)
    pack_one, pack_two, pack_three = run_kernel(
        pack_kernel,
        "pack",
        (shards[0].T, shards[1].T, *shards[2:], embedding),
        (
            shape_of((1, CONV_PACK, LANES), BF16),
            shape_of((1, SECOND_ROWS, LANES), BF16),
            shape_of((1, THIRD_ROWS, LANES), BF16),
        ),
        room=62,
    )
    one = send(pack_one, first)
    two = send(pack_two, first)
    params, qkv_bias, film_bias, region_col, region_row, grouping = run_kernel(
        prepare_kernel,
        "prepare",
        (
            me, after(region, pack_one), bias_one, bias_two, gain_one, shift_one, gain_two, shift_two,
            gain_three, shift_three, proj_bias, q_bias, v_bias, emb_bias,
        ),
        (
            shape_of((16, WIDTH), F32),
            shape_of((1, SLOTS), F32),
            shape_of((1, 2 * WIDTH), F32),
            shape_of((MAPS, PIXELS, 1), jnp.int32),
            shape_of((MAPS, 1, PIXELS), jnp.int32),
            shape_of((WIDTH, WIDTH), F32),
        ),
        room=62,
    )
    held_one = join(pack_one, one)
    one = send(held_one, second)
    held_two = join(pack_two, after(two, held_one))
    two = send(held_two, second)
    held_one = join(held_one, after(one, held_two, params))
    one = send(held_one, third)
    held_two = join(held_two, after(two, held_one))
    two = send(held_two, third)
    three = send(after(pack_three, held_two), first)
    held_one = join(held_one, after(one, held_two))
    far_one = send(held_one, fourth)
    near_core_one = send(held_one, core)
    shifted_one, stats_one = run_kernel(
        norm_one_kernel,
        "norm_one",
        (after(inputs, held_one), region_col, params, grouping),
        (shape_of(shifted_shape, BF16), stats_shape),
        (sums_scratch,),
    )
    held_three = join(pack_three, after(three, stats_one))
    three = send(held_three, second)
    held_two = join(held_two, after(two, held_three))
    far_two = send(held_two, fourth)
    near_core_two = send(held_two, core)
    held_three = join(held_three, after(three, held_two))
    three = send(held_three, third)
    far_one = after(far_one, held_three)
    far_core_one = send(far_one, core)
    shifted_core_one = send(shifted_one, core)
    weight_shape = shape_of((WIDTH, TAPS), BF16)
    weight_one, conv_out, stats_two = run_kernel(
        conv_one_kernel,
        "conv_one",
        (
            me, after(shifted_one, held_three), region_col, params, grouping,
            held_one, far_one, near_core_one, far_core_one,
        ),
        (weight_shape, shape_of(map_shape, F32), stats_shape),
        (sums_scratch,),
        blocks=(32, CONV_PACK, LANES),
    )
    held_three = join(held_three, after(three, conv_out))
    far_three = send(held_three, fourth)
    near_core_three = send(held_three, core)
    far_two = after(far_two, conv_out, held_three)
    far_core_two = send(far_two, core)
    weight_two, film_weight, hidden_two, shifted_two, residual, attend_in, stats_three, film = run_kernel(
        conv_two_kernel,
        "conv_two",
        (
            me, after(conv_out, held_three), stats_two, inputs, embedding, film_bias, region_col,
            params, grouping, held_two, far_two, near_core_two, far_core_two,
        ),
        (
            weight_shape,
            shape_of((EMBED, 2 * WIDTH), BF16),
            shape_of(map_shape, BF16),
            shape_of(shifted_shape, BF16),
            shape_of(map_shape, F32),
            shape_of(map_shape, BF16),
            stats_shape,
            shape_of((MAPS, 2 * WIDTH), F32),
        ),
        (sums_scratch,),
        blocks=(32, SECOND_ROWS, LANES),
    )
    far_three = after(far_three, attend_in)
    far_core_three = send(far_three, core)
    proj_shape = shape_of((8, PROJ_PACK, LANES), BF16)
    output, grad_attend, column_sums, sums_three, embeds, *proj_terms = run_kernel(
        attend_kernel,
        "attend",
        (
            me, attend_in, qkv_bias, region_col, region_row, cotangent, residual, stats_three, params,
            held_three, far_three, near_core_three, far_core_three,
        ),
        (
            shape_of(map_shape, BF16), shape_of(map_shape, F32), shape_of((1, SLOTS), F32), stats_shape,
            shape_of((32 * MAPS, EMBED), F32),
        )
        + (proj_shape,) * 4,
        (
            pltpu.VMEM((WIDTH, SLOTS), BF16),
            pltpu.VMEM((WIDTH, HEADS * LANES), BF16),
            pltpu.VMEM((PIXELS, SLOTS), BF16),
            pltpu.VMEM((MAPS * PIXELS, SLOTS), BF16),
            pltpu.VMEM((MAPS * PIXELS, HEADS * LANES), BF16),
            pltpu.VMEM((32, PROJ_PACK, LANES), BF16),
        ),
        blocks=(32, THIRD_ROWS, LANES),
        terms=4,
    )
    near_proj, far_proj, near_came, far_came = proj_terms
    near_came, far_came = send(near_came, core), send(far_came, core)
    hidden_core_two = send(after(hidden_two, output), core)
    turned_shape = shape_of((2 * HEAD_DIM, MAPS * PIXELS), BF16)
    grad_residual, grad_conv_two, kept, sent, small_three = run_kernel(
        back_three_kernel,
        "back_three",
        (
            me, grad_attend, sums_three, region_col, cotangent, residual, stats_three, params, grouping,
        ),
        (shape_of(map_shape, F32), shape_of(map_shape, BF16), turned_shape, turned_shape, small_shape),
    )
    came = send(after(sent, near_came, far_came, hidden_core_two), core)
    total_shape = (3, 2 * HEAD_DIM, 3 * WIDTH)
    grads_scratch = pltpu.VMEM(total_shape, F32)
    (begun,) = run_kernel(
        own_grads_kernel, "own_grads", (kept, shifted_two), (shape_of(total_shape, F32),)
    )
    grads_rows = CONV_PACK + PROJ_PACK
    near_two, far_two = run_kernel(
        grads_two_kernel,
        "weight_grads_two",
        (me, after(came, begun), hidden_core_two, begun, near_proj, far_proj, near_came, far_came),
        (shape_of((8, grads_rows, LANES), BF16),) * 2,
        (
            grads_scratch,
            pltpu.VMEM(shifted_shape, BF16),
            pltpu.VMEM((16, grads_rows, LANES), BF16),
        ),
        terms=2,
    )
    two = send(far_two, fourth)
    back_scratch = (
        pltpu.VMEM((3, 3 * WIDTH, WIDTH), BF16),
        pltpu.VMEM(shifted_shape, BF16),
        pltpu.VMEM(map_shape, F32),
        sums_scratch,
    )
    grad_conv_one, kept, sent, grad_film, small_two = run_kernel(
        back_two_kernel,
        "back_two",
        (
            me, after(grad_conv_two, near_two, shifted_core_one), weight_two, conv_out, stats_two, film,
            region_col, params, grouping,
        ),
        (
            shape_of(map_shape, BF16),
            turned_shape,
            turned_shape,
            shape_of((MAPS, 2 * WIDTH), F32),
            small_shape,
        ),
        back_scratch,
    )
    came = send(sent, core)
    (begun,) = run_kernel(
        own_grads_kernel, "own_grads", (kept, shifted_one), (shape_of(total_shape, F32),)
    )
    (grad_embedding,) = run_kernel(
        back_film_kernel,
        "back_film",
        (embedding, film_weight, after(grad_film, begun)),
        (shape_of((MAPS, EMBED), F32),),
    )
    far_two, near_two = add_split(near_two, after(two, grad_embedding))
    two = send(far_two, third)
    near_one, far_one = run_kernel(
        grads_one_kernel,
        "weight_grads_one",
        (me, after(came, far_two), shifted_core_one, begun),
        (shape_of((8, CONV_PACK, LANES), BF16),) * 2,
        (grads_scratch, pltpu.VMEM((16, CONV_PACK, LANES), BF16)),
        terms=2,
    )
    one = send(far_one, fourth)
    grad_inputs, small_one = run_kernel(
        back_one_kernel,
        "back_one",
        (
            after(grad_conv_one, near_one), weight_one, inputs, stats_one, grad_residual,
            region_col, params, grouping,
        ),
        (shape_of(map_shape, BF16), small_shape),
        back_scratch,
    )
    far_two, near_two = add_split(near_two, after(two, small_one))
    two = send(far_two, second)

    def message(count):
        return (shape_of((SUM_ROWS + MAPS * count, 2 * WIDTH), BF16),)

    def next_message(parts, count):
        return run_kernel(next_message_kernel, "next_message", parts, message(count), room=8)[0]

    (rows,) = run_kernel(
        first_message_kernel,
        "first_message",
        (after(small_one, far_two), small_two, small_three, column_sums, grad_film),
        message(1),
        room=8,
    )
    came = send(rows, second)
    far_one, near_one = add_split(near_one, after(one, rows))
    one = send(far_one, third)
    rows = next_message((rows, after(came, far_one)), 2)
    came = send(rows, first)
    far_two, near_two = add_split(near_two, after(two, rows))
    two = send(far_two, first)
    rows = next_message((rows, after(came, far_two)), 4)
    came = send(rows, third)
    far_one, near_one = add_split(near_one, after(one, rows))
    one = send(far_one, second)
    rows = next_message((rows, after(came, far_one)), 8)
    came = send(rows, fourth)
    conv_grad_shape = shape_of((HEAD_DIM, CONV_ROWS), F32)
    grad_weight_two, grad_qkv_weight, grad_proj_weight = run_kernel(
        finish_two_kernel,
        "finish_two",
        (near_two, after(two, rows)),
        (conv_grad_shape, shape_of((48, 3 * HEAD_DIM), F32), shape_of((48, HEAD_DIM), F32)),
        room=8,
    )
    far_one, near_one = add_split(near_one, after(one, grad_weight_two))
    one = send(far_one, first)
    rows = next_message((rows, after(came, far_one)), 16)
    came = (rows, send(rows, core))
    vector = shape_of((WIDTH,), F32)
    grad_emb_weight, *vectors = run_kernel(
        finish_rows_kernel,
        "finish_rows",
        (me, embeds, *came),
        (shape_of((EMBED // BLOCK_GROUPS, 2 * WIDTH // HEADS), F32),)
        + (vector,) * 11
        + (shape_of((2 * WIDTH,), F32),),
        room=8,
    )
    (grad_weight_one,) = run_kernel(
        finish_one_kernel,
        "finish_one",
        (near_one, after(one, grad_emb_weight)),
        (conv_grad_shape,),
        room=8,
    )
    finals = [
        inner_scatter(grad, sizes)
        for grad in (
            grad_weight_one.T, grad_weight_two.T, grad_emb_weight, grad_qkv_weight, grad_proj_weight,
        )
    ]
    vectors = [inner_sum(vector, sizes) for vector in vectors]
    return (
        output,
        grad_inputs,
        grad_embedding,
        *finals,
        vectors[4],
        vectors[8],
        vectors[11],
        vectors[9],
        vectors[10],
        vectors[7],
        vectors[0],
        vectors[1],
        vectors[2],
        vectors[3],
        vectors[5],
        vectors[6],
    )


def solution(mesh):
    own = P(AXES)
    split = P("dp", "head")
    whole = P()
    in_specs = (own, own, P("dp"), own, split, whole, split, whole, split, whole, split) + (
        (whole, whole, split) + (whole,) * 7
    )
    out_specs = (own,) * 3 + (split,) * 5 + (whole,) * 12
    return jax.shard_map(
        per_device, mesh=mesh, in_specs=in_specs, out_specs=out_specs, check_vma=False
    )
```

```python
import functools

import jax
import jax.numpy as jnp
from jax import lax
from jax.experimental import pallas as pl
from jax.experimental.pallas import tpu as pltpu
from jax.sharding import PartitionSpec as P

WIDTH = 384
EMBED = 512
HEADS = 4
HEAD_DIM = 96
GROUP_SIZE = 12
SIDE = 16
PIXELS = 256
MAPS = 4
LANES = 128
TAPS = 9 * WIDTH
PADDED = PIXELS + 2 * SIDE
SLOTS = 3 * HEADS * LANES
FACTOR = HEAD_DIM ** (-0.5)
EPS = 1e-05
AXES = ("dp", "head")

BLOCK_GROUPS = 8
CONV_ROWS = TAPS // BLOCK_GROUPS
CONV_PACK = 336
EMB_PACK = 96
SUM_ROWS = 16
PROJ_PACK = 144
SECOND_ROWS = CONV_PACK + EMB_PACK
THIRD_ROWS = PROJ_PACK + 16
ROOM = 28
FLOPS_PER_US = 1.5e9
DURATIONS = {
    "norm_one": 2.4,
    "conv_one": 6,
    "conv_two": 8,
    "attend": 15,
    "back_three": 2.5,
    "own_grads": 3.5,
    "weight_grads_two": 4.5,
    "back_two": 7.5,
    "back_film": 1.1,
    "weight_grads_one": 4,
    "back_one": 7,
    "join": 1.0,
    "prepare": 3,
}

F32 = jnp.float32
BF16 = jnp.bfloat16
BIAS_ONE, BIAS_TWO, GAIN_ONE, SHIFT_ONE, GAIN_TWO, SHIFT_TWO, GAIN_THREE, SHIFT_THREE, PROJ_BIAS = (
    range(9)
)

VMEM = pl.BlockSpec(memory_space=pltpu.VMEM)
SMEM = pl.BlockSpec(memory_space=pltpu.SMEM)


def after(value, *others):
    return lax.optimization_barrier((value, *others))[0]


class Parts:
    def __init__(self, parts, ref):
        self.parts, self.ref = parts, ref

    def collect(self):
        first = self.ref.shape[1] - self.parts[0].shape[1]
        for index, part in enumerate(self.parts):
            self.ref[8 * index : 8 * index + 8, first:] = part[...]


def run_kernel(kernel, name, operands, outs, scratch=(), room=ROOM, blocks=None, terms=0):
    operands = tuple(operands)
    plain = len(operands) - (blocks[0] // 8 if blocks else 0)
    direct = len(outs) - terms
    in_specs = [SMEM if value.dtype == jnp.int32 and value.ndim == 1 else VMEM for value in operands]
    scratch = list(scratch)
    own = len(scratch)
    if blocks:
        scratch.append(pltpu.VMEM(blocks, BF16))

    def body(*refs):
        ins = refs[: len(operands)]
        results = refs[len(operands) : len(operands) + len(outs)]
        given = refs[len(operands) + len(outs) :]
        held = [Parts(ins[plain:], given[own])] if blocks else []
        kernel(*ins[:plain], *held, *results[:direct], *given[:own])
        for k in range(terms):
            results[direct + k][...] = given[own - 1][8 * k : 8 * k + 8]

    return pl.pallas_call(
        body,
        out_shape=list(outs),
        in_specs=in_specs,
        out_specs=[VMEM] * len(outs),
        scratch_shapes=scratch,
        compiler_params=pltpu.CompilerParams(vmem_limit_bytes=room * 2**20),
        cost_estimate=pl.CostEstimate(
            flops=int(FLOPS_PER_US * DURATIONS.get(name, 0.5)), bytes_accessed=0, transcendentals=0
        ),
        name=name,
    )(*operands)


def shape_of(shape, dtype):
    return jax.ShapeDtypeStruct(shape, dtype)


def dot(left, right, dims=(1, 0)):
    return lax.dot_general(
        left, right, (((dims[0],), (dims[1],)), ((), ())), preferred_element_type=F32
    )


def group_total(rows, grouping):
    return lax.dot_general(
        rows,
        grouping,
        (((1,), (0,)), ((), ())),
        preferred_element_type=F32,
        precision=lax.Precision.HIGHEST,
    )


def sigmoid(values):
    return 1.0 / (1.0 + jnp.exp(-values))


def valid_of(region_ref, index):
    return (region_ref[index] > 0).astype(F32)


def cells_of(region_ref):
    counts = [jnp.sum(valid_of(region_ref, m), axis=0, keepdims=True) for m in range(MAPS)]
    return jnp.concatenate(counts, axis=0) * float(GROUP_SIZE)


def column_sum(values):
    return jnp.sum(values, axis=0, keepdims=True)


def store_shifted(target_ref, index, values):
    column = lax.broadcasted_iota(jnp.int32, (PIXELS, 1), 0) % SIDE
    left = jnp.where(column == 0, 0.0, pltpu.roll(values, 1, 0))
    right = jnp.where(column == SIDE - 1, 0.0, pltpu.roll(values, PIXELS - 1, 0))
    border = jnp.zeros((SIDE, 3 * WIDTH), BF16)
    target_ref[index, 0:SIDE, :] = border
    target_ref[index, SIDE + PIXELS : PADDED, :] = border
    for position, part in enumerate((left, values, right)):
        target_ref[index, SIDE : SIDE + PIXELS, position * WIDTH : (position + 1) * WIDTH] = (
            part.astype(BF16)
        )


def convolve(shifted_ref, index, weight_ref):
    total = None
    for tap_row in range(3):
        part = dot(
            shifted_ref[index, tap_row * SIDE : tap_row * SIDE + PIXELS, :],
            weight_ref[:, tap_row * 3 * WIDTH : (tap_row + 1) * 3 * WIDTH],
            (1, 1),
        )
        total = part if total is None else total + part
    return total


def flip_weight(flipped_ref, weight_ref):
    for tap_row in range(3):
        for tap_col in range(3):
            start = (3 * (2 - tap_row) + 2 - tap_col) * WIDTH
            flipped_ref[tap_row, tap_col * WIDTH : (tap_col + 1) * WIDTH, :] = weight_ref[
                :, start : start + WIDTH
            ]


def convolve_back(shifted_ref, index, flipped_ref):
    total = None
    for tap_row in range(3):
        part = dot(
            shifted_ref[index, tap_row * SIDE : tap_row * SIDE + PIXELS, :],
            flipped_ref[tap_row],
        )
        total = part if total is None else total + part
    return total


def pack_conv(shard):
    tail = shard[:, 3 * LANES :]
    parts = [shard[:, LANES * k : LANES * (k + 1)] for k in range(3)]
    parts.append(jnp.concatenate([tail[:48], tail[48:], jnp.zeros((48, 32), shard.dtype)], axis=1))
    return jnp.concatenate(parts, axis=0)


def pack_proj(qkv, proj):
    wide = jnp.concatenate([qkv, proj], axis=1)
    return jnp.concatenate([wide[:, LANES * k : LANES * (k + 1)] for k in range(3)], axis=0)


def pack_emb(shard):
    side = shard[:, LANES:]
    half = side.shape[0] // 2
    return jnp.concatenate(
        [shard[:, :LANES], jnp.concatenate([side[:half], side[half:]], axis=1)], axis=0
    )


def prepare_kernel(
    me_ref, region, bias_one, bias_two, gain_one, shift_one, gain_two, shift_two, gain_three,
    shift_three, proj_bias, q_bias, v_bias, emb_bias,
    params, qkv_bias, film_bias, region_col, region_row, grouping,
):
    vectors = (
        bias_one, bias_two, gain_one, shift_one, gain_two, shift_two, gain_three, shift_three,
        proj_bias,
    )
    for row, vector in enumerate(vectors):
        params[row : row + 1, :] = vector[...].reshape(1, WIDTH)
    queries, values = q_bias[...].reshape(1, WIDTH), v_bias[...].reshape(1, WIDTH)
    gap = jnp.zeros((1, LANES - HEAD_DIM), F32)
    for head in range(HEADS):
        part = slice(HEAD_DIM * head, HEAD_DIM * (head + 1))
        base = 3 * LANES * head
        qkv_bias[:, base : base + LANES] = jnp.concatenate([queries[:, part], gap], axis=1)
        qkv_bias[:, base + LANES : base + 2 * LANES] = jnp.zeros((1, LANES), F32)
        qkv_bias[:, base + 2 * LANES : base + 3 * LANES] = jnp.concatenate(
            [values[:, part], gap], axis=1
        )
    film_bias[...] = emb_bias[...].reshape(1, 2 * WIDTH)
    rows = region[...].astype(F32)
    home = me_ref[1] * MAPS
    turned = jnp.concatenate([rows, jnp.zeros((LANES - rows.shape[0], PIXELS), F32)], axis=0).T
    lane = lax.broadcasted_iota(jnp.int32, (PIXELS, LANES), 1)
    for m in range(MAPS):
        region_row[m] = region[pl.ds(home + m, 1)]
        region_col[m] = jnp.sum(
            jnp.where(lane == home + m, turned, 0.0), axis=1, keepdims=True
        ).astype(jnp.int32)
    down = lax.broadcasted_iota(jnp.int32, (WIDTH, WIDTH), 0)
    along = lax.broadcasted_iota(jnp.int32, (WIDTH, WIDTH), 1)
    grouping[...] = (down // GROUP_SIZE == along // GROUP_SIZE).astype(F32)


def pack_kernel(conv_one, conv_two, emb, qkv, proj, embedding, first, second, third):
    first[0] = pack_conv(conv_one[...].astype(F32)).astype(BF16)
    second[0, 0:CONV_PACK] = pack_conv(conv_two[...].astype(F32)).astype(BF16)
    second[0, CONV_PACK:] = pack_emb(emb[...].astype(F32)).astype(BF16)
    third[0, 0:PROJ_PACK] = pack_proj(qkv[...].astype(F32), proj[...].astype(F32)).astype(BF16)
    embed = embedding[...].astype(F32)
    low = embed * sigmoid(embed)
    third[0, PROJ_PACK:] = jnp.concatenate(
        [low[:, LANES * k : LANES * (k + 1)] for k in range(EMBED // LANES)], axis=0
    ).astype(BF16)


def place_of(group, head, me_ref):
    far_group = group ^ me_ref[0]
    far_head = head ^ me_ref[1]
    bits = [far_group // 4, (far_group // 2) & 1, far_head // 2, far_group & 1]
    if head % 2 == 1:
        bits[2:] = bits[:1:-1]
    place = 16 * (far_head & 1)
    for position, bit in enumerate(bits):
        place = place + (1 << position) * bit
    return place


def place_of_own(group, over_x, me_ref):
    far_group = group ^ me_ref[0]
    far_x = over_x ^ (me_ref[1] // 2)
    far_y = far_group & 1
    odd = (me_ref[1] & 1) == 1
    place = far_group // 4 + 2 * ((far_group // 2) & 1)
    return place + jnp.where(odd, 4 * far_y + 8 * far_x, 4 * far_x + 8 * far_y)


def turn_halves(values, index, me_ref, kept, sent):
    odd = (me_ref[1] & 1) == 1
    turned = values.T
    place = pl.ds(index * PIXELS, PIXELS)
    for over_x in range(2):
        low = turned[2 * HEAD_DIM * over_x : 2 * HEAD_DIM * over_x + HEAD_DIM]
        high = turned[2 * HEAD_DIM * over_x + HEAD_DIM : 2 * HEAD_DIM * (over_x + 1)]
        rows = slice(HEAD_DIM * over_x, HEAD_DIM * (over_x + 1))
        kept[rows, place] = jnp.where(odd, high, low).astype(BF16)
        sent[rows, place] = jnp.where(odd, low, high).astype(BF16)


def repeat(count, step):
    def body(index, carry):
        step(index)
        return carry

    lax.fori_loop(0, count, body, 0)


def rows_of(index, size):
    return pl.ds(pl.multiple_of(index * size, 16), size)


def unpack_conv(blocks, me_ref, weight_ref):
    for head in range(HEADS):
        pieces = []
        for group in range(BLOCK_GROUPS):
            block = blocks[place_of(group, head, me_ref), 0:CONV_PACK]
            pieces += [block[HEAD_DIM * k : HEAD_DIM * (k + 1)] for k in range(3)]
            pieces.append(jnp.concatenate([block[288:, :48], block[288:, 48:96]], axis=0))
        weight_ref[HEAD_DIM * head : HEAD_DIM * (head + 1), :] = jnp.concatenate(
            pieces, axis=1
        )


def unpack_emb(blocks, me_ref, emb_ref):
    for group in range(BLOCK_GROUPS):
        embs = []
        for head in range(HEADS):
            emb = blocks[place_of(group, head, me_ref), CONV_PACK:].astype(F32)
            side = jnp.concatenate([emb[64:96, :64], emb[64:96, 64:]], axis=0)
            embs.append(jnp.concatenate([emb[:64], side], axis=1))
        emb_ref[64 * group : 64 * group + 64] = jnp.concatenate(embs, axis=1).astype(BF16)


def unpack_proj(blocks, me_ref, qkv_ref, proj_ref):
    gap = jnp.zeros((48, LANES - HEAD_DIM), F32)
    for group in range(BLOCK_GROUPS):
        rows = slice(48 * group, 48 * group + 48)
        for head in range(HEADS):
            block = blocks[place_of(group, head, me_ref)].astype(F32)
            wide = jnp.concatenate([block[48 * k : 48 * k + 48] for k in range(3)], axis=1)
            for part in range(3):
                piece = wide[:, HEAD_DIM * part : HEAD_DIM * (part + 1)]
                slot = (3 * head + part) * LANES
                qkv_ref[rows, slot : slot + LANES] = jnp.concatenate([piece, gap], axis=1).astype(
                    BF16
                )
            proj_ref[rows, LANES * head : LANES * (head + 1)] = jnp.concatenate(
                [wide[:, 3 * HEAD_DIM :], gap], axis=1
            ).astype(BF16)


def norm_stats(sums, squares, cells, grouping):
    totals = group_total(jnp.concatenate([sums, squares], axis=0), grouping)
    mean = totals[:MAPS] / cells
    inverse = lax.rsqrt(totals[MAPS:] / cells - mean * mean + EPS)
    return jnp.concatenate([mean, inverse], axis=0)


def norm_one_kernel(inputs, region, params, grouping, shifted, stats, sums):
    def add_map(m):
        values = inputs[m].astype(F32)
        masked = values * valid_of(region, m)
        sums[pl.ds(m, 1)] = column_sum(masked)
        sums[pl.ds(MAPS + m, 1)] = column_sum(masked * values)

    def one_map(m):
        hat = (inputs[m].astype(F32) - stats[pl.ds(m, 1)]) * stats[pl.ds(MAPS + m, 1)]
        normed = hat * params[GAIN_ONE : GAIN_ONE + 1] + params[SHIFT_ONE : SHIFT_ONE + 1]
        store_shifted(shifted, m, normed * sigmoid(normed) * valid_of(region, m))

    repeat(MAPS, add_map)
    stats[...] = norm_stats(sums[:MAPS], sums[MAPS:], cells_of(region), grouping[...])
    repeat(MAPS, one_map)


def conv_one_kernel(
    me_ref, shifted, region, params, grouping, blocks, weight, result, stats, sums
):
    blocks.collect()
    unpack_conv(blocks.ref, me_ref, weight)

    def one_map(m, carry):
        value = convolve(shifted, m, weight) + params[BIAS_ONE : BIAS_ONE + 1]
        result[m] = value
        masked = value * valid_of(region, m)
        sums[pl.ds(m, 1)] = column_sum(masked)
        sums[pl.ds(MAPS + m, 1)] = column_sum(masked * value)
        return carry

    lax.fori_loop(0, MAPS, one_map, 0, unroll=True)
    stats[...] = norm_stats(sums[:MAPS], sums[MAPS:], cells_of(region), grouping[...])


def modulate(value, stats, film, params, m):
    hat = (value - stats[pl.ds(m, 1)]) * stats[pl.ds(MAPS + m, 1)]
    modulated = hat * params[GAIN_TWO : GAIN_TWO + 1] + params[SHIFT_TWO : SHIFT_TWO + 1]
    scale = 1.0 + film[pl.ds(m, 1), :WIDTH]
    return hat, modulated, scale, modulated * scale + film[pl.ds(m, 1), WIDTH:]


def conv_two_kernel(
    me_ref, conv_out, stats_two, inputs, embedding, emb_bias, region, params, grouping, blocks,
    weight, emb_weight, hidden, shifted, residual, attend_in, stats, film,
    sums,
):
    blocks.collect()
    unpack_conv(blocks.ref, me_ref, weight)
    unpack_emb(blocks.ref, me_ref, emb_weight)
    embed = embedding[...].astype(F32)
    film[...] = dot((embed * sigmoid(embed)).astype(BF16), emb_weight[...]) + emb_bias[...]

    def one_map(m, carry):
        _, _, _, normed = modulate(conv_out[m], stats_two, film, params, m)
        valid = valid_of(region, m)
        active = normed * sigmoid(normed) * valid
        hidden[m] = active.astype(BF16)
        store_shifted(shifted, m, active)
        value = (
            inputs[m].astype(F32)
            + convolve(shifted, m, weight)
            + params[BIAS_TWO : BIAS_TWO + 1]
        )
        residual[m] = value
        sums[pl.ds(m, 1)] = column_sum(value * valid)
        sums[pl.ds(MAPS + m, 1)] = column_sum(value * value * valid)
        return carry

    lax.fori_loop(0, MAPS, one_map, 0, unroll=True)
    stats[...] = norm_stats(sums[:MAPS], sums[MAPS:], cells_of(region), grouping[...])
    for m in range(MAPS):
        hat = (residual[m] - stats[m : m + 1]) * stats[MAPS + m : MAPS + m + 1]
        attend_in[m] = (
            hat * params[GAIN_THREE : GAIN_THREE + 1] + params[SHIFT_THREE : SHIFT_THREE + 1]
        ).astype(BF16)


def norm_back(grad, hat, along, cross, inverse, valid, cells):
    return inverse * (grad - valid * (along + cross * hat) / cells)


def attend_kernel(
    me_ref, attend_in, qkv_bias, region, region_row, cotangent, residual, stats, params, blocks,
    output, grad_attend, bias_sums, sums, embeds,
    qkv_weight, proj_weight, columns, grad_columns, attended, terms,
):
    blocks.collect()
    unpack_proj(blocks.ref, me_ref, qkv_weight, proj_weight)

    def two_devices(pair):
        rows = []
        for index in (2 * pair, 2 * pair + 1):
            low = ((index >> 1) & 1) + 2 * (index & 1)
            block = blocks.ref[low + 4 * (index >> 2), PROJ_PACK:, :].astype(F32)
            tiles = [block[MAPS * k : MAPS * (k + 1)] for k in range(EMBED // LANES)]
            rows.append(jnp.concatenate(tiles, axis=1))
        embeds[pl.ds(pl.multiple_of(2 * MAPS * pair, 8), 2 * MAPS)] = jnp.concatenate(rows, axis=0)

    repeat(16, two_devices)

    def one_map(m, carry):
        rows = pl.ds(pl.multiple_of(m * PIXELS, PIXELS), PIXELS)
        columns[...] = (dot(attend_in[m], qkv_weight[...]) + qkv_bias[...]).astype(BF16)
        grad_attended = dot(cotangent[m], proj_weight[...]).astype(BF16)
        key_region = region[m]
        query_region = region_row[m]
        allowed = (key_region > 0) & ((key_region == query_region) | (query_region == 0))
        for head in range(HEADS):
            base = 3 * LANES * head
            queries = columns[:, base : base + LANES]
            keys = columns[:, base + LANES : base + 2 * LANES]
            values = columns[:, base + 2 * LANES : base + 3 * LANES]
            grad_out = grad_attended[:, LANES * head : LANES * (head + 1)]
            logits = jnp.where(allowed, dot(keys, queries, (1, 1)) * FACTOR, -1e30)
            raised = jnp.exp(logits - jnp.max(logits, axis=0, keepdims=True))
            weights = raised * (1.0 / jnp.sum(raised, axis=0, keepdims=True))
            weights_low = weights.astype(BF16)
            attended[rows, LANES * head : LANES * (head + 1)] = dot(
                weights_low, values, (0, 0)
            ).astype(BF16)
            grad_weights = dot(values, grad_out, (1, 1))
            inner = jnp.sum(grad_weights * weights, axis=0, keepdims=True)
            grad_logits = (weights * (grad_weights - inner)).astype(BF16)
            grad_columns[rows, base : base + LANES] = (
                dot(grad_logits, keys, (0, 0)) * FACTOR
            ).astype(BF16)
            grad_columns[rows, base + LANES : base + 2 * LANES] = (
                dot(grad_logits, queries) * FACTOR
            ).astype(BF16)
            grad_columns[rows, base + 2 * LANES : base + 3 * LANES] = dot(
                weights_low, grad_out
            ).astype(BF16)
        output[m] = (
            residual[m]
            + dot(attended[rows, :], proj_weight[...], (1, 1))
            + params[PROJ_BIAS : PROJ_BIAS + 1]
        ).astype(BF16)
        grad = dot(grad_columns[rows, :], qkv_weight[...], (1, 1))
        grad_attend[m] = grad
        hat = (residual[m] - stats[pl.ds(m, 1)]) * stats[pl.ds(MAPS + m, 1)]
        sums[pl.ds(m, 1)] = column_sum(grad)
        sums[pl.ds(MAPS + m, 1)] = column_sum(grad * hat)
        return carry

    lax.fori_loop(0, MAPS, one_map, 0)
    bias_sums[...] = column_sum(grad_columns[...].astype(F32))
    grad_qkv, grad_proj = None, None
    for m in range(MAPS):
        rows = slice(m * PIXELS, (m + 1) * PIXELS)
        qkv_part = dot(attend_in[m], grad_columns[rows, :], (0, 0))
        proj_part = dot(cotangent[m], attended[rows, :], (0, 0))
        grad_qkv = qkv_part if m == 0 else grad_qkv + qkv_part
        grad_proj = proj_part if m == 0 else grad_proj + proj_part
    for group in range(BLOCK_GROUPS):
        rows = slice(48 * group, 48 * group + 48)
        for head in range(HEADS):
            pieces = [
                grad_qkv[rows, slot * LANES : slot * LANES + HEAD_DIM]
                for slot in range(3 * head, 3 * head + 3)
            ]
            pieces.append(grad_proj[rows, head * LANES : head * LANES + HEAD_DIM])
            wide = jnp.concatenate(pieces, axis=1)
            terms[place_of(group, head, me_ref)] = jnp.concatenate(
                [wide[:, LANES * part : LANES * (part + 1)] for part in range(3)], axis=0
            ).astype(BF16)


def back_three_kernel(
    me_ref, grad_attend, sums, region, cotangent, residual, stats, params, grouping,
    grad_residual, grad_conv, kept, sent, small_sums,
):
    gain = params[GAIN_THREE : GAIN_THREE + 1]
    totals = group_total(sums[...] * gain, grouping[...])
    cells = cells_of(region)
    small_sums[...] = jnp.zeros_like(small_sums)
    small_sums[0:1] = column_sum(sums[MAPS:])
    small_sums[1:2] = column_sum(sums[:MAPS])
    top_sum = jnp.zeros((1, WIDTH), F32)
    low_sum = jnp.zeros((1, WIDTH), F32)
    for m in range(MAPS):
        inverse = stats[MAPS + m : MAPS + m + 1]
        hat = (residual[m] - stats[m : m + 1]) * inverse
        top = cotangent[m].astype(F32)
        grad = top + norm_back(
            grad_attend[m] * gain,
            hat,
            totals[m : m + 1],
            totals[MAPS + m : MAPS + m + 1],
            inverse,
            valid_of(region, m),
            cells[m : m + 1],
        )
        grad_residual[m] = grad
        low = grad.astype(BF16)
        grad_conv[m] = low
        turn_halves(low.astype(F32), m, me_ref, kept, sent)
        top_sum = top_sum + column_sum(top)
        low_sum = low_sum + column_sum(low.astype(F32))
    small_sums[2:3] = top_sum
    small_sums[3:4] = low_sum


def back_two_kernel(
    me_ref, grad_conv, weight, conv_out, stats, film, region, params, grouping,
    grad_low, kept, sent, grad_film, small_sums,
    flipped, shifted, grad_normed, sums,
):
    flip_weight(flipped, weight)

    def one_map(m, carry):
        store_shifted(shifted, m, grad_conv[m].astype(F32))
        hat, modulated, scale, normed = modulate(conv_out[m], stats, film, params, m)
        logistic = sigmoid(normed)
        slope = logistic * (1.0 + normed * (1.0 - logistic)) * valid_of(region, m)
        grad = convolve_back(shifted, m, flipped) * slope
        grad_film[pl.ds(m, 1), :WIDTH] = column_sum(grad * modulated)
        grad_film[pl.ds(m, 1), WIDTH:] = column_sum(grad)
        scaled = grad * scale
        grad_normed[m] = scaled
        sums[pl.ds(m, 1)] = column_sum(scaled)
        sums[pl.ds(MAPS + m, 1)] = column_sum(scaled * hat)
        return carry

    lax.fori_loop(0, MAPS, one_map, 0, unroll=2)
    gain = params[GAIN_TWO : GAIN_TWO + 1]
    totals = group_total(sums[...] * gain, grouping[...])
    cells = cells_of(region)
    small_sums[...] = jnp.zeros_like(small_sums)
    small_sums[0:1] = column_sum(sums[MAPS:])
    small_sums[1:2] = column_sum(sums[:MAPS])
    low_sum = jnp.zeros((1, WIDTH), F32)
    for m in range(MAPS):
        inverse = stats[MAPS + m : MAPS + m + 1]
        low = norm_back(
            grad_normed[m] * gain,
            (conv_out[m] - stats[m : m + 1]) * inverse,
            totals[m : m + 1],
            totals[MAPS + m : MAPS + m + 1],
            inverse,
            valid_of(region, m),
            cells[m : m + 1],
        ).astype(BF16)
        grad_low[m] = low
        turn_halves(low.astype(F32), m, me_ref, kept, sent)
        low_sum = low_sum + column_sum(low.astype(F32))
    small_sums[2:3] = low_sum


def back_film_kernel(embedding, emb_weight, grad_film, grad_embed):
    embed = embedding[...].astype(F32)
    logistic = sigmoid(embed)
    film_high = grad_film[...].astype(BF16)
    film_rest = (grad_film[...] - film_high.astype(F32)).astype(BF16)
    grad_embed[...] = (
        dot(film_high, emb_weight[...], (1, 1)) + dot(film_rest, emb_weight[...], (1, 1))
    ) * (logistic * (1.0 + embed * (1.0 - logistic)))


def back_one_kernel(
    grad_conv, weight, inputs, stats, grad_residual, region, params, grouping,
    grad_inputs, small_sums,
    flipped, shifted, grad_normed, sums,
):
    flip_weight(flipped, weight)
    gain = params[GAIN_ONE : GAIN_ONE + 1]

    def one_map(m, carry):
        store_shifted(shifted, m, grad_conv[m].astype(F32))
        hat = (inputs[m].astype(F32) - stats[pl.ds(m, 1)]) * stats[pl.ds(MAPS + m, 1)]
        normed = hat * gain + params[SHIFT_ONE : SHIFT_ONE + 1]
        logistic = sigmoid(normed)
        slope = logistic * (1.0 + normed * (1.0 - logistic)) * valid_of(region, m)
        grad = convolve_back(shifted, m, flipped) * slope
        grad_normed[m] = grad
        sums[pl.ds(m, 1)] = column_sum(grad)
        sums[pl.ds(MAPS + m, 1)] = column_sum(grad * hat)
        return carry

    lax.fori_loop(0, MAPS, one_map, 0)
    totals = group_total(sums[...] * gain, grouping[...])
    cells = cells_of(region)
    small_sums[...] = jnp.zeros_like(small_sums)
    small_sums[0:1] = column_sum(sums[MAPS:])
    small_sums[1:2] = column_sum(sums[:MAPS])
    for m in range(MAPS):
        inverse = stats[MAPS + m : MAPS + m + 1]
        grad_inputs[m] = (
            grad_residual[m]
            + norm_back(
                grad_normed[m] * gain,
                (inputs[m].astype(F32) - stats[m : m + 1]) * inverse,
                totals[m : m + 1],
                totals[MAPS + m : MAPS + m + 1],
                inverse,
                valid_of(region, m),
                cells[m : m + 1],
            )
        ).astype(BF16)


def conv_weight_grads(shifted, turned, total, begun=None):
    def one_row(tap_row, carry):
        rows = pl.ds(pl.multiple_of(tap_row * SIDE, SIDE), PIXELS)
        part = None if begun is None else begun[tap_row]
        for m in range(MAPS):
            term = dot(turned[:, m * PIXELS : (m + 1) * PIXELS], shifted[m, rows, :])
            part = term if part is None else part + term
        total[tap_row] = part
        return carry

    lax.fori_loop(0, 3, one_row, 0)


def own_grads_kernel(kept, shifted, total):
    conv_weight_grads(shifted, kept, total)


def pack_conv_grads(total, me_ref, blocks):
    def one_half(over_x):
        rows = rows_of(over_x, HEAD_DIM)
        for group in range(BLOCK_GROUPS):
            start, stop = group * CONV_ROWS, (group + 1) * CONV_ROWS
            values = []
            for tap_row in range(3):
                low, high = tap_row * 3 * WIDTH, (tap_row + 1) * 3 * WIDTH
                if max(low, start) < min(high, stop):
                    values.append(total[tap_row, rows, max(low, start) - low : min(high, stop) - low])
            block = values[0] if len(values) == 1 else jnp.concatenate(values, axis=1)
            place = place_of_own(group, over_x, me_ref)
            blocks[place, 0:CONV_PACK, :] = pack_conv(block.astype(BF16))

    repeat(2, one_half)


def grads_one_kernel(me_ref, came, shifted_core, begun, total, blocks):
    conv_weight_grads(shifted_core, came, total, begun)
    pack_conv_grads(total, me_ref, blocks)


def grads_two_kernel(
    me_ref, came, hidden_core, begun, near, far, near_came, far_came, total, shifted_core, blocks
):
    for m in range(MAPS):
        store_shifted(shifted_core, m, hidden_core[m].astype(F32))
    conv_weight_grads(shifted_core, came, total, begun)
    pack_conv_grads(total, me_ref, blocks)
    for index, (mine, other) in enumerate(((near, near_came), (far, far_came))):
        blocks[8 * index : 8 * index + 8, CONV_PACK:, :] = (
            mine[...].astype(F32) + other[...].astype(F32)
        ).astype(BF16)


def unpack_conv_grad(block, result):
    for part in range(3):
        result[:, LANES * part : LANES * (part + 1)] = block[HEAD_DIM * part : HEAD_DIM * (part + 1)]
    result[:, 3 * LANES :] = jnp.concatenate([block[288:336, :48], block[288:336, 48:96]], axis=0)


def first_message_kernel(small_one, small_two, small_three, column_sums, grad_film, message):
    pieces = [small_one[0:1], small_one[1:2], small_two[0:1], small_two[1:2], small_two[2:3]]
    pieces += [small_three[row : row + 1] for row in range(4)]
    for part in (0, 2):
        slots = [(3 * head + part) * LANES for head in range(HEADS)]
        pieces.append(
            jnp.concatenate([column_sums[:, slot : slot + HEAD_DIM] for slot in slots], axis=1)
        )
    film = column_sum(grad_film[...])
    pieces.append(jnp.zeros((1, WIDTH), F32))
    rows = [jnp.concatenate(pieces[k : k + 2], axis=1) for k in range(0, 12, 2)]
    sums = jnp.concatenate(rows + [film, jnp.zeros((1, 2 * WIDTH), F32)], axis=0)
    store_message(sums, [grad_film[...]], message)


def store_message(sums, films, message):
    high = sums.astype(BF16).astype(F32)
    message[...] = jnp.concatenate([high, sums - high, *films], axis=0).astype(BF16)


def added_sums(parts):
    half = SUM_ROWS // 2
    total = None
    for part in parts:
        both = part[:half] + part[half:SUM_ROWS]
        total = both if total is None else total + both
    return total


def next_message_kernel(left, right, message):
    parts = [left[...].astype(F32), right[...].astype(F32)]
    store_message(added_sums(parts), [part[SUM_ROWS:] for part in parts], message)


def finish_one_kernel(mine, other, result):
    unpack_conv_grad(mine[0].astype(F32) + other[0].astype(F32), result)


def finish_rows_kernel(me_ref, embeds, left, right, emb, *vectors):
    parts = [left[...].astype(F32), right[...].astype(F32)]
    sums = added_sums(parts)
    for index, vector in enumerate(vectors[:11]):
        row, place = index // 2, (index % 2) * WIDTH
        vector[...] = sums[row, place : place + WIDTH]
    vectors[11][...] = sums[6]
    films = jnp.concatenate([part[SUM_ROWS:] for part in parts], axis=0)
    rows, cols = emb.shape
    mine = films[:, 0:cols]
    for head in range(1, HEADS):
        mine = jnp.where(me_ref[1] == head, films[:, cols * head : cols * (head + 1)], mine)
    products = dot(embeds[...].astype(BF16), mine.astype(BF16), (0, 0))
    total = products[0:rows]
    for group in range(1, BLOCK_GROUPS):
        total = jnp.where(me_ref[0] == group, products[rows * group : rows * (group + 1)], total)
    emb[...] = total


def finish_two_kernel(mine, other, result, qkv, proj):
    block = mine[0].astype(F32) + other[0].astype(F32)
    unpack_conv_grad(block, result)
    tiles = [block[CONV_PACK + 48 * k : CONV_PACK + 48 * k + 48] for k in range(3)]
    wide = jnp.concatenate(tiles, axis=1)
    qkv[...] = wide[:, : 3 * HEAD_DIM]
    proj[...] = wide[:, 3 * HEAD_DIM :]


def join_kernel(left, right, joined):
    count = left.shape[0]
    joined[:count] = left[...]
    joined[count:] = right[...]


def add_split_kernel(left, right, send, keep):
    half = keep.shape[0]
    send[...] = (left[half:].astype(F32) + right[half:].astype(F32)).astype(BF16)
    keep[...] = (left[:half].astype(F32) + right[:half].astype(F32)).astype(BF16)


def swap(values, masks, sizes):
    pairs = [(own, own ^ masks[own % 2]) for own in range(sizes[0] * sizes[1])]
    return lax.ppermute(values, AXES, pairs)


def stages_of(sizes):
    inner = sizes[0] // BLOCK_GROUPS
    group_bit = sizes[1] * inner
    over_x, over_y = 2, group_bit
    return ((4 * group_bit,) * 2, (2 * group_bit,) * 2, (over_x, over_y), (over_y, over_x))


def join(left, right):
    joined = shape_of((left.shape[0] + right.shape[0],) + left.shape[1:], left.dtype)
    return run_kernel(join_kernel, "join", (left, right), (joined,), room=8)[0]


def add_split(left, right):
    half = shape_of((left.shape[0] // 2,) + left.shape[1:], BF16)
    return run_kernel(add_split_kernel, "add_split", (left, right), (half, half), room=8)


def inner_groups(sizes):
    inner = sizes[0] // BLOCK_GROUPS
    return [[group * inner + k for k in range(inner)] for group in range(BLOCK_GROUPS)]


def inner_gather(shard, sizes):
    if sizes[0] == BLOCK_GROUPS:
        return shard
    return lax.all_gather(shard, "dp", axis=0, tiled=True, axis_index_groups=inner_groups(sizes))


def inner_scatter(grad, sizes):
    if sizes[0] == BLOCK_GROUPS:
        return grad
    return lax.psum_scatter(
        grad, "dp", scatter_dimension=0, tiled=True, axis_index_groups=inner_groups(sizes)
    )


def inner_sum(vector, sizes):
    if sizes[0] == BLOCK_GROUPS:
        return vector
    return jnp.sum(lax.all_gather(vector, "dp", axis_index_groups=inner_groups(sizes)), axis=0)


def per_device(
    inputs, embedding, region, cotangent, conv_one, bias_one, conv_two, bias_two, emb_weight,
    emb_bias, qkv_weight, q_bias, v_bias, proj_weight, proj_bias, gain_one, shift_one, gain_two,
    shift_two, gain_three, shift_three,
):
    sizes = (lax.axis_size("dp"), lax.axis_size("head"))
    inner = sizes[0] // BLOCK_GROUPS
    dp_id, head_id = lax.axis_index("dp"), lax.axis_index("head")
    me = jnp.stack([dp_id // inner, head_id]).astype(jnp.int32)
    kernel = functools.partial
    map_shape = (MAPS, PIXELS, WIDTH)
    shifted_shape = (MAPS, PADDED, 3 * WIDTH)

    shards = [inner_gather(w, sizes) for w in (conv_one, conv_two, emb_weight, qkv_weight, proj_weight)]

    first, second, third, fourth = stages_of(sizes)
    core = (1, 1)

    def send(values, masks):
        return swap(values, masks, sizes)

    stats_shape = shape_of((2 * MAPS, WIDTH), F32)
    small_shape = shape_of((8, WIDTH), F32)
    sums_scratch = pltpu.VMEM((2 * MAPS, WIDTH), F32)
    pack_one, pack_two, pack_three = run_kernel(
        pack_kernel,
        "pack",
        (shards[0].T, shards[1].T, *shards[2:], embedding),
        (
            shape_of((1, CONV_PACK, LANES), BF16),
            shape_of((1, SECOND_ROWS, LANES), BF16),
            shape_of((1, THIRD_ROWS, LANES), BF16),
        ),
        room=62,
    )
    one = send(pack_one, first)
    two = send(pack_two, first)
    params, qkv_bias, film_bias, region_col, region_row, grouping = run_kernel(
        prepare_kernel,
        "prepare",
        (
            me, after(region, pack_one), bias_one, bias_two, gain_one, shift_one, gain_two, shift_two,
            gain_three, shift_three, proj_bias, q_bias, v_bias, emb_bias,
        ),
        (
            shape_of((16, WIDTH), F32),
            shape_of((1, SLOTS), F32),
            shape_of((1, 2 * WIDTH), F32),
            shape_of((MAPS, PIXELS, 1), jnp.int32),
            shape_of((MAPS, 1, PIXELS), jnp.int32),
            shape_of((WIDTH, WIDTH), F32),
        ),
        room=62,
    )
    held_one = join(pack_one, one)
    one = send(held_one, second)
    held_two = join(pack_two, after(two, held_one))
    two = send(held_two, second)
    held_one = join(held_one, after(one, held_two, params))
    one = send(held_one, third)
    held_two = join(held_two, after(two, held_one))
    two = send(held_two, third)
    three = send(after(pack_three, held_two), first)
    held_one = join(held_one, after(one, held_two))
    far_one = send(held_one, fourth)
    near_core_one = send(held_one, core)
    shifted_one, stats_one = run_kernel(
        norm_one_kernel,
        "norm_one",
        (after(inputs, held_one), region_col, params, grouping),
        (shape_of(shifted_shape, BF16), stats_shape),
        (sums_scratch,),
    )
    held_three = join(pack_three, after(three, stats_one))
    three = send(held_three, second)
    held_two = join(held_two, after(two, held_three))
    far_two = send(held_two, fourth)
    near_core_two = send(held_two, core)
    held_three = join(held_three, after(three, held_two))
    three = send(held_three, third)
    far_one = after(far_one, held_three)
    far_core_one = send(far_one, core)
    shifted_core_one = send(shifted_one, core)
    weight_shape = shape_of((WIDTH, TAPS), BF16)
    weight_one, conv_out, stats_two = run_kernel(
        conv_one_kernel,
        "conv_one",
        (
            me, after(shifted_one, held_three), region_col, params, grouping,
            held_one, far_one, near_core_one, far_core_one,
        ),
        (weight_shape, shape_of(map_shape, F32), stats_shape),
        (sums_scratch,),
        blocks=(32, CONV_PACK, LANES),
    )
    held_three = join(held_three, after(three, conv_out))
    far_three = send(held_three, fourth)
    near_core_three = send(held_three, core)
    far_two = after(far_two, conv_out, held_three)
    far_core_two = send(far_two, core)
    weight_two, film_weight, hidden_two, shifted_two, residual, attend_in, stats_three, film = run_kernel(
        conv_two_kernel,
        "conv_two",
        (
            me, after(conv_out, held_three), stats_two, inputs, embedding, film_bias, region_col,
            params, grouping, held_two, far_two, near_core_two, far_core_two,
        ),
        (
            weight_shape,
            shape_of((EMBED, 2 * WIDTH), BF16),
            shape_of(map_shape, BF16),
            shape_of(shifted_shape, BF16),
            shape_of(map_shape, F32),
            shape_of(map_shape, BF16),
            stats_shape,
            shape_of((MAPS, 2 * WIDTH), F32),
        ),
        (sums_scratch,),
        blocks=(32, SECOND_ROWS, LANES),
    )
    far_three = after(far_three, attend_in)
    far_core_three = send(far_three, core)
    proj_shape = shape_of((8, PROJ_PACK, LANES), BF16)
    output, grad_attend, column_sums, sums_three, embeds, *proj_terms = run_kernel(
        attend_kernel,
        "attend",
        (
            me, attend_in, qkv_bias, region_col, region_row, cotangent, residual, stats_three, params,
            held_three, far_three, near_core_three, far_core_three,
        ),
        (
            shape_of(map_shape, BF16), shape_of(map_shape, F32), shape_of((1, SLOTS), F32), stats_shape,
            shape_of((32 * MAPS, EMBED), F32),
        )
        + (proj_shape,) * 4,
        (
            pltpu.VMEM((WIDTH, SLOTS), BF16),
            pltpu.VMEM((WIDTH, HEADS * LANES), BF16),
            pltpu.VMEM((PIXELS, SLOTS), BF16),
            pltpu.VMEM((MAPS * PIXELS, SLOTS), BF16),
            pltpu.VMEM((MAPS * PIXELS, HEADS * LANES), BF16),
            pltpu.VMEM((32, PROJ_PACK, LANES), BF16),
        ),
        blocks=(32, THIRD_ROWS, LANES),
        terms=4,
    )
    near_proj, far_proj, near_came, far_came = proj_terms
    near_came, far_came = send(near_came, core), send(far_came, core)
    hidden_core_two = send(after(hidden_two, output), core)
    turned_shape = shape_of((2 * HEAD_DIM, MAPS * PIXELS), BF16)
    grad_residual, grad_conv_two, kept, sent, small_three = run_kernel(
        back_three_kernel,
        "back_three",
        (
            me, grad_attend, sums_three, region_col, cotangent, residual, stats_three, params, grouping,
        ),
        (shape_of(map_shape, F32), shape_of(map_shape, BF16), turned_shape, turned_shape, small_shape),
    )
    came = send(after(sent, near_came, far_came, hidden_core_two), core)
    total_shape = (3, 2 * HEAD_DIM, 3 * WIDTH)
    grads_scratch = pltpu.VMEM(total_shape, F32)
    (begun,) = run_kernel(
        own_grads_kernel, "own_grads", (kept, shifted_two), (shape_of(total_shape, F32),)
    )
    grads_rows = CONV_PACK + PROJ_PACK
    near_two, far_two = run_kernel(
        grads_two_kernel,
        "weight_grads_two",
        (me, after(came, begun), hidden_core_two, begun, near_proj, far_proj, near_came, far_came),
        (shape_of((8, grads_rows, LANES), BF16),) * 2,
        (
            grads_scratch,
            pltpu.VMEM(shifted_shape, BF16),
            pltpu.VMEM((16, grads_rows, LANES), BF16),
        ),
        terms=2,
    )
    two = send(far_two, fourth)
    back_scratch = (
        pltpu.VMEM((3, 3 * WIDTH, WIDTH), BF16),
        pltpu.VMEM(shifted_shape, BF16),
        pltpu.VMEM(map_shape, F32),
        sums_scratch,
    )
    grad_conv_one, kept, sent, grad_film, small_two = run_kernel(
        back_two_kernel,
        "back_two",
        (
            me, after(grad_conv_two, near_two, shifted_core_one), weight_two, conv_out, stats_two, film,
            region_col, params, grouping,
        ),
        (
            shape_of(map_shape, BF16),
            turned_shape,
            turned_shape,
            shape_of((MAPS, 2 * WIDTH), F32),
            small_shape,
        ),
        back_scratch,
    )
    came = send(sent, core)
    (begun,) = run_kernel(
        own_grads_kernel, "own_grads", (kept, shifted_one), (shape_of(total_shape, F32),)
    )
    (grad_embedding,) = run_kernel(
        back_film_kernel,
        "back_film",
        (embedding, film_weight, after(grad_film, begun)),
        (shape_of((MAPS, EMBED), F32),),
    )
    far_two, near_two = add_split(near_two, after(two, grad_embedding))
    two = send(far_two, third)
    near_one, far_one = run_kernel(
        grads_one_kernel,
        "weight_grads_one",
        (me, after(came, far_two), shifted_core_one, begun),
        (shape_of((8, CONV_PACK, LANES), BF16),) * 2,
        (grads_scratch, pltpu.VMEM((16, CONV_PACK, LANES), BF16)),
        terms=2,
    )
    one = send(far_one, fourth)
    grad_inputs, small_one = run_kernel(
        back_one_kernel,
        "back_one",
        (
            after(grad_conv_one, near_one), weight_one, inputs, stats_one, grad_residual,
            region_col, params, grouping,
        ),
        (shape_of(map_shape, BF16), small_shape),
        back_scratch,
    )
    far_two, near_two = add_split(near_two, after(two, small_one))
    two = send(far_two, second)

    def message(count):
        return (shape_of((SUM_ROWS + MAPS * count, 2 * WIDTH), BF16),)

    def next_message(parts, count):
        return run_kernel(next_message_kernel, "next_message", parts, message(count), room=8)[0]

    (rows,) = run_kernel(
        first_message_kernel,
        "first_message",
        (after(small_one, far_two), small_two, small_three, column_sums, grad_film),
        message(1),
        room=8,
    )
    came = send(rows, second)
    far_one, near_one = add_split(near_one, after(one, rows))
    one = send(far_one, third)
    rows = next_message((rows, after(came, far_one)), 2)
    came = send(rows, first)
    far_two, near_two = add_split(near_two, after(two, rows))
    two = send(far_two, first)
    rows = next_message((rows, after(came, far_two)), 4)
    came = send(rows, third)
    far_one, near_one = add_split(near_one, after(one, rows))
    one = send(far_one, second)
    rows = next_message((rows, after(came, far_one)), 8)
    came = send(rows, fourth)
    conv_grad_shape = shape_of((HEAD_DIM, CONV_ROWS), F32)
    grad_weight_two, grad_qkv_weight, grad_proj_weight = run_kernel(
        finish_two_kernel,
        "finish_two",
        (near_two, after(two, rows)),
        (conv_grad_shape, shape_of((48, 3 * HEAD_DIM), F32), shape_of((48, HEAD_DIM), F32)),
        room=8,
    )
    far_one, near_one = add_split(near_one, after(one, grad_weight_two))
    one = send(far_one, first)
    rows = next_message((rows, after(came, far_one)), 16)
    came = (rows, send(rows, core))
    vector = shape_of((WIDTH,), F32)
    grad_emb_weight, *vectors = run_kernel(
        finish_rows_kernel,
        "finish_rows",
        (me, embeds, *came),
        (shape_of((EMBED // BLOCK_GROUPS, 2 * WIDTH // HEADS), F32),)
        + (vector,) * 11
        + (shape_of((2 * WIDTH,), F32),),
        room=8,
    )
    (grad_weight_one,) = run_kernel(
        finish_one_kernel,
        "finish_one",
        (near_one, after(one, grad_emb_weight)),
        (conv_grad_shape,),
        room=8,
    )
    finals = [
        inner_scatter(grad, sizes)
        for grad in (
            grad_weight_one.T, grad_weight_two.T, grad_emb_weight, grad_qkv_weight, grad_proj_weight,
        )
    ]
    vectors = [inner_sum(vector, sizes) for vector in vectors]
    return (
        output,
        grad_inputs,
        grad_embedding,
        *finals,
        vectors[4],
        vectors[8],
        vectors[11],
        vectors[9],
        vectors[10],
        vectors[7],
        vectors[0],
        vectors[1],
        vectors[2],
        vectors[3],
        vectors[5],
        vectors[6],
    )


def solution(mesh):
    own = P(AXES)
    split = P("dp", "head")
    whole = P()
    in_specs = (own, own, P("dp"), own, split, whole, split, whole, split, whole, split) + (
        (whole, whole, split) + (whole,) * 7
    )
    out_specs = (own,) * 3 + (split,) * 5 + (whole,) * 12
    return jax.shard_map(
        per_device, mesh=mesh, in_specs=in_specs, out_specs=out_specs, check_vma=False
    )
```
